32 devices in a mesh: wide: 8 (over z, x), narrow: 4 (over y, core).
Axes of the slice: x: 2, y: 2, z: 4, core: 2. Of those that a mesh axis runs over, the one named last changes fastest.
Arguments:
- tokens: bfloat16 [2, 32768, 512], P(None, ('wide', 'narrow')), may hold values from -6 to 6
- out_grad: bfloat16 [2, 32768, 512], P(None, ('wide', 'narrow')), may hold values from -6 to 6
- long_count: int32 [2, 32], P(None, ('wide', 'narrow')), may hold values from 0 to 1
- params: float32 [3676160], P(('wide', 'narrow')), may hold values from -3 to 3, as said below
Outputs:
- outputs: bfloat16 [2, 32768, 512], P(None, ('wide', 'narrow'))
- input_grad: bfloat16 [2, 32768, 512], P(None, ('wide', 'narrow'))
- param_grad: float32 [3676160], P(('wide', 'narrow'))
The draws below stay inside these ranges and needn't reach their ends.
Inputs may be any that keep to these rules, and one draw needn't show every extreme that they name: `params`: the packed parameters, laid out as the first step states.
All inputs are finite; a program needn't handle non-finite values.
Results may differ from the reference program's by a relative error of at most 0.011.
Values may be sent and summed in bfloat16 or wider, within the bound.
No kernel may reach another device: no remote copies, remote signals or barrier semaphores. Data moves between devices by JAX's collectives and lax.ppermute only.
A program may use at most 192 MiB of HBM per device.

```python
import math
import jax
import jax.numpy as jnp
from jax import lax

D = 512
FF = 2048
HEADS = 8
HD = 64
SHORT = 512
LONG = 1024
SUB_TOK = 1024
SUBS = 2
ROWS = 32768
N_WIDE = 8
N_NARROW = 4
DEVICES = 32


def draw_params(key, part):
    key = jax.random.fold_in(key, 11)
    square = D * D
    entries = 6 * square + 2 * D * FF + 8 * D + FF
    unit_draw = jax.random.truncated_normal(key, -3.0, 3.0, (entries,), jnp.float32)
    out_factor = max(1.0, math.sqrt(SHORT) / 6.0)
    pieces = [(3 * square, D ** (-0.5), 0.0), (square, out_factor * D ** (-0.5), 0.0), (2 * square, D ** (-0.5), 0.0), (D * FF, D ** (-0.5), 0.0), (FF * D, 1.5 * FF ** (-0.5), 0.0), (D, 0.25, 1.0), (D, 0.2, 0.0), (D, 0.2, 0.0), (D, 0.5, 0.0), (D, 0.25, 1.0), (D, 0.2, 0.0), (D, 1.0, 0.0), (D, 0.5, 0.0), (FF, 0.2, 0.0)]
    scales = jnp.concatenate([jnp.full((amount,), factor, jnp.float32) for amount, factor, shift in pieces])
    shifts = jnp.concatenate([jnp.full((amount,), shift, jnp.float32) for amount, factor, shift in pieces])
    return shifts + scales * unit_draw


def plant(array, own_key, least, high):
    extent = array.shape
    place = [jax.random.randint(jax.random.fold_in(own_key, axis), (), 0, extent[axis]) for axis in range(len(extent))]
    array = array.at[tuple(place)].set(least)
    longest = extent.index(max(extent))
    place[longest] = (place[longest] + 1) % extent[longest]
    return array.at[tuple(place)].set(high)


def level_of(key, extent, shards, least, top_value):
    gain = 1.0
    for dim, blocks in shards:
        steps = jax.random.uniform(jax.random.fold_in(jax.random.fold_in(key, 6), dim), (blocks,), jnp.float32, least / len(shards), top_value / len(shards))
        gain = gain * jnp.repeat(jnp.exp(steps), extent[dim] // blocks).reshape((-1,) + (1,) * (len(extent) - 1 - dim))
    return gain


def gaussian(key, dims, width, bound, cuts=(), kind=jnp.bfloat16):
    values = jax.random.normal(key, dims, jnp.float32) * width
    if len(cuts) > 0:
        values = level_of(key, dims, cuts, -0.22, 0.18) * values
    return jnp.clip(values, min=-bound, max=bound).astype(kind)


def setup_inputs(seed: int = 0) -> dict:
    splits = jax.random.split(jax.random.key(seed), 5)
    tokens = gaussian(splits[0], (SUBS, ROWS, D), 1.0, 6.0, ((1, 32),))
    out_grad = gaussian(splits[1], (SUBS, ROWS, D), 1.0, 6.0, ((1, 32),))
    long_count = plant(jax.random.randint(splits[2], (SUBS, DEVICES), 0, SUB_TOK // LONG + 1), jax.random.fold_in(splits[2], 1), 0, (SUB_TOK // LONG + 1) - 1).astype(jnp.int32)
    params = draw_params(jax.random.fold_in(splits[4], 71), 0)
    return {"tokens": tokens, "out_grad": out_grad, "long_count": long_count, "params": params}


@jax.custom_vjp
def low(v):
    return lax.optimization_barrier(v.astype(jnp.bfloat16)).astype(jnp.float32)

@jax.custom_vjp
def low_back(v):
    return v

def low_keep(v):
    return (low(v), None)

def low_pass(kept, grad):
    return (grad,)

def back_keep(v):
    return (v, None)

def back_low(kept, grad):
    return (low(grad),)
low.defvjp(low_keep, low_pass)
low_back.defvjp(back_keep, back_low)
layer_eps = 1e-05
masked_value = -1000000000.0

def product(left, right):
    return jnp.dot(left, right, precision=lax.Precision.HIGHEST, preferred_element_type=jnp.float32)

def unpack(buffer):
    square = D * D
    matrices = tuple((buffer[position * square:(position + 1) * square].reshape(D, D) for position in range(6)))
    offset = 6 * square
    weight_in = buffer[offset:offset + D * FF].reshape(D, FF)
    offset = offset + D * FF
    weight_out = buffer[offset:offset + FF * D].reshape(FF, D)
    offset = offset + FF * D
    vectors = tuple((buffer[offset + position * D:offset + (position + 1) * D] for position in range(8)))
    offset = offset + 8 * D
    bias_in = buffer[offset:offset + FF]
    return matrices + (weight_in, weight_out) + vectors + (bias_in,)

def normalize(values):
    average = lax.optimization_barrier(jnp.mean(values, -1, keepdims=True))
    centred = values - average
    variance = lax.optimization_barrier(jnp.mean(centred * centred, -1, keepdims=True))
    return centred * lax.rsqrt(variance + layer_eps)

def attention(query_rows, key_rows, value_rows, long_seqs):
    length = query_rows.shape[0]
    query_heads = query_rows.reshape(length, HEADS, HD)
    key_heads = key_rows.reshape(length, HEADS, HD)
    value_heads = value_rows.reshape(length, HEADS, HD)
    scores = jnp.einsum('qhd,khd->hqk', query_heads, key_heads, precision=lax.Precision.HIGHEST)
    scores = low_back(scores * (1.0 / math.sqrt(HD)))
    row_ids = jnp.arange(length, dtype=jnp.int32)
    limit = long_seqs * LONG
    segment = jnp.where(row_ids < limit, row_ids // LONG, long_seqs + (row_ids - limit) // SHORT)
    allowed = (segment[:, None] == segment[None, :]) & (row_ids[:, None] >= row_ids[None, :])
    scores = jnp.where(allowed[None], scores, masked_value)
    largest = lax.optimization_barrier(jnp.max(scores, -1, keepdims=True))
    shifted = jnp.exp(scores - largest)
    soft = shifted / lax.optimization_barrier(jnp.sum(shifted, -1, keepdims=True))
    probs = low(soft)
    output = jnp.einsum('hqk,khd->qhd', probs, value_heads, precision=lax.Precision.HIGHEST)
    return output.reshape(length, D)

def layer_block(weights, inputs, long_seqs):
    w_query, w_key, w_value, w_out, gate_attn, gate_ffn, weight_in, weight_out, gain_a, shift_a, bias_out, bias_gate_a, gain_f, shift_f, bias_down, bias_gate_f, bias_in = weights
    hidden_a = low(normalize(inputs) * gain_a + shift_a)
    query_rows = low_back(low(product(hidden_a, w_query)))
    key_rows = low_back(low(product(hidden_a, w_key)))
    value_rows = low_back(low(product(hidden_a, w_value)))
    attended = low_back(low(attention(query_rows, key_rows, value_rows, long_seqs)))
    branch_a = low_back(product(attended, w_out) + bias_out)
    gate_a = jax.nn.sigmoid(low_back(product(hidden_a, gate_attn) + bias_gate_a))
    middle = inputs + gate_a * branch_a
    hidden_f = low(normalize(middle) * gain_f + shift_f)
    pre_active = low_back(product(hidden_f, weight_in) + bias_in)
    active = low(jax.nn.gelu(pre_active))
    branch_f = low_back(product(active, weight_out) + bias_down)
    gate_f = jax.nn.sigmoid(low_back(product(hidden_f, gate_ffn) + bias_gate_f))
    return middle + gate_f * branch_f

def reference(tokens, out_grad, long_count, params):
    blocks = tokens.astype(jnp.float32).reshape(SUBS * N_WIDE * N_NARROW, SUB_TOK, D)
    counts = long_count.reshape(-1).astype(jnp.int32)
    block_step = jax.checkpoint(layer_block)

    def forward(buffer, inputs):
        weights = unpack(low(buffer))

        def scan_step(carried, bundle):
            return (carried, block_step(weights, bundle[0], bundle[1]))
        unused, results = lax.scan(scan_step, jnp.zeros((), jnp.float32), (inputs, counts))
        return results
    result, pullback = jax.vjp(forward, params, blocks)
    grad_params, grad_blocks = pullback(out_grad.astype(jnp.float32).reshape(blocks.shape))
    return (result.reshape(tokens.shape).astype(jnp.bfloat16), grad_blocks.reshape(tokens.shape).astype(jnp.bfloat16), grad_params)
```

```python
import functools
import math

import jax
import jax.numpy as jnp
from jax import lax
from jax.experimental import pallas as pl
from jax.experimental.pallas import tpu as pltpu
from jax.sharding import PartitionSpec as P

D = 512
FF = 2048
HEADS = 8
HD = 64
SHORT = 512
LONG = 1024
PAIR = 2 * HD
PAIRS = HEADS // 2
STRIP = 256

TILE_ROWS = 16
TILE = TILE_ROWS * D

layer_eps = 1e-05
far_below = -1e30

F32 = jnp.float32
BF16 = jnp.bfloat16
MB = 1024 * 1024


def dot_nn(left, right):
    return lax.dot_general(left, right, (((1,), (0,)), ((), ())), preferred_element_type=F32)


def dot_nt(left, right):
    return lax.dot_general(left, right, (((1,), (1,)), ((), ())), preferred_element_type=F32)


def dot_tn(left, right):
    return lax.dot_general(left, right, (((0,), (0,)), ((), ())), preferred_element_type=F32)


def layer_stats(values):
    average = jnp.mean(values, -1, keepdims=True)
    centred = values - average
    variance = jnp.mean(centred * centred, -1, keepdims=True)
    inv_std = lax.rsqrt(variance + layer_eps)
    return (centred * inv_std, inv_std)


def norm_back(grad_hat, normed, inv_std):
    return inv_std * (
        grad_hat
        - jnp.mean(grad_hat, -1, keepdims=True)
        - normed * jnp.mean(grad_hat * normed, -1, keepdims=True)
    )


def sigmoid(values):
    return 0.5 * jnp.tanh(0.5 * values) + 0.5


def fold_rows(values):
    return jnp.sum(values.reshape(values.shape[0] // 8, 8, values.shape[1]), 0)


ROW_QUERY = 0
ROW_KEY = 512
ROW_VALUE = 1024
ROW_OUT = 1536
ROW_GATE_A = 2048
ROW_GATE_F = 2560
ROW_IN = 3072
ROW_DOWN = 5120
ROW_VEC = 7168
ALL_ROWS = 7184


def whole(shape, index=None, single=True):
    rank = len(shape)
    spot = index if index is not None else (0,) * rank
    kwargs = {"pipeline_mode": pl.Buffered(1)} if single else {}
    return pl.BlockSpec(shape, lambda *unused: spot, **kwargs)


PROJ_ROWS = 512


def project_body(tok, w_query, w_key, w_value, vec, hidden, query, key, value):
    normed, unused = layer_stats(tok[...].astype(F32))
    rows = vec[...].astype(F32)
    hid = (normed * rows[0:1] + rows[1:2]).astype(BF16)
    hidden[...] = hid
    query[...] = (dot_nn(hid, w_query[...]) * (1.0 / math.sqrt(HD))).astype(BF16)
    key[...] = dot_nn(hid, w_key[...]).astype(BF16)
    value[...] = dot_nn(hid, w_value[...]).astype(BF16)


def project(tokens, weights):
    total = tokens.shape[0]
    rows = pl.BlockSpec((PROJ_ROWS, D), lambda i: (i, 0))
    square = lambda at: whole((D, D), (at // D, 0))
    shape = jax.ShapeDtypeStruct((total, D), BF16)
    return pl.pallas_call(
        project_body,
        name="project",
        grid=(total // PROJ_ROWS,),
        in_specs=[rows, square(ROW_QUERY), square(ROW_KEY), square(ROW_VALUE), whole((16, D), (ROW_VEC // 16, 0))],
        out_specs=[rows] * 4,
        out_shape=[shape] * 4,
        compiler_params=pltpu.CompilerParams(vmem_limit_bytes=40 * MB),
    )(tokens, weights, weights, weights, weights)


def split_three(values):
    high = values.astype(BF16)
    rest = values - high.astype(F32)
    middle = rest.astype(BF16)
    low = (rest - middle.astype(F32)).astype(BF16)
    return high, middle, low


def pick_lanes(base, lane, first, columns):
    out = base
    for offset, column in enumerate(columns):
        out = jnp.where(lane == first + offset, column, out)
    return out


def attend_body(long_ref, query, key, value, attended, extra):
    sub = pl.program_id(0)
    is_long = long_ref[sub] > 0
    lane = lax.broadcasted_iota(jnp.int32, (STRIP, PAIR), 1)
    row_ids = lax.broadcasted_iota(jnp.int32, (STRIP, STRIP), 0)
    col_ids = lax.broadcasted_iota(jnp.int32, (STRIP, STRIP), 1)
    causal = row_ids >= col_ids
    cut = jnp.where(is_long, 0.0, far_below)
    keys = key[...]
    values = value[...]
    for strip in range(LONG // STRIP):
        rows = pl.ds(strip * STRIP, STRIP)
        reach = (strip + 1) * STRIP
        q_rows = query[rows, :]
        far = strip * STRIP >= SHORT
        tail = jnp.zeros((STRIP, PAIR), F32)
        outs = []
        for head in range(2):
            mine = (lane < HD) if head == 0 else (lane >= HD)
            q_head = jnp.where(mine, q_rows, jnp.zeros_like(q_rows))
            scores = dot_nt(q_head, keys[:reach])
            parts = []
            if far:
                parts.append(scores[:, :SHORT] + cut)
                if reach - STRIP > SHORT:
                    parts.append(scores[:, SHORT : reach - STRIP])
            elif strip:
                parts.append(scores[:, : reach - STRIP])
            parts.append(jnp.where(causal, scores[:, reach - STRIP :], far_below))
            scores = jnp.concatenate(parts, 1)
            largest = jnp.max(scores, -1, keepdims=True)
            shifted = jnp.exp(scores - largest)
            sum_exp = jnp.sum(shifted, -1, keepdims=True)
            out = dot_nn(shifted.astype(BF16), values[:reach]) * (1.0 / sum_exp)
            outs.append(out)
            high, middle, low = split_three(-(largest + jnp.log(sum_exp)))
            tail = pick_lanes(tail, lane, 3 * head, [t.astype(F32) for t in (high, middle, low)])
        if far:
            tail = jnp.where(lane == 6, jnp.where(is_long, 0.0, 1.0), tail)
        attended[rows, :] = jnp.where(lane < HD, outs[0], outs[1]).astype(BF16)
        extra[rows, :] = tail.astype(BF16)


def attend(longs, query, key, value):
    total = query.shape[0]
    block = pl.BlockSpec((LONG, PAIR), lambda s, p, l: (s, p))
    shape = jax.ShapeDtypeStruct((total, D), BF16)
    return pl.pallas_call(
        attend_body,
        name="attend",
        grid_spec=pltpu.PrefetchScalarGridSpec(
            num_scalar_prefetch=1,
            grid=(total // LONG, PAIRS),
            in_specs=[block] * 3,
            out_specs=[block] * 2,
        ),
        out_shape=[shape] * 2,
        compiler_params=pltpu.CompilerParams(vmem_limit_bytes=40 * MB),
    )(longs, query, key, value)


def attend_back_body(long_ref, query, key, value, extra, attended, grad, grad_query, grad_key, grad_value):
    lane = lax.broadcasted_iota(jnp.int32, (LONG, PAIR), 1)
    row = lax.broadcasted_iota(jnp.int32, (LONG, PAIR), 0)
    row_ids = lax.broadcasted_iota(jnp.int32, (STRIP, STRIP), 0)
    col_ids = lax.broadcasted_iota(jnp.int32, (STRIP, STRIP), 1)
    causal = col_ids >= row_ids
    q_all, k_all, v_all, g_all, x_all = query[...], key[...], value[...], grad[...], extra[...]
    product = g_all.astype(F32) * attended[...].astype(F32)
    zero = jnp.zeros_like(q_all)
    early = jnp.where((lane == 6) & (row < SHORT), far_below, 0.0)
    v_tail = jnp.where(lane < 3, 1.0, 0.0).astype(BF16)
    v_wide = jnp.concatenate([v_all, v_tail], 1)
    heads = []
    for head in range(2):
        mine = (lane < HD) if head == 0 else (lane >= HD)
        delta = jnp.sum(jnp.where(mine, product, 0.0), -1, keepdims=True)
        d_tail = pick_lanes(jnp.zeros((LONG, PAIR), F32), lane, 0, [t.astype(F32) for t in split_three(-delta)])
        q_head = jnp.where(mine, q_all, zero)
        g_head = jnp.where(mine, g_all, zero)
        k_head = jnp.where(mine, k_all, zero)
        ones = jnp.where((lane >= 3 * head) & (lane < 3 * head + 3), 1.0, early).astype(BF16)
        heads.append(
            (
                q_head,
                g_head,
                k_head,
                jnp.concatenate([q_head, x_all], 1),
                jnp.concatenate([g_head, d_tail.astype(BF16)], 1),
                jnp.concatenate([k_all, ones], 1),
            )
        )
    blocks = LONG // STRIP
    query_sum = [jnp.zeros((STRIP, PAIR), F32) for unused in range(blocks)]
    for block in range(blocks):
        lo, hi = block * STRIP, (block + 1) * STRIP
        key_sum = jnp.zeros((STRIP, PAIR), F32)
        value_sum = jnp.zeros((STRIP, PAIR), F32)
        for q_head, g_head, k_head, q_wide, g_wide, k_wide in heads:
            soft = jnp.exp(dot_nt(k_wide[lo:hi], q_wide[lo:]))
            first = jnp.where(causal, soft[:, :STRIP], 0.0)
            soft = first if hi == LONG else jnp.concatenate([first, soft[:, STRIP:]], 1)
            slope = dot_nt(v_wide[lo:hi], g_wide[lo:])
            scores = (soft * slope).astype(BF16)
            value_sum += dot_nn(soft.astype(BF16), g_head[lo:])
            key_sum += dot_nn(scores, q_head[lo:])
            part = dot_tn(scores, k_head[lo:hi])
            for later in range(block, blocks):
                query_sum[later] += part[(later - block) * STRIP : (later - block + 1) * STRIP]
        grad_key[lo:hi, :] = key_sum.astype(BF16)
        grad_value[lo:hi, :] = value_sum.astype(BF16)
        grad_query[lo:hi, :] = (query_sum[block] * (1.0 / math.sqrt(HD))).astype(BF16)


def attend_back(longs, query, key, value, extra, attended, grad):
    total = query.shape[0]
    block = pl.BlockSpec((LONG, PAIR), lambda s, p, l: (s, p))
    shape = jax.ShapeDtypeStruct((total, D), BF16)
    return pl.pallas_call(
        attend_back_body,
        name="attend_back",
        grid_spec=pltpu.PrefetchScalarGridSpec(
            num_scalar_prefetch=1,
            grid=(total // LONG, PAIRS),
            in_specs=[block] * 6,
            out_specs=[block] * 3,
        ),
        out_shape=[shape] * 3,
        compiler_params=pltpu.CompilerParams(vmem_limit_bytes=48 * MB),
    )(longs, query, key, value, extra, attended, grad)


MID_ROWS = 256
CHUNKS = FF // D
TANH_SCALE = math.sqrt(2.0 / math.pi)


def spread_matrix(size):
    quarter = size // CHUNKS
    to = lax.broadcasted_iota(jnp.int32, (size, size), 0)
    source = lax.broadcasted_iota(jnp.int32, (size, size), 1)
    return (source == CHUNKS * (to % quarter) + to // quarter).astype(BF16)


def middle_body(
    steps,
    tok,
    grad_out,
    hidden_a,
    attended,
    w_out,
    gate_attn,
    gate_ffn,
    w_in,
    w_down,
    vec,
    outputs,
    grad_middle_ref,
    grad_za_ref,
    grad_attended,
    d_out,
    d_gate_a,
    d_gate_f,
    d_in,
    d_down,
    d_vec,
    wide,
    slope,
    s_active,
    s_grad_pre,
    s_hidden_f,
    s_grad_f,
    s_grad_zf,
    s_grad_a,
    s_grad_za,
    s_hidden_a,
    s_attended,
    s_vec,
):
    step = pl.program_id(0)

    @pl.when(step == 0)
    def _():
        shuffle = spread_matrix(256)
        for block in range(FF // 256):
            part = dot_nn(shuffle, w_in[block * 256 : (block + 1) * 256, :]).astype(BF16)
            for chunk in range(CHUNKS):
                wide[chunk, block * 64 : (block + 1) * 64, :] = part[chunk * 64 : (chunk + 1) * 64]
        s_vec[...] = jnp.zeros_like(s_vec)

    here = pl.ds(pl.multiple_of(step * MID_ROWS, MID_ROWS), MID_ROWS)
    vecs = vec[...].astype(F32)
    hid_a = hidden_a[...]
    att = attended[...]
    grad = grad_out[...].astype(F32)
    branch_a = dot_nn(att, w_out[...]) + vecs[2:3]
    gate_a = sigmoid(dot_nn(hid_a, gate_attn[...]) + vecs[3:4])
    middle = tok[...].astype(F32) + gate_a * branch_a
    normed, inv_std = layer_stats(middle)
    hid_f = (normed * vecs[4:5] + vecs[5:6]).astype(BF16)
    s_hidden_f[here, :] = hid_f
    s_hidden_a[here, :] = hid_a
    s_attended[here, :] = att
    gate_f = sigmoid(dot_nn(hid_f, gate_ffn[...]) + vecs[7:8])
    branch_f = jnp.zeros((MID_ROWS, D), F32) + vecs[6:7]
    for chunk in range(CHUNKS):
        cols = slice(chunk * D, (chunk + 1) * D)
        pre = dot_nn(hid_f, wide[chunk]) + vecs[8 + chunk : 9 + chunk]
        square = pre * pre
        bend = jnp.tanh(pre * (TANH_SCALE + (TANH_SCALE * 0.044715) * square))
        half = 0.5 * (1.0 + bend)
        active = (pre * half).astype(BF16)
        slope[:, cols] = half + (0.5 * pre) * (1.0 - bend * bend) * (
            TANH_SCALE + (3.0 * 0.044715 * TANH_SCALE) * square
        )
        s_active[here, cols] = active
        branch_f += dot_nn(active, w_down[chunk * D : (chunk + 1) * D, :])
    outputs[...] = (middle + gate_f * branch_f).astype(BF16)

    grad_branch_f = (grad * gate_f).astype(BF16)
    grad_zf = (grad * branch_f * gate_f * (1.0 - gate_f)).astype(BF16)
    s_grad_f[here, :] = grad_branch_f
    s_grad_zf[here, :] = grad_zf
    s_vec[6] += fold_rows(grad_branch_f.astype(F32))
    s_vec[7] += fold_rows(grad_zf.astype(F32))
    grad_hidden = dot_nt(grad_zf, gate_ffn[...])
    for chunk in range(CHUNKS):
        cols = slice(chunk * D, (chunk + 1) * D)
        grad_active = dot_nt(grad_branch_f, w_down[chunk * D : (chunk + 1) * D, :])
        grad_pre = (grad_active * slope[:, cols]).astype(BF16)
        s_grad_pre[here, cols] = grad_pre
        s_vec[8 + chunk] += fold_rows(grad_pre.astype(F32))
        grad_hidden += dot_nt(grad_pre, wide[chunk])
    s_vec[4] += fold_rows(grad_hidden * normed)
    s_vec[5] += fold_rows(grad_hidden)
    grad_middle = grad + norm_back(grad_hidden * vecs[4:5], normed, inv_std)
    grad_middle_ref[...] = grad_middle
    grad_branch_a = (grad_middle * gate_a).astype(BF16)
    grad_za = (grad_middle * branch_a * gate_a * (1.0 - gate_a)).astype(BF16)
    grad_za_ref[...] = grad_za
    s_grad_a[here, :] = grad_branch_a
    s_grad_za[here, :] = grad_za
    s_vec[2] += fold_rows(grad_branch_a.astype(F32))
    s_vec[3] += fold_rows(grad_za.astype(F32))
    grad_attended[...] = dot_nt(grad_branch_a, w_out[...]).astype(BF16)

    @pl.when(step == steps - 1)
    def _():
        for chunk in range(CHUNKS):
            cols = slice(chunk * D, (chunk + 1) * D)
            d_down[cols, :] = dot_tn(s_active[:, cols], s_grad_f[...]).astype(BF16)
            wide[chunk] = dot_tn(s_hidden_f[...], s_grad_pre[:, cols]).astype(BF16)
        shuffle = spread_matrix(256)
        for block in range(FF // 256):
            parts = [wide[chunk, block * 64 : (block + 1) * 64, :] for chunk in range(CHUNKS)]
            d_in[block * 256 : (block + 1) * 256, :] = dot_tn(shuffle, jnp.concatenate(parts, 0)).astype(BF16)
        d_out[...] = dot_tn(s_attended[...], s_grad_a[...]).astype(BF16)
        d_gate_a[...] = dot_tn(s_hidden_a[...], s_grad_za[...]).astype(BF16)
        d_gate_f[...] = dot_tn(s_hidden_f[...], s_grad_zf[...]).astype(BF16)
        d_vec[...] = jnp.sum(s_vec[...], 1)


def middle_part(tokens, grad_out, hidden_a, attended, weights):
    total = tokens.shape[0]
    steps = total // MID_ROWS
    rows = pl.BlockSpec((MID_ROWS, D), lambda i: (i, 0))
    square = lambda at: whole((D, D), (at // D, 0))
    rows_of = lambda kind: jax.ShapeDtypeStruct((total, D), kind)
    kept = lambda count: pltpu.VMEM((total, count), BF16)
    fixed = lambda count, kind: jax.ShapeDtypeStruct((count, D), kind)
    return pl.pallas_call(
        functools.partial(middle_body, steps),
        name="middle_part",
        grid=(steps,),
        in_specs=[rows] * 4
        + [square(ROW_OUT), square(ROW_GATE_A), square(ROW_GATE_F)]
        + [
            pl.BlockSpec((pl.Element(FF), pl.Element(D)), lambda i: (ROW_IN, 0), pipeline_mode=pl.Buffered(1)),
            pl.BlockSpec((pl.Element(FF), pl.Element(D)), lambda i: (ROW_DOWN, 0), pipeline_mode=pl.Buffered(1)),
            whole((16, D), (ROW_VEC // 16, 0)),
        ],
        out_specs=[rows] * 4
        + [whole((D, D))] * 3
        + [whole((FF, D))] * 2
        + [whole((16, D))],
        out_shape=[rows_of(BF16), rows_of(F32), rows_of(BF16), rows_of(BF16)]
        + [fixed(D, BF16)] * 3
        + [fixed(FF, BF16)] * 2
        + [fixed(16, F32)],
        scratch_shapes=[
            pltpu.VMEM((CHUNKS, D, D), BF16),
            pltpu.VMEM((MID_ROWS, FF), F32),
            kept(FF),
            kept(FF),
            kept(D),
            kept(D),
            kept(D),
            kept(D),
            kept(D),
            kept(D),
            kept(D),
            pltpu.VMEM((16, 8, D), F32),
        ],
        compiler_params=pltpu.CompilerParams(vmem_limit_bytes=62 * MB),
    )(tokens, grad_out, hidden_a, attended, *([weights] * 6))


LAST_ROWS = 512


def last_body(
    steps,
    tok,
    grad_middle,
    grad_za,
    hidden_a,
    grad_query,
    grad_key,
    grad_value,
    w_query,
    w_key,
    w_value,
    gate_attn,
    vec,
    input_grad,
    d_query,
    d_key,
    d_value,
    d_vec,
    s_vec,
):
    step = pl.program_id(0)

    @pl.when(step == 0)
    def _():
        s_vec[...] = jnp.zeros_like(s_vec)

    here = pl.ds(pl.multiple_of(step * LAST_ROWS, LAST_ROWS), LAST_ROWS)
    vecs = vec[...].astype(F32)
    normed, inv_std = layer_stats(tok[...].astype(F32))
    grad_hidden = (
        dot_nt(grad_query[here, :], w_query[...])
        + dot_nt(grad_key[here, :], w_key[...])
        + dot_nt(grad_value[here, :], w_value[...])
        + dot_nt(grad_za[...], gate_attn[...])
    )
    s_vec[0] += fold_rows(grad_hidden * normed)
    s_vec[1] += fold_rows(grad_hidden)
    input_grad[...] = (grad_middle[...] + norm_back(grad_hidden * vecs[0:1], normed, inv_std)).astype(BF16)

    @pl.when(step == steps - 1)
    def _():
        d_query[...] = dot_tn(hidden_a[...], grad_query[...]).astype(BF16)
        d_key[...] = dot_tn(hidden_a[...], grad_key[...]).astype(BF16)
        d_value[...] = dot_tn(hidden_a[...], grad_value[...]).astype(BF16)
        d_vec[...] = jnp.sum(s_vec[...], 1)


def last_part(tokens, grad_middle, grad_za, hidden_a, grad_query, grad_key, grad_value, weights):
    total = tokens.shape[0]
    steps = total // LAST_ROWS
    rows = pl.BlockSpec((LAST_ROWS, D), lambda i: (i, 0))
    square = lambda at: whole((D, D), (at // D, 0))
    full = whole((total, D))
    fixed = jax.ShapeDtypeStruct((D, D), BF16)
    return pl.pallas_call(
        functools.partial(last_body, steps),
        name="last_part",
        grid=(steps,),
        in_specs=[rows] * 3
        + [full] * 4
        + [square(ROW_QUERY), square(ROW_KEY), square(ROW_VALUE), square(ROW_GATE_A), whole((16, D), (ROW_VEC // 16, 0))],
        out_specs=[rows] + [whole((D, D))] * 3 + [whole((16, D))],
        out_shape=[jax.ShapeDtypeStruct((total, D), BF16)] + [fixed] * 3 + [jax.ShapeDtypeStruct((16, D), F32)],
        scratch_shapes=[pltpu.VMEM((16, 8, D), F32)],
        compiler_params=pltpu.CompilerParams(vmem_limit_bytes=48 * MB),
    )(tokens, grad_middle, grad_za, hidden_a, grad_query, grad_key, grad_value, *([weights] * 5))


def local_part(weights, tokens, out_grad, longs):
    subs, length, unused = tokens.shape
    rows = tokens.reshape(subs * length, D)
    grads = out_grad.reshape(subs * length, D)
    hidden_a, query, key, value = project(rows, weights)
    attended, extra = attend(longs, query, key, value)
    (outputs, grad_middle, grad_za, grad_attended, d_out, d_gate_a, d_gate_f, d_in, d_down, vec_one) = middle_part(
        rows, grads, hidden_a, attended, weights
    )
    grad_query, grad_key, grad_value = attend_back(longs, query, key, value, extra, attended, grad_attended)
    input_grad, d_query, d_key, d_value, vec_two = last_part(
        rows, grad_middle, grad_za, hidden_a, grad_query, grad_key, grad_value, weights
    )
    gradient = jnp.concatenate(
        [d_query, d_key, d_value, d_out, d_gate_a, d_gate_f, d_in, d_down, (vec_one + vec_two).astype(BF16)], 0
    )
    return outputs.reshape(tokens.shape), input_grad.reshape(tokens.shape), gradient


def share_tiles(share, count):
    starts = [index * share // TILE for index in range(count)]
    ends = [-(-((index + 1) * share) // TILE) for index in range(count)]
    return starts, max(end - start for start, end in zip(starts, ends))


def assemble(blocks, starts):
    count, rows, unused = blocks.shape
    pieces = []
    for index in range(count):
        lo = starts[index] * TILE_ROWS
        hi = (starts[index + 1] if index + 1 < count else ALL_ROWS // TILE_ROWS) * TILE_ROWS
        piece = blocks[index, : hi - lo]
        if index and (starts[index - 1] * TILE_ROWS + rows) > lo:
            over = starts[index - 1] * TILE_ROWS + rows - lo
            before = blocks[index - 1, rows - over :]
            piece = jnp.concatenate([piece[:over] + before, piece[over:]], 0)
        pieces.append(piece)
    return jnp.concatenate(pieces, 0)


def on_device(axes, sizes, tokens, out_grad, long_count, params):
    count = math.prod(sizes)
    share = params.shape[0]
    starts, tiles = share_tiles(share, count)
    rows = tiles * TILE_ROWS
    me = lax.axis_index(axes)
    offset = (me * share) % TILE
    padded = lax.dynamic_update_slice(jnp.zeros((rows * D,), F32), params, (offset,))
    block = padded.reshape(rows, D).astype(BF16)
    gathered = lax.all_gather(block, axes, axis=0, tiled=False)
    weights = assemble(gathered, starts)
    outputs, input_grad, gradient = local_part(weights, tokens, out_grad, long_count.reshape(-1))
    limit = gradient.shape[0]
    spread = []
    for index in range(count):
        lo = starts[index] * TILE_ROWS
        piece = gradient[lo : min(lo + rows, limit)]
        if lo + rows > limit:
            piece = jnp.pad(piece, ((0, lo + rows - limit), (0, 0)))
        spread.append(piece)
    summed = lax.psum_scatter(jnp.stack(spread), axes, scatter_dimension=0, tiled=False)
    param_grad = lax.dynamic_slice(summed.astype(F32).reshape(-1), (offset,), (share,))
    return (outputs, input_grad, param_grad)


def solution(mesh):
    axes = ("wide", "narrow")
    sizes = tuple(mesh.shape[axis] for axis in axes)
    return jax.shard_map(
        functools.partial(on_device, axes, sizes),
        mesh=mesh,
        in_specs=(
            P(None, axes, None),
            P(None, axes, None),
            P(None, axes),
            P(axes),
        ),
        out_specs=(
            P(None, axes, None),
            P(None, axes, None),
            P(axes),
        ),
        check_vma=False,
    )
```

```python
import functools
import math

import jax
import jax.numpy as jnp
from jax import lax
from jax.experimental import pallas as pl
from jax.experimental.pallas import tpu as pltpu
from jax.sharding import Mesh, PartitionSpec as P

D = 512
FF = 2048
HEADS = 8
HD = 64
SHORT = 512
LONG = 1024
PAIR = 2 * HD
PAIRS = HEADS // 2
STRIP = 256

TILE_ROWS = 16
TILE = TILE_ROWS * D

layer_eps = 1e-05
far_below = -1e30

F32 = jnp.float32
BF16 = jnp.bfloat16
MB = 1024 * 1024


def dot_nn(left, right):
    return lax.dot_general(left, right, (((1,), (0,)), ((), ())), preferred_element_type=F32)


def dot_nt(left, right):
    return lax.dot_general(left, right, (((1,), (1,)), ((), ())), preferred_element_type=F32)


def dot_tn(left, right):
    return lax.dot_general(left, right, (((0,), (0,)), ((), ())), preferred_element_type=F32)


def layer_stats(values):
    average = jnp.mean(values, -1, keepdims=True)
    centred = values - average
    variance = jnp.mean(centred * centred, -1, keepdims=True)
    inv_std = lax.rsqrt(variance + layer_eps)
    return (centred * inv_std, inv_std)


def norm_back(grad_hat, normed, inv_std):
    return inv_std * (
        grad_hat
        - jnp.mean(grad_hat, -1, keepdims=True)
        - normed * jnp.mean(grad_hat * normed, -1, keepdims=True)
    )


def sigmoid(values):
    return 0.5 * jnp.tanh(0.5 * values) + 0.5


def fold_rows(values):
    return jnp.sum(values.reshape(values.shape[0] // 8, 8, values.shape[1]), 0)


ROW_QUERY = 0
ROW_KEY = 512
ROW_VALUE = 1024
ROW_OUT = 1536
ROW_GATE_A = 2048
ROW_GATE_F = 2560
ROW_IN = 3072
ROW_DOWN = 5120
ROW_VEC = 7168
ALL_ROWS = 7184
VEC_ROWS = 16
ENTRIES = 6 * D * D + 2 * D * FF + 8 * D + FF

SHARES = 32
PLANES = 4
IN_PLANE = SHARES // PLANES
HALF = IN_PLANE // 2
STARTS = [index * (ENTRIES // SHARES) // TILE * TILE_ROWS for index in range(SHARES)]
BLOCK = max(
    -(-((index + 1) * (ENTRIES // SHARES)) // TILE) * TILE_ROWS - STARTS[index] for index in range(SHARES)
)
PLANE_END = [STARTS[(plane + 1) * IN_PLANE - 1] + BLOCK for plane in range(PLANES)]
VEC_AT = ROW_VEC - STARTS[-1]

VMEM = pltpu.CompilerParams(vmem_limit_bytes=60 * MB)


def whole(shape, single=True):
    rank = len(shape)
    kwargs = {"pipeline_mode": pl.Buffered(1)} if single else {}
    return pl.BlockSpec(shape, lambda *unused: (0,) * rank, **kwargs)


def share_row(where, plane, spot, other):
    core = 1 - where[3] if other else where[3]
    share = 2 * ((where[1] * 2 + where[2]) ^ spot) + core
    return ((plane * IN_PLANE + share) * (ENTRIES // SHARES)) // TILE * TILE_ROWS


class Piece:
    def __init__(self, array, blocks, other, column):
        self.array, self.blocks, self.other, self.column = array, blocks, other, column


def place_piece(target, base, where, piece, source):
    width = source.shape[-1]
    for index, (plane, spot) in enumerate(piece.blocks):
        at = share_row(where, plane, spot, piece.other) - base
        rows = pl.ds(pl.multiple_of(at, TILE_ROWS), BLOCK)
        cols = slice(piece.column, piece.column + width)
        target[rows, cols] = target[rows, cols] + source[index, :BLOCK, :]


def without(body, start, count):
    return lambda *refs: body(*refs[:start], *refs[start + count :])


UNREAD = pl.BlockSpec(memory_space=pl.ANY)


def emit_blocks(source, base, plane, where, keep, send):
    for spot in range(HALF):
        for out, other in ((keep, False), (send, True)):
            at = share_row(where, plane, spot, other) - base
            out[spot, :BLOCK, :] = source[pl.ds(pl.multiple_of(at, TILE_ROWS), BLOCK), :]


def split_three(values):
    high = values.astype(BF16)
    rest = values - high.astype(F32)
    middle = rest.astype(BF16)
    low = (rest - middle.astype(F32)).astype(BF16)
    return high, middle, low


def pick_lanes(base, lane, first, columns):
    out = base
    for offset, column in enumerate(columns):
        out = jnp.where(lane == first + offset, column, out)
    return out


def attend_rows(is_long, query, key, value, attended, extra):
    lane = lax.broadcasted_iota(jnp.int32, (STRIP, PAIR), 1)
    row_ids = lax.broadcasted_iota(jnp.int32, (STRIP, STRIP), 0)
    col_ids = lax.broadcasted_iota(jnp.int32, (STRIP, STRIP), 1)
    causal = row_ids >= col_ids
    cut = jnp.where(is_long, 0.0, far_below)
    for strip in range(LONG // STRIP):
        rows = pl.ds(strip * STRIP, STRIP)
        reach = (strip + 1) * STRIP
        q_rows = query[strip * STRIP : reach]
        far = strip * STRIP >= SHORT
        tail = jnp.zeros((STRIP, PAIR), F32)
        outs = []
        for head in range(2):
            mine = (lane < HD) if head == 0 else (lane >= HD)
            q_head = jnp.where(mine, q_rows, jnp.zeros_like(q_rows))
            scores = dot_nt(q_head, key[:reach])
            parts = []
            if far:
                parts.append(scores[:, :SHORT] + cut)
                if reach - STRIP > SHORT:
                    parts.append(scores[:, SHORT : reach - STRIP])
            elif strip:
                parts.append(scores[:, : reach - STRIP])
            parts.append(jnp.where(causal, scores[:, reach - STRIP :], far_below))
            scores = jnp.concatenate(parts, 1)
            largest = jnp.max(scores, -1, keepdims=True)
            shifted = jnp.exp(scores - largest)
            sum_exp = jnp.sum(shifted, -1, keepdims=True)
            out = dot_nn(shifted.astype(BF16), value[:reach]) * (1.0 / sum_exp)
            outs.append(out)
            tail = pick_lanes(
                tail, lane, 3 * head, [t.astype(F32) for t in split_three(-(largest + jnp.log(sum_exp)))]
            )
        if far:
            tail = jnp.where(lane == 6, jnp.where(is_long, 0.0, 1.0), tail)
        attended[rows, :] = jnp.where(lane < HD, outs[0], outs[1]).astype(BF16)
        extra[rows, :] = tail.astype(BF16)


def pair_body(first, pieces, longs, where, rows_in, *rest):
    sources, rest = rest[: len(pieces)], rest[len(pieces) :]
    if first:
        query, key, value, attended, extra, w_three, w_out, hidden, vec, weights = rest
    else:
        query, key, value, attended, extra, w_three, w_out, weights = rest
    sub = pl.program_id(0)

    @pl.when(sub == 0)
    def _():
        weights[...] = jnp.zeros_like(weights)
        for piece, source in zip(pieces, sources):
            place_piece(weights, 0, where, piece, source)
        w_three[...] = weights[:ROW_OUT, :]
        w_out[...] = weights[ROW_OUT:, :]
        if first:
            total = jnp.zeros((HALF * VEC_ROWS, PAIR), BF16)
            for source in sources:
                for index in range(source.shape[0]):
                    total = total + source[index, BLOCK:, :]
            for part in range(D // PAIR):
                vec[:, part * PAIR : (part + 1) * PAIR] = total[part * VEC_ROWS : (part + 1) * VEC_ROWS]

    if first:
        normed, unused = layer_stats(rows_in[...].astype(F32))
        lines = vec[...].astype(F32)
        hid = (normed * lines[0:1] + lines[1:2]).astype(BF16)
        hidden[...] = hid
    else:
        hid = rows_in[...]
    factors = jnp.concatenate(
        [weights[ROW_QUERY : ROW_QUERY + D, :], weights[ROW_KEY : ROW_KEY + D, :], weights[ROW_VALUE : ROW_VALUE + D, :]], 1
    )
    three = dot_nn(hid, factors)
    q_rows = (three[:, :PAIR] * (1.0 / math.sqrt(HD))).astype(BF16)
    k_rows = three[:, PAIR : 2 * PAIR].astype(BF16)
    v_rows = three[:, 2 * PAIR :].astype(BF16)
    query[...] = q_rows
    key[...] = k_rows
    value[...] = v_rows
    attend_rows(longs[sub] > 0, q_rows, k_rows, v_rows, attended, extra)


def pair_forward(first, column, longs, where, rows_in, pieces, deps=()):
    total = rows_in.shape[0]
    rows = pl.BlockSpec((LONG, D), lambda s, *refs: (s, 0))
    narrow = pl.BlockSpec((LONG, PAIR), lambda s, *refs: (s, 0))
    blocks = [
        pl.BlockSpec(piece.array.shape[:2] + (PAIR,), lambda s, *refs: (0, 0, column), pipeline_mode=pl.Buffered(1))
        for piece in pieces
    ]
    tail = PLANE_END[0] - ROW_OUT
    narrow_shape = jax.ShapeDtypeStruct((total, PAIR), BF16)
    out_specs = [narrow] * 5 + [whole((ROW_OUT, PAIR)), whole((tail, PAIR))]
    out_shape = [narrow_shape] * 5 + [
        jax.ShapeDtypeStruct((ROW_OUT, PAIR), BF16),
        jax.ShapeDtypeStruct((tail, PAIR), BF16),
    ]
    if first:
        out_specs += [rows, whole((VEC_ROWS, D))]
        out_shape += [jax.ShapeDtypeStruct((total, D), BF16), jax.ShapeDtypeStruct((VEC_ROWS, D), BF16)]
    return pl.pallas_call(
        without(functools.partial(pair_body, first, pieces), 3 + len(pieces), len(deps)),
        name="pair_forward",
        grid_spec=pltpu.PrefetchScalarGridSpec(
            num_scalar_prefetch=2,
            grid=(total // LONG,),
            in_specs=[rows] + blocks + [UNREAD] * len(deps),
            out_specs=out_specs,
            scratch_shapes=[pltpu.VMEM((PLANE_END[0], PAIR), BF16)],
        ),
        out_shape=out_shape,
        compiler_params=VMEM,
        cost_estimate=pl.CostEstimate(flops=int(4e9), bytes_accessed=int(8e6), transcendentals=int(2e6)),
    )(longs, where, rows_in, *[piece.array for piece in pieces], *deps)


def attend_back_body(longs, query, key, value, extra, attended, grad, grad_query, grad_key, grad_value):
    lane = lax.broadcasted_iota(jnp.int32, (LONG, PAIR), 1)
    row = lax.broadcasted_iota(jnp.int32, (LONG, PAIR), 0)
    row_ids = lax.broadcasted_iota(jnp.int32, (STRIP, STRIP), 0)
    col_ids = lax.broadcasted_iota(jnp.int32, (STRIP, STRIP), 1)
    causal = col_ids >= row_ids
    q_all, k_all, v_all, g_all, x_all = query[...], key[...], value[...], grad[...], extra[...]
    product = g_all.astype(F32) * attended[...].astype(F32)
    zero = jnp.zeros_like(q_all)
    early = jnp.where((lane == 6) & (row < SHORT), far_below, 0.0)
    v_tail = jnp.where(lane < 3, 1.0, 0.0).astype(BF16)
    v_wide = jnp.concatenate([v_all, v_tail], 1)
    heads = []
    for head in range(2):
        mine = (lane < HD) if head == 0 else (lane >= HD)
        delta = jnp.sum(jnp.where(mine, product, 0.0), -1, keepdims=True)
        d_tail = pick_lanes(jnp.zeros((LONG, PAIR), F32), lane, 0, [t.astype(F32) for t in split_three(-delta)])
        q_head = jnp.where(mine, q_all, zero)
        g_head = jnp.where(mine, g_all, zero)
        k_head = jnp.where(mine, k_all, zero)
        ones = jnp.where((lane >= 3 * head) & (lane < 3 * head + 3), 1.0, early).astype(BF16)
        heads.append(
            (
                q_head,
                g_head,
                k_head,
                jnp.concatenate([q_head, x_all], 1),
                jnp.concatenate([g_head, d_tail.astype(BF16)], 1),
                jnp.concatenate([k_all, ones], 1),
            )
        )
    blocks = LONG // STRIP
    query_sum = [jnp.zeros((STRIP, PAIR), F32) for unused in range(blocks)]
    for block in range(blocks):
        lo, hi = block * STRIP, (block + 1) * STRIP
        key_sum = jnp.zeros((STRIP, PAIR), F32)
        value_sum = jnp.zeros((STRIP, PAIR), F32)
        for q_head, g_head, k_head, q_wide, g_wide, k_wide in heads:
            soft = jnp.exp(dot_nt(k_wide[lo:hi], q_wide[lo:]))
            first = jnp.where(causal, soft[:, :STRIP], 0.0)
            soft = first if hi == LONG else jnp.concatenate([first, soft[:, STRIP:]], 1)
            slope = dot_nt(v_wide[lo:hi], g_wide[lo:])
            scores = (soft * slope).astype(BF16)
            value_sum += dot_nn(soft.astype(BF16), g_head[lo:])
            key_sum += dot_nn(scores, q_head[lo:])
            part = dot_tn(scores, k_head[lo:hi])
            for later in range(block, blocks):
                query_sum[later] += part[(later - block) * STRIP : (later - block + 1) * STRIP]
        grad_key[lo:hi, :] = key_sum.astype(BF16)
        grad_value[lo:hi, :] = value_sum.astype(BF16)
        grad_query[lo:hi, :] = (query_sum[block] * (1.0 / math.sqrt(HD))).astype(BF16)


def attend_back(pair, longs, query, key, value, extra, attended, grad, deps=()):
    total = query.shape[0]
    block = pl.BlockSpec((LONG, PAIR), lambda s, l: (s, 0))
    shape = jax.ShapeDtypeStruct((total, PAIR), BF16)
    return pl.pallas_call(
        without(attend_back_body, 7, len(deps)),
        name="attend_back",
        grid_spec=pltpu.PrefetchScalarGridSpec(
            num_scalar_prefetch=1,
            grid=(total // LONG,),
            in_specs=[block] * 5 + [pl.BlockSpec((LONG, PAIR), lambda s, l: (s, pair))] + [UNREAD] * len(deps),
            out_specs=[block] * 3,
        ),
        out_shape=[shape] * 3,
        compiler_params=VMEM,
        cost_estimate=pl.CostEstimate(flops=int(6e9), bytes_accessed=int(5e6), transcendentals=int(2e6)),
    )(longs, query, key, value, extra, attended, grad, *deps)


MID_ROWS = 256
CHUNKS = FF // D
TANH_SCALE = math.sqrt(2.0 / math.pi)


def spread_matrix(size):
    quarter = size // CHUNKS
    to = lax.broadcasted_iota(jnp.int32, (size, size), 0)
    source = lax.broadcasted_iota(jnp.int32, (size, size), 1)
    return (source == CHUNKS * (to % quarter) + to // quarter).astype(BF16)


def middle_body(steps, pieces, where, tok, grad_out, hidden_a, *refs):
    att_refs, wo_refs, refs = refs[:PAIRS], refs[PAIRS : 2 * PAIRS], refs[2 * PAIRS :]
    sources, refs = refs[: len(pieces)], refs[len(pieces) :]
    (outputs, grad_middle_ref, grad_za_ref, grad_attended, hid_f_ref, active_ref, grad_pre_ref, grad_f_ref) = refs[:8]
    (grad_zf_ref, grad_a_ref, d_vec, gate_copy, weights, wide, slope, s_vec) = refs[8:]
    step = pl.program_id(0)
    base = ROW_OUT

    @pl.when(step == 0)
    def _():
        weights[...] = jnp.zeros_like(weights)
        for pair in range(PAIRS):
            weights[: PLANE_END[0] - ROW_OUT, pair * PAIR : (pair + 1) * PAIR] = wo_refs[pair][...]
        for piece, source in zip(pieces, sources):
            place_piece(weights, base, where, piece, source)
        shuffle = spread_matrix(256)
        for block in range(FF // 256):
            at = ROW_IN - base + block * 256
            part = dot_nn(shuffle, weights[at : at + 256, :]).astype(BF16)
            for chunk in range(CHUNKS):
                wide[chunk, block * 64 : (block + 1) * 64, :] = part[chunk * 64 : (chunk + 1) * 64]
        gate_copy[...] = weights[ROW_GATE_A - base : ROW_GATE_A - base + D, :]
        s_vec[...] = jnp.zeros_like(s_vec)

    w_out = weights.at[ROW_OUT - base : ROW_OUT - base + D]
    gate_attn = weights.at[ROW_GATE_A - base : ROW_GATE_A - base + D]
    gate_ffn = weights.at[ROW_GATE_F - base : ROW_GATE_F - base + D]
    w_down = weights.at[ROW_DOWN - base : ROW_DOWN - base + FF]
    vecs = weights[ROW_VEC - base : ROW_VEC - base + VEC_ROWS, :].astype(F32)
    hid_a = hidden_a[...]
    att = jnp.concatenate([ref[...] for ref in att_refs], 1)
    grad = grad_out[...].astype(F32)
    branch_a = dot_nn(att, w_out[...]) + vecs[2:3]
    gate_a = sigmoid(dot_nn(hid_a, gate_attn[...]) + vecs[3:4])
    middle = tok[...].astype(F32) + gate_a * branch_a
    normed, inv_std = layer_stats(middle)
    hid_f = (normed * vecs[4:5] + vecs[5:6]).astype(BF16)
    hid_f_ref[...] = hid_f
    gate_f = sigmoid(dot_nn(hid_f, gate_ffn[...]) + vecs[7:8])
    branch_f = jnp.zeros((MID_ROWS, D), F32) + vecs[6:7]
    for chunk in range(CHUNKS):
        cols = slice(chunk * D, (chunk + 1) * D)
        pre = dot_nn(hid_f, wide[chunk]) + vecs[8 + chunk : 9 + chunk]
        square = pre * pre
        bend = jnp.tanh(pre * (TANH_SCALE + (TANH_SCALE * 0.044715) * square))
        half = 0.5 * (1.0 + bend)
        active = (pre * half).astype(BF16)
        slope[:, cols] = half + (0.5 * pre) * (1.0 - bend * bend) * (
            TANH_SCALE + (3.0 * 0.044715 * TANH_SCALE) * square
        )
        active_ref[:, cols] = active
        branch_f += dot_nn(active, w_down[chunk * D : (chunk + 1) * D, :])
    outputs[...] = (middle + gate_f * branch_f).astype(BF16)

    grad_branch_f = (grad * gate_f).astype(BF16)
    grad_zf = (grad * branch_f * gate_f * (1.0 - gate_f)).astype(BF16)
    grad_f_ref[...] = grad_branch_f
    grad_zf_ref[...] = grad_zf
    s_vec[6] += fold_rows(grad_branch_f.astype(F32))
    s_vec[7] += fold_rows(grad_zf.astype(F32))
    grad_hidden = dot_nt(grad_zf, gate_ffn[...])
    for chunk in range(CHUNKS):
        cols = slice(chunk * D, (chunk + 1) * D)
        grad_active = dot_nt(grad_branch_f, w_down[chunk * D : (chunk + 1) * D, :])
        grad_pre = (grad_active * slope[:, cols]).astype(BF16)
        grad_pre_ref[:, cols] = grad_pre
        s_vec[8 + chunk] += fold_rows(grad_pre.astype(F32))
        grad_hidden += dot_nt(grad_pre, wide[chunk])
    s_vec[4] += fold_rows(grad_hidden * normed)
    s_vec[5] += fold_rows(grad_hidden)
    grad_middle = grad + norm_back(grad_hidden * vecs[4:5], normed, inv_std)
    grad_middle_ref[...] = grad_middle
    grad_branch_a = (grad_middle * gate_a).astype(BF16)
    grad_za = (grad_middle * branch_a * gate_a * (1.0 - gate_a)).astype(BF16)
    grad_za_ref[...] = grad_za
    grad_a_ref[...] = grad_branch_a
    s_vec[2] += fold_rows(grad_branch_a.astype(F32))
    s_vec[3] += fold_rows(grad_za.astype(F32))
    grad_attended[...] = dot_nt(grad_branch_a, w_out[...]).astype(BF16)

    @pl.when(step == steps - 1)
    def _():
        d_vec[...] = jnp.sum(s_vec[...], 1).astype(BF16)


def middle_part(where, tokens, grad_out, hidden_a, attended, w_outs, pieces):
    total = tokens.shape[0]
    steps = total // MID_ROWS
    rows_at = lambda width: pl.BlockSpec((MID_ROWS, width), lambda i, *refs: (i, 0))
    shape = lambda width, kind=BF16: jax.ShapeDtypeStruct((total, width), kind)
    return pl.pallas_call(
        functools.partial(middle_body, steps, pieces),
        name="middle_part",
        grid_spec=pltpu.PrefetchScalarGridSpec(
            num_scalar_prefetch=1,
            grid=(steps,),
            in_specs=[rows_at(D)] * 3
            + [rows_at(PAIR)] * PAIRS
            + [whole(w_outs[0].shape)] * PAIRS
            + [whole(piece.array.shape) for piece in pieces],
            out_specs=[rows_at(D)] * 5 + [rows_at(FF)] * 2 + [rows_at(D)] * 3 + [whole((VEC_ROWS, D)), whole((D, D))],
            scratch_shapes=[
                pltpu.VMEM((ALL_ROWS - ROW_OUT, D), BF16),
                pltpu.VMEM((CHUNKS, D, D), BF16),
                pltpu.VMEM((MID_ROWS, FF), F32),
                pltpu.VMEM((VEC_ROWS, 8, D), F32),
            ],
        ),
        out_shape=[shape(D), shape(D, F32), shape(D), shape(D), shape(D), shape(FF), shape(FF)]
        + [shape(D)] * 3
        + [jax.ShapeDtypeStruct((VEC_ROWS, D), BF16), jax.ShapeDtypeStruct((D, D), BF16)],
        compiler_params=VMEM,
        cost_estimate=pl.CostEstimate(flops=int(24e9), bytes_accessed=int(50e6), transcendentals=int(4e6)),
    )(where, tokens, grad_out, hidden_a, *attended, *w_outs, *[piece.array for piece in pieces])


PLANE_OUT = [jax.ShapeDtypeStruct((HALF, BLOCK, D), BF16)] * 2
PLANE_SPEC = [whole((HALF, BLOCK, D))] * 2


def down_body(steps, where, active, grad_f, d_vec, keep, send, carry, rows):
    step = pl.program_id(0)
    rows[pl.ds(pl.multiple_of(step * D, D), D), :] = dot_tn(active[...], grad_f[...]).astype(BF16)

    @pl.when(step == steps - 1)
    def _():
        rows[FF:, :] = d_vec[...]
        emit_blocks(rows, ROW_DOWN, 3, where, keep, send)
        carry[...] = rows[: PLANE_END[2] - ROW_DOWN, :]


def down_gradient(where, active, grad_f, d_vec, deps=()):
    total = active.shape[0]
    carry = PLANE_END[2] - ROW_DOWN
    return pl.pallas_call(
        without(functools.partial(down_body, CHUNKS), 4, len(deps)),
        name="down_gradient",
        grid_spec=pltpu.PrefetchScalarGridSpec(
            num_scalar_prefetch=1,
            grid=(CHUNKS,),
            in_specs=[
                pl.BlockSpec((total, D), lambda i, *refs: (0, i)),
                whole((total, D)),
                whole((VEC_ROWS, D)),
            ]
            + [UNREAD] * len(deps),
            out_specs=PLANE_SPEC + [whole((carry, D))],
            scratch_shapes=[pltpu.VMEM((ALL_ROWS - ROW_DOWN, D), BF16)],
        ),
        out_shape=PLANE_OUT + [jax.ShapeDtypeStruct((carry, D), BF16)],
        compiler_params=VMEM,
        cost_estimate=pl.CostEstimate(flops=int(4.3e9), bytes_accessed=int(12e6), transcendentals=0),
    )(where, active, grad_f, d_vec, *deps)


def up_body(steps, where, hidden_f, grad_pre, late, keep, send, carry, rows, wide):
    step = pl.program_id(0)
    wide[step] = dot_tn(hidden_f[...], grad_pre[...]).astype(BF16)

    @pl.when(step == steps - 1)
    def _():
        shuffle = spread_matrix(256)
        for block in range(FF // 256):
            parts = [wide[chunk, block * 64 : (block + 1) * 64, :] for chunk in range(CHUNKS)]
            rows[block * 256 : (block + 1) * 256, :] = dot_tn(shuffle, jnp.concatenate(parts, 0)).astype(BF16)
        rows[FF:, :] = late[...]
        emit_blocks(rows, ROW_IN, 2, where, keep, send)
        carry[...] = rows[: PLANE_END[1] - ROW_IN, :]


def up_gradient(where, hidden_f, grad_pre, late, deps=()):
    total = hidden_f.shape[0]
    carry = PLANE_END[1] - ROW_IN
    return pl.pallas_call(
        without(functools.partial(up_body, CHUNKS), 4, len(deps)),
        name="up_gradient",
        grid_spec=pltpu.PrefetchScalarGridSpec(
            num_scalar_prefetch=1,
            grid=(CHUNKS,),
            in_specs=[
                whole((total, D)),
                pl.BlockSpec((total, D), lambda i, *refs: (0, i)),
                whole(late.shape),
            ]
            + [UNREAD] * len(deps),
            out_specs=PLANE_SPEC + [whole((carry, D))],
            scratch_shapes=[
                pltpu.VMEM((FF + late.shape[0], D), BF16),
                pltpu.VMEM((CHUNKS, D, D), BF16),
            ],
        ),
        out_shape=PLANE_OUT + [jax.ShapeDtypeStruct((carry, D), BF16)],
        compiler_params=VMEM,
        cost_estimate=pl.CostEstimate(flops=int(4.3e9), bytes_accessed=int(12e6), transcendentals=0),
    )(where, hidden_f, grad_pre, late, *deps)


def gates_body(where, *refs):
    att_refs, refs = refs[:PAIRS], refs[PAIRS:]
    hidden_a, hidden_f, grad_a, grad_za, grad_zf, late, keep, send, carry, rows = refs
    att = jnp.concatenate([ref[...] for ref in att_refs], 1)
    rows[:D, :] = dot_tn(att, grad_a[...]).astype(BF16)
    rows[D : 2 * D, :] = dot_tn(hidden_a[...], grad_za[...]).astype(BF16)
    rows[2 * D : 3 * D, :] = dot_tn(hidden_f[...], grad_zf[...]).astype(BF16)
    rows[3 * D :, :] = late[...]
    emit_blocks(rows, ROW_OUT, 1, where, keep, send)
    carry[...] = rows[: PLANE_END[0] - ROW_OUT, :]


def gates_gradient(where, attended, hidden_a, hidden_f, grad_a, grad_za, grad_zf, late, deps=()):
    total = hidden_a.shape[0]
    carry = PLANE_END[0] - ROW_OUT
    full = whole((total, D))
    return pl.pallas_call(
        without(gates_body, 7 + PAIRS, len(deps)),
        name="gates_gradient",
        grid_spec=pltpu.PrefetchScalarGridSpec(
            num_scalar_prefetch=1,
            grid=(1,),
            in_specs=[whole((total, PAIR))] * PAIRS + [full] * 5 + [whole(late.shape)] + [UNREAD] * len(deps),
            out_specs=PLANE_SPEC + [whole((carry, D))],
            scratch_shapes=[pltpu.VMEM((3 * D + late.shape[0], D), BF16)],
        ),
        out_shape=PLANE_OUT + [jax.ShapeDtypeStruct((carry, D), BF16)],
        compiler_params=VMEM,
        cost_estimate=pl.CostEstimate(flops=int(3.2e9), bytes_accessed=int(14e6), transcendentals=0),
    )(where, *attended, hidden_a, hidden_f, grad_a, grad_za, grad_zf, late, *deps)


LAST_ROWS = 512


def three_body(where, hidden_a, *refs):
    grads, refs = refs[: 3 * PAIRS], refs[3 * PAIRS :]
    late, keep, send, rows = refs
    hid = hidden_a[...]
    for part, at in enumerate((ROW_QUERY, ROW_KEY, ROW_VALUE)):
        grad = jnp.concatenate([grads[3 * pair + part][...] for pair in range(PAIRS)], 1)
        rows[at : at + D, :] = dot_tn(hid, grad).astype(BF16)
    rows[ROW_OUT:, :] = late[...]
    emit_blocks(rows, 0, 0, where, keep, send)


def three_gradient(where, hidden_a, grads, late, deps=()):
    total = hidden_a.shape[0]
    return pl.pallas_call(
        without(three_body, 3 + 3 * PAIRS, len(deps)),
        name="three_gradient",
        grid_spec=pltpu.PrefetchScalarGridSpec(
            num_scalar_prefetch=1,
            grid=(1,),
            in_specs=[whole((total, D))]
            + [whole((total, PAIR))] * (3 * PAIRS)
            + [whole(late.shape)]
            + [UNREAD] * len(deps),
            out_specs=PLANE_SPEC,
            scratch_shapes=[pltpu.VMEM((ROW_OUT + late.shape[0], D), BF16)],
        ),
        out_shape=PLANE_OUT,
        compiler_params=VMEM,
        cost_estimate=pl.CostEstimate(flops=int(3.2e9), bytes_accessed=int(12e6), transcendentals=0),
    )(where, hidden_a, *grads, late, *deps)


def last_body(steps, tok, grad_middle, grad_za, *refs):
    grads, refs = refs[: 3 * PAIRS], refs[3 * PAIRS :]
    w_three, refs = refs[:PAIRS], refs[PAIRS:]
    gate_attn, vec, input_grad, d_vec, factors, s_vec = refs
    step = pl.program_id(0)

    @pl.when(step == 0)
    def _():
        s_vec[...] = jnp.zeros_like(s_vec)
        for pair in range(PAIRS):
            factors[:, pair * PAIR : (pair + 1) * PAIR] = w_three[pair][...]

    vecs = vec[...].astype(F32)
    normed, inv_std = layer_stats(tok[...].astype(F32))
    grad_hidden = dot_nt(grad_za[...], gate_attn[...])
    for part, at in enumerate((ROW_QUERY, ROW_KEY, ROW_VALUE)):
        grad = jnp.concatenate([grads[3 * pair + part][...] for pair in range(PAIRS)], 1)
        grad_hidden += dot_nt(grad, factors[at : at + D, :])
    s_vec[0] += fold_rows(grad_hidden * normed)
    s_vec[1] += fold_rows(grad_hidden)
    input_grad[...] = (grad_middle[...] + norm_back(grad_hidden * vecs[0:1], normed, inv_std)).astype(BF16)

    @pl.when(step == steps - 1)
    def _():
        d_vec[...] = jnp.sum(s_vec[...], 1)


def last_part(tokens, grad_middle, grad_za, grads, w_three, gate_attn, vec, deps=()):
    total = tokens.shape[0]
    steps = total // LAST_ROWS
    rows_at = lambda width: pl.BlockSpec((LAST_ROWS, width), lambda i, *refs: (i, 0))
    return pl.pallas_call(
        without(functools.partial(last_body, steps), 5 + 4 * PAIRS, len(deps)),
        name="last_part",
        grid=(steps,),
        in_specs=[rows_at(D)] * 3
        + [rows_at(PAIR)] * (3 * PAIRS)
        + [whole((ROW_OUT, PAIR))] * PAIRS
        + [whole((D, D)), whole((VEC_ROWS, D))]
        + [UNREAD] * len(deps),
        out_specs=[rows_at(D), whole((VEC_ROWS, D))],
        scratch_shapes=[
            pltpu.VMEM((ROW_OUT, D), BF16),
            pltpu.VMEM((VEC_ROWS, 8, D), F32),
        ],
        out_shape=[jax.ShapeDtypeStruct((total, D), BF16), jax.ShapeDtypeStruct((VEC_ROWS, D), F32)],
        compiler_params=VMEM,
        cost_estimate=pl.CostEstimate(flops=int(4.3e9), bytes_accessed=int(20e6), transcendentals=0),
    )(tokens, grad_middle, grad_za, *grads, *w_three, gate_attn, vec, *deps)


def local_part(where, longs, tokens, out_grad, first_pieces, later_pieces, middle_pieces, wait, collect):
    subs, length, unused = tokens.shape
    rows = tokens.reshape(subs * length, D)
    grads_in = out_grad.reshape(subs * length, D)
    *kept, hidden_a, vec = pair_forward(True, 0, longs, where, rows, first_pieces)
    pairs = [kept]
    for pair in range(1, PAIRS):
        pairs.append(pair_forward(False, pair - 1, longs, where, hidden_a, later_pieces, wait(f"pair{pair}")))
    attended = [pair[3] for pair in pairs]
    (outputs, grad_middle, grad_za, grad_attended, hidden_f, active, grad_pre, grad_f, grad_zf, grad_a, d_vec, gate_attn) = (
        middle_part(where, rows, grads_in, hidden_a, attended, [pair[6] for pair in pairs], middle_pieces)
    )
    *plane, carry = down_gradient(where, active, grad_f, d_vec)
    collect(3, *plane)
    *plane, carry = up_gradient(where, hidden_f, grad_pre, carry, wait("up"))
    collect(2, *plane)
    *plane, carry = gates_gradient(
        where, attended, hidden_a, hidden_f, grad_a, grad_za, grad_zf, carry, wait("gates")
    )
    collect(1, *plane)
    grads = []
    for pair, (query, key, value, att, extra, *unused_two) in enumerate(pairs):
        grads += attend_back(pair, longs, query, key, value, extra, att, grad_attended, wait(f"back{pair}"))
    collect(0, *three_gradient(where, hidden_a, grads, carry, wait("three")))
    input_grad, d_vec = last_part(
        rows, grad_middle, grad_za, grads, [pair[5] for pair in pairs], gate_attn, vec, wait("last")
    )
    return outputs.reshape(tokens.shape), input_grad.reshape(tokens.shape), d_vec


def own_block(params, start, rows):
    share = params.shape[0]
    room = jnp.pad(params, (TILE, rows * D - share))
    return lax.dynamic_slice(room, (TILE - start % TILE,), (rows * D,)).reshape(rows, D).astype(BF16)


def narrow_vec(vec):
    return jnp.concatenate([vec[:, i * PAIR : (i + 1) * PAIR] for i in range(D // PAIR)], 0)


def move(axis, count, step):
    perm = [(i, step(i)) for i in range(count) if step(i) is not None]
    return lambda value: lax.ppermute(value, axis, perm)


def on_slice(tokens, out_grad, long_count, params):
    z, x, y, c = (lax.axis_index(axis) for axis in ("z", "x", "y", "c"))
    me = ((z * 2 + x) * 2 + y) * 2 + c
    share = params.shape[0]
    block = own_block(params, me * share, BLOCK)
    odd = z % 2 == 1
    ends = (z == 0) | (z == 3)
    swap_c = move("c", 2, lambda i: 1 - i)
    swap_x = move("x", 2, lambda i: 1 - i)
    swap_y = move("y", 2, lambda i: 1 - i)
    swap_xy = move(("x", "y"), 4, lambda i: 3 - i)
    z_one = move("z", 4, lambda i: i ^ 1)
    z_two = move("z", 4, lambda i: i ^ 2)
    z_ends = move("z", 4, lambda i: {0: 2, 3: 1}.get(i))
    z_mid = move("z", 4, lambda i: {1: 2, 2: 1}.get(i))
    z_out = move("z", 4, lambda i: {1: 0, 2: 3}.get(i))

    vec = block[VEC_AT : VEC_AT + VEC_ROWS]
    vec = narrow_vec(jnp.where(me == SHARES - 1, vec, jnp.zeros_like(vec)))
    mine_a = jnp.concatenate([block[:, :PAIR], vec], 0)
    mine_b = block[:, PAIR:]
    held_a = jnp.where(ends, mine_a, z_ends(mine_a))
    held_b = jnp.where(ends, mine_b, z_ends(mine_b))
    got_mid = z_mid(block)
    other_a = z_one(held_a)
    other_b = z_one(held_b)
    low_a, high_a = jnp.where(odd, other_a, held_a), jnp.where(odd, held_a, other_a)
    low_b, high_b = jnp.where(odd, other_b, held_b), jnp.where(odd, held_b, other_b)
    both = jnp.stack([jnp.where(z == 1, block, got_mid), jnp.where(z == 1, got_mid, block)])
    got_out = z_out(both)
    both = jnp.where(ends, got_out, both)
    low_a = jnp.concatenate([low_a[:BLOCK], high_a[BLOCK:]], 0)

    def straight(value):
        near = jnp.stack([value, swap_y(value), swap_x(value), swap_xy(value)])
        blocks = [(0, spot) for spot in range(HALF)]
        return [Piece(near, blocks, False, 0), Piece(swap_c(near), blocks, True, 0)]

    first_pieces = straight(low_a)
    later_pieces = straight(low_b)

    def two_steps(value, planes, one, one_spot, two, two_spot, column):
        step_one = one(value)
        held = jnp.concatenate([value, step_one], 0)
        got = two(held)
        blocks = [(plane, spot) for spot in (0, one_spot) for plane in planes]
        later = [(plane, spot ^ two_spot) for plane, spot in blocks]
        pieces = [
            Piece(held, blocks, False, column),
            Piece(got, later, False, column),
            Piece(swap_c(held), blocks, True, column),
            Piece(swap_c(got), later, True, column),
        ]
        return step_one, got, pieces

    high = jnp.concatenate([high_a[:BLOCK], high_b], 1)[None]
    step_high, got_high, middle_pieces = two_steps(high, (3,), swap_y, 1, swap_x, 2, 0)
    step_left, got_left, pieces = two_steps(both[:, :, : D // 2], (1, 2), swap_x, 2, swap_y, 1, 0)
    middle_pieces = middle_pieces + pieces
    step_right, got_right, pieces = two_steps(both[:, :, D // 2 :], (1, 2), swap_y, 1, swap_x, 2, D // 2)
    middle_pieces = middle_pieces + pieces

    waits = {
        "pair1": [step_high],
        "pair2": [step_left, step_right, got_high],
        "pair3": [],
    }

    parts, totals, arrived = {}, {}, {}

    def core_sum(plane):
        keep, got = arrived[plane]
        parts[plane] = (keep.astype(F32) + got.astype(F32)).astype(BF16)
        part = parts[plane]
        arrived[plane] = (swap_y(part[1]), swap_x(part[2]), swap_xy(part[3]))

    def plane_sum(plane):
        total = parts[plane][0].astype(F32)
        for got in arrived[plane]:
            total = total + got.astype(F32)
        totals[plane] = total.astype(BF16)

    def collect(plane, keep, send):
        arrived[plane] = (keep, swap_c(send))
        if plane == 0:
            core_sum(0)

    z_state = {}

    def wait(name):
        if name in waits:
            return waits[name]
        if name == "gates":
            core_sum(3)
            return [parts[3]]
        if name == "back0":
            core_sum(2)
            return [parts[2]]
        if name == "back1":
            core_sum(1)
            plane_sum(3)
            return [totals[3], parts[1]]
        if name == "back2":
            plane_sum(2)
            return [totals[2]]
        if name == "back3":
            plane_sum(1)
            lower = z < 2
            z_state["two"] = z_two(jnp.stack([jnp.where(lower, totals[2], totals[1]), totals[3]]))
            return [totals[1]]
        if name == "last":
            return [z_state["two"]]
        return []

    where = jnp.stack([z, x, y, c]).astype(jnp.int32)
    outputs, input_grad, d_vec = local_part(
        where,
        long_count.reshape(-1),
        tokens,
        out_grad,
        first_pieces,
        later_pieces,
        middle_pieces,
        wait,
        collect,
    )
    lower = z < 2
    got = z_state["two"]
    near = jnp.where(lower, totals[1], totals[2]).astype(F32) + got[0].astype(F32)
    far = totals[3].astype(F32) + got[1].astype(F32)
    got = z_one(jnp.where(z == 2, far, near).astype(BF16)).astype(F32)
    total = jnp.where(z == 3, far, near) + got
    plane_sum(0)
    gains = d_vec[:2]
    for swap in (swap_c, swap_x, swap_y):
        gains = gains + swap(gains)
    low = totals[0].astype(F32) + z_two(totals[0]).astype(F32)
    low = low + z_one(low.astype(BF16)).astype(F32)
    for swap in (z_two, z_one):
        gains = gains + swap(gains)
    total = jnp.where(z == 0, low, total)
    gains = jnp.where(me == SHARES - 1, gains, jnp.zeros_like(gains))
    total = total + jnp.pad(gains, ((VEC_AT, BLOCK - VEC_AT - 2), (0, 0)))
    param_grad = lax.dynamic_slice(total.reshape(-1), ((me * share) % TILE,), (share,))
    return (outputs, input_grad, param_grad)


def on_any(axes, count, tokens, out_grad, long_count, params):
    share = params.shape[0]
    me = lax.axis_index(axes)
    starts = [index * share // TILE * TILE_ROWS for index in range(count)]
    rows = max(-(-((index + 1) * share) // TILE) * TILE_ROWS - starts[index] for index in range(count))
    gathered = lax.all_gather(own_block(params, me * share, rows), axes, axis=0)
    merged = jnp.zeros((starts[-1] + rows, D), BF16)
    for index in range(count):
        merged = merged.at[starts[index] : starts[index] + rows].add(gathered[index])
    merged = merged[:ALL_ROWS]
    near, far = [], []
    for plane in range(PLANES):
        blocks = []
        for index in range(plane * IN_PLANE, (plane + 1) * IN_PLANE):
            end = STARTS[index + 1] if index + 1 < SHARES else ALL_ROWS
            piece = merged[STARTS[index] : end]
            blocks.append(jnp.pad(piece, ((0, BLOCK - piece.shape[0]), (0, 0))))
        spots = [(plane, spot) for spot in range(HALF)]
        near.append(Piece(jnp.stack(blocks[0::2]), spots, False, 0))
        far.append(Piece(jnp.stack(blocks[1::2]), spots, True, 0))
    vec = narrow_vec(merged[ROW_VEC : ROW_VEC + VEC_ROWS])
    first_pieces, later_pieces = [], []
    for piece in (near[0], far[0]):
        lines = jnp.zeros((HALF,) + vec.shape, BF16)
        if piece is near[0]:
            lines = lines.at[0].set(vec)
        whole_piece = jnp.concatenate([piece.array[:, :, :PAIR], lines], 1)
        first_pieces.append(Piece(whole_piece, piece.blocks, piece.other, 0))
        later_pieces.append(Piece(piece.array[:, :, PAIR:], piece.blocks, piece.other, 0))
    by_share = [None] * SHARES

    def collect(plane, keep, send):
        for spot in range(HALF):
            by_share[plane * IN_PLANE + 2 * spot] = keep[spot]
            by_share[plane * IN_PLANE + 2 * spot + 1] = send[spot]

    outputs, input_grad, d_vec = local_part(
        jnp.zeros((4,), jnp.int32),
        long_count.reshape(-1),
        tokens,
        out_grad,
        first_pieces,
        later_pieces,
        near[1:] + far[1:],
        lambda name: [],
        collect,
    )
    ends = STARTS[1:] + [ALL_ROWS]
    gradient = jnp.concatenate([part[: ends[i] - STARTS[i]] for i, part in enumerate(by_share)], 0)
    gradient = gradient.at[ROW_VEC : ROW_VEC + VEC_ROWS].add(d_vec.astype(BF16))
    gradient = jnp.pad(gradient, ((0, max(0, starts[-1] + rows - ALL_ROWS)), (0, 0)))
    spread = jnp.stack([gradient[start : start + rows] for start in starts])
    summed = lax.psum_scatter(spread, axes, scatter_dimension=0)
    param_grad = lax.dynamic_slice(summed.astype(F32).reshape(-1), ((me * share) % TILE,), (share,))
    return (outputs, input_grad, param_grad)


def solution(mesh):
    axes = ("wide", "narrow")
    count = math.prod(mesh.shape[axis] for axis in axes)
    step = functools.partial(on_any, axes, count)
    if mesh.shape["wide"] == 8 and mesh.shape["narrow"] == 4:
        axes = ("z", "x", "y", "c")
        mesh = Mesh(mesh.devices.reshape(4, 2, 2, 2), axes)
        step = on_slice
    return jax.shard_map(
        step,
        mesh=mesh,
        in_specs=(P(None, axes, None), P(None, axes, None), P(None, axes), P(axes)),
        out_specs=(P(None, axes, None), P(None, axes, None), P(axes)),
        check_vma=False,
    )
```

```python
import functools
import math

import jax
import jax.numpy as jnp
from jax import lax
from jax.experimental import pallas as pl
from jax.experimental.pallas import tpu as pltpu
from jax.sharding import Mesh, PartitionSpec as P

D = 512
FF = 2048
HEADS = 8
HD = 64
SHORT = 512
LONG = 1024
PAIR = 2 * HD
GROUP = 2 * PAIR
GROUPS = D // GROUP
STRIP = 256

TILE_ROWS = 16
TILE = TILE_ROWS * D

layer_eps = 1e-05
far_below = -1e30

F32 = jnp.float32
BF16 = jnp.bfloat16
MB = 1024 * 1024


def dot_nn(left, right):
    return lax.dot_general(left, right, (((1,), (0,)), ((), ())), preferred_element_type=F32)


def dot_nt(left, right):
    return lax.dot_general(left, right, (((1,), (1,)), ((), ())), preferred_element_type=F32)


def dot_tn(left, right):
    return lax.dot_general(left, right, (((0,), (0,)), ((), ())), preferred_element_type=F32)


def layer_stats(values):
    average = jnp.mean(values, -1, keepdims=True)
    centred = values - average
    variance = jnp.mean(centred * centred, -1, keepdims=True)
    inv_std = lax.rsqrt(variance + layer_eps)
    return (centred * inv_std, inv_std)


def norm_back(grad_hat, normed, inv_std):
    return inv_std * (
        grad_hat
        - jnp.mean(grad_hat, -1, keepdims=True)
        - normed * jnp.mean(grad_hat * normed, -1, keepdims=True)
    )


def sigmoid(values):
    return 0.5 * jnp.tanh(0.5 * values) + 0.5


def fold_rows(values):
    return jnp.sum(values.reshape(values.shape[0] // 8, 8, values.shape[1]), 0)


ROW_QUERY = 0
ROW_KEY = 512
ROW_VALUE = 1024
ROW_OUT = 1536
ROW_GATE_A = 2048
ROW_GATE_F = 2560
ROW_IN = 3072
ROW_DOWN = 5120
ROW_VEC = 7168
ALL_ROWS = 7184
VEC_ROWS = 16
ENTRIES = 6 * D * D + 2 * D * FF + 8 * D + FF

SHARES = 32
PLANES = 4
IN_PLANE = SHARES // PLANES
HALF = IN_PLANE // 2
STARTS = [index * (ENTRIES // SHARES) // TILE * TILE_ROWS for index in range(SHARES)]
BLOCK = max(
    -(-((index + 1) * (ENTRIES // SHARES)) // TILE) * TILE_ROWS - STARTS[index] for index in range(SHARES)
)
PLANE_END = [STARTS[(plane + 1) * IN_PLANE - 1] + BLOCK for plane in range(PLANES)]
VEC_AT = ROW_VEC - STARTS[-1]

VMEM = pltpu.CompilerParams(vmem_limit_bytes=60 * MB)


def whole(shape, single=True):
    rank = len(shape)
    kwargs = {"pipeline_mode": pl.Buffered(1)} if single else {}
    return pl.BlockSpec(shape, lambda *unused: (0,) * rank, **kwargs)


def share_row(where, plane, spot, other):
    core = 1 - where[3] if other else where[3]
    share = 2 * ((where[1] * 2 + where[2]) ^ spot) + core
    return ((plane * IN_PLANE + share) * (ENTRIES // SHARES)) // TILE * TILE_ROWS


class Piece:
    def __init__(self, array, blocks, other, column):
        self.array, self.blocks, self.other, self.column = array, blocks, other, column


def place_piece(target, base, where, piece, source, lowest):
    width = min(source.shape[-1], target.shape[-1] - piece.column)

    def place(index, plane, spot):
        at = share_row(where, plane, spot, piece.other) - base
        rows = pl.ds(pl.multiple_of(at, TILE_ROWS), BLOCK)
        cols = slice(piece.column, piece.column + width)
        target[rows, cols] = target[rows, cols] + source[index, :BLOCK, :width]

    for index, (plane, spot) in enumerate(piece.blocks):
        if not isinstance(plane, tuple):
            if (plane == 0) == lowest:
                place(index, plane, spot)
            continue
        plane = where[plane[0]]
        pl.when((plane == 0) == lowest)(functools.partial(place, index, plane, spot))


UNREAD = pl.BlockSpec(memory_space=pl.ANY)


def call_kernel(body, arguments, through, in_specs, out_specs, out_shape, grid, name, cost, scalars=1, scratch=(), alias=None):
    inputs, outputs, passed = len(arguments), len(out_specs), len(through)
    aliases = {inputs + index: outputs + index for index in range(passed)}
    aliases.update(alias or {})

    def run(*refs):
        at = inputs + passed
        body(*refs[:inputs], *refs[at : at + outputs], *refs[at + outputs + passed :])

    results = pl.pallas_call(
        run,
        name=name,
        grid_spec=pltpu.PrefetchScalarGridSpec(
            num_scalar_prefetch=scalars,
            grid=grid,
            in_specs=list(in_specs) + [UNREAD] * passed,
            out_specs=list(out_specs) + [UNREAD] * passed,
            scratch_shapes=list(scratch),
        ),
        out_shape=list(out_shape) + [jax.ShapeDtypeStruct(array.shape, array.dtype) for array in through],
        input_output_aliases=aliases,
        compiler_params=VMEM,
        cost_estimate=pl.CostEstimate(flops=int(cost[0]), bytes_accessed=int(cost[1]), transcendentals=int(cost[2])),
    )(*arguments, *through)
    return results[:outputs], results[outputs:]


def emit_blocks(source, base, plane, where, keep, send):
    @pl.loop(0, HALF)
    def _(spot):
        for out, other in ((keep, False), (send, True)):
            at = share_row(where, plane, spot, other) - base
            out[spot] = source[pl.ds(pl.multiple_of(at, TILE_ROWS), BLOCK), :]


def split_three(values):
    high = values.astype(BF16)
    rest = values - high.astype(F32)
    middle = rest.astype(BF16)
    low = (rest - middle.astype(F32)).astype(BF16)
    return high, middle, low


def pick_lanes(base, lane, first, columns):
    out = base
    for offset, column in enumerate(columns):
        out = jnp.where(lane == first + offset, column, out)
    return out


def pipeline(units, *stages):
    held, results = {}, {}
    count = len(units)
    for turn in range(count + len(stages) - 1):
        for at in range(len(stages)):
            stage = (0, *range(len(stages) - 1, 0, -1))[at]
            unit = turn - stage
            if 0 <= unit < count:
                value = stages[stage](units[unit], *(held.pop(unit) if stage else ()))
                if stage + 1 < len(stages):
                    held[unit] = value
                else:
                    results[units[unit]] = value
    return results


def attend_columns(is_long, query, key, value, attended, extra):
    strips = LONG // STRIP
    key_ids = lax.broadcasted_iota(jnp.int32, (STRIP, STRIP), 0)
    query_ids = lax.broadcasted_iota(jnp.int32, (STRIP, STRIP), 1)
    causal = query_ids >= key_ids
    cut = jnp.where(is_long, 0.0, far_below)
    late = jnp.where(is_long, 0.0, 1.0)
    lane = lax.broadcasted_iota(jnp.int32, (LONG, PAIR), 1)
    ones = jnp.ones((TILE_ROWS, LONG), BF16)
    q_heads, k_pairs, v_heads = [], [], []
    for pair in range(query.shape[1] // PAIR):
        cols = slice(pair * PAIR, (pair + 1) * PAIR)
        rows = query[:, cols]
        zero = jnp.zeros_like(rows)
        q_heads += [jnp.where(lane < HD, rows, zero), jnp.where(lane >= HD, rows, zero)]
        k_pairs.append(key[:, cols])
        turned = value[:, cols].astype(F32).T.astype(BF16)
        v_heads += [jnp.concatenate([turned[:HD], ones], 0), jnp.concatenate([turned[HD:], ones], 0)]

    def scores_of(unit):
        strip, head = unit
        lo, reach = strip * STRIP, (strip + 1) * STRIP
        return (dot_nt(k_pairs[head // 2][:reach], q_heads[head][lo:reach]),)

    def soften(unit, scores):
        strip, unused = unit
        lo = strip * STRIP
        parts = []
        if lo >= SHORT:
            parts.append(scores[:SHORT] + cut)
            if lo > SHORT:
                parts.append(scores[SHORT:lo])
        elif strip:
            parts.append(scores[:lo])
        parts.append(jnp.where(causal, scores[lo:], far_below))
        scores = jnp.concatenate(parts, 0)
        largest = jnp.max(scores, 0, keepdims=True)
        return jnp.exp(scores - largest).astype(BF16), largest

    def finish(unit, shifted, largest):
        strip, head = unit
        out = dot_nn(v_heads[head][:, : (strip + 1) * STRIP], shifted)
        sum_exp = out[HD : HD + 1]
        return out[:HD] * (1.0 / sum_exp), largest + jnp.log(sum_exp)

    units = [(strip, head) for strip in range(strips) for head in range(len(q_heads))]
    results = pipeline(units, scores_of, soften, finish)
    for strip in range(strips):
        rows = slice(strip * STRIP, (strip + 1) * STRIP)
        for pair in range(len(k_pairs)):
            cols = slice(pair * PAIR, (pair + 1) * PAIR)
            two = [results[(strip, 2 * pair + side)] for side in range(2)]
            attended[rows, cols] = jnp.concatenate([out for out, unused in two], 0).T.astype(BF16)
            lines = [part.astype(F32) for unused, logsum in two for part in split_three(-logsum)]
            lines.append(jnp.broadcast_to(late if strip * STRIP >= SHORT else 0.0, (1, STRIP)))
            lines.append(jnp.zeros((PAIR - 7, STRIP), F32))
            extra[rows, cols] = jnp.concatenate(lines, 0).T.astype(BF16)


def forward_body(first, pieces, longs, where, rows_in, *rest):
    sources, rest = rest[: len(pieces)], rest[len(pieces) :]
    if first:
        query, key, value, attended, extra, w_three, w_out, hidden, vec, weights = rest
    else:
        query, key, value, attended, extra, w_three, w_out, weights = rest
    sub = pl.program_id(0)

    @pl.when(sub == 0)
    def _():
        weights[...] = jnp.zeros_like(weights)
        for piece, source in zip(pieces, sources):
            place_piece(weights, 0, where, piece, source, True)
        w_three[...] = weights[:ROW_OUT, :]
        w_out[...] = weights[ROW_OUT:, :]
        if first:
            total = jnp.zeros((VEC_ROWS, D), BF16)
            for source in sources:
                if source.shape[1] > BLOCK:
                    for index in range(source.shape[0]):
                        total = total + source[index, BLOCK:, :]
            vec[...] = total

    if first:
        normed, unused = layer_stats(rows_in[...].astype(F32))
        lines = vec[...].astype(F32)
        hid = (normed * lines[0:1] + lines[1:2]).astype(BF16)
        hidden[...] = hid
    else:
        hid = rows_in[...]
    q_rows = (dot_nn(hid, weights[ROW_QUERY : ROW_QUERY + D, :]) * (1.0 / math.sqrt(HD))).astype(BF16)
    k_rows = dot_nn(hid, weights[ROW_KEY : ROW_KEY + D, :]).astype(BF16)
    v_rows = dot_nn(hid, weights[ROW_VALUE : ROW_VALUE + D, :]).astype(BF16)
    query[...] = q_rows
    key[...] = k_rows
    value[...] = v_rows
    attend_columns(longs[sub] > 0, q_rows, k_rows, v_rows, attended, extra)


def forward_group(group, longs, where, rows_in, pieces, through):
    first = group == 0
    total = rows_in.shape[0]
    rows = pl.BlockSpec((LONG, D), lambda s, *refs: (s, 0))
    part = pl.BlockSpec((LONG, GROUP), lambda s, *refs: (s, 0))
    width = D if first else GROUP
    blocks = [
        pl.BlockSpec(piece.array.shape[:2] + (width,), lambda s, *refs: (0, 0, group), pipeline_mode=pl.Buffered(1))
        for piece in pieces
    ]
    tail = PLANE_END[0] - ROW_OUT
    out_specs = [part] * 5 + [whole((ROW_OUT, GROUP)), whole((tail, GROUP))]
    out_shape = [jax.ShapeDtypeStruct((total, GROUP), BF16)] * 5 + [
        jax.ShapeDtypeStruct((ROW_OUT, GROUP), BF16),
        jax.ShapeDtypeStruct((tail, GROUP), BF16),
    ]
    if first:
        out_specs += [rows, whole((VEC_ROWS, D))]
        out_shape += [jax.ShapeDtypeStruct((total, D), BF16), jax.ShapeDtypeStruct((VEC_ROWS, D), BF16)]
    return call_kernel(
        functools.partial(forward_body, first, pieces),
        [longs, where, rows_in, *[piece.array for piece in pieces]],
        through,
        [rows] + blocks,
        out_specs,
        out_shape,
        (total // LONG,),
        "forward_group",
        (8e9, 12e6, 4e6) if first else (0, 0, 0),
        scalars=2,
        scratch=[pltpu.VMEM((PLANE_END[0], GROUP), BF16)],
    )


def attend_back_rows(query, key, value, extra, attended, grad, grad_query, grad_key, grad_value):
    strips = LONG // STRIP
    lane = lax.broadcasted_iota(jnp.int32, (LONG, PAIR), 1)
    row = lax.broadcasted_iota(jnp.int32, (LONG, PAIR), 0)
    row_ids = lax.broadcasted_iota(jnp.int32, (STRIP, STRIP), 0)
    col_ids = lax.broadcasted_iota(jnp.int32, (STRIP, STRIP), 1)
    causal = col_ids >= row_ids
    early = jnp.where((lane == 6) & (row < SHORT), far_below, 0.0)
    v_tail = jnp.where(lane < 3, 1.0, 0.0).astype(BF16)
    heads, pairs = [], query.shape[1] // PAIR
    for pair in range(pairs):
        cols = slice(pair * PAIR, (pair + 1) * PAIR)
        q_all, k_all, v_all, g_all, x_all = (ref[:, cols] for ref in (query, key, value, grad, extra))
        product = g_all.astype(F32) * attended[:, cols].astype(F32)
        zero = jnp.zeros_like(q_all)
        v_wide = jnp.concatenate([v_all, v_tail], 1)
        turned = k_all.astype(F32).T.astype(BF16)
        for side in range(2):
            mine = (lane < HD) if side == 0 else (lane >= HD)
            delta = jnp.sum(jnp.where(mine, product, 0.0), -1, keepdims=True)
            d_tail = pick_lanes(
                jnp.zeros((LONG, PAIR), F32), lane, 0, [part.astype(F32) for part in split_three(-delta)]
            )
            q_head = jnp.where(mine, q_all, zero)
            g_head = jnp.where(mine, g_all, zero)
            ones = jnp.where((lane >= 3 * side) & (lane < 3 * side + 3), 1.0, early).astype(BF16)
            heads.append(
                (
                    q_head,
                    g_head,
                    turned[side * HD : (side + 1) * HD],
                    jnp.concatenate([q_head, x_all], 1),
                    jnp.concatenate([g_head, d_tail.astype(BF16)], 1),
                    jnp.concatenate([k_all, ones], 1),
                    v_wide,
                )
            )

    def products(unit):
        block, head = unit
        lo, hi = block * STRIP, (block + 1) * STRIP
        unused, unused, unused, q_wide, g_wide, k_wide, v_wide = heads[head]
        return dot_nt(k_wide[lo:hi], q_wide[lo:]), dot_nt(v_wide[lo:hi], g_wide[lo:])

    def soften(unit, scores, slope):
        soft = jnp.exp(scores)
        first = jnp.where(causal, soft[:, :STRIP], 0.0)
        soft = first if soft.shape[1] == STRIP else jnp.concatenate([first, soft[:, STRIP:]], 1)
        return soft.astype(BF16), (soft * slope).astype(BF16)

    query_sum = {}

    def gradients(unit, soft, scores):
        block, head = unit
        lo, hi = block * STRIP, (block + 1) * STRIP
        q_head, g_head, k_turned, *unused = heads[head]
        part = dot_nn(k_turned[:, lo:hi], scores)
        for later in range(block, strips):
            piece = part[:, (later - block) * STRIP : (later - block + 1) * STRIP]
            at = (later, head)
            query_sum[at] = query_sum[at] + piece if at in query_sum else piece
        return dot_nn(soft, g_head[lo:]), dot_nn(scores, q_head[lo:])

    units = [(block, head) for block in range(strips) for head in range(len(heads))]
    results = pipeline(units, products, soften, gradients)
    for block in range(strips):
        rows = slice(block * STRIP, (block + 1) * STRIP)
        for pair in range(pairs):
            cols = slice(pair * PAIR, (pair + 1) * PAIR)
            (value_a, key_a), (value_b, key_b) = results[(block, 2 * pair)], results[(block, 2 * pair + 1)]
            grad_value[rows, cols] = (value_a + value_b).astype(BF16)
            grad_key[rows, cols] = (key_a + key_b).astype(BF16)
            two = jnp.concatenate([query_sum[(block, 2 * pair + side)] for side in range(2)], 0)
            grad_query[rows, cols] = (two * (1.0 / math.sqrt(HD))).T.astype(BF16)


def backward_body(steps, where, query, key, value, extra, attended, grad, hidden, late, *refs):
    grad_query, grad_key, grad_value, keep, send, total, rows = refs
    step = pl.program_id(0)
    attend_back_rows(query, key, value, extra, attended, grad, grad_query, grad_key, grad_value)
    three = jnp.concatenate([grad_query[...], grad_key[...], grad_value[...]], 1)
    now = dot_tn(hidden[...], three)

    @pl.when(step == 0)
    def _():
        total[...] = now

    @pl.when(step > 0)
    def _():
        total[...] = total[...] + now

    @pl.when(step == steps - 1)
    def _():
        for part, at in enumerate((ROW_QUERY, ROW_KEY, ROW_VALUE)):
            rows[at : at + D, :] = total[:, part * GROUP : (part + 1) * GROUP].astype(BF16)
        rows[ROW_OUT:, :] = late[...]
        emit_blocks(rows, 0, 0, where, keep, send)


def backward_group(group, where, query, key, value, extra, attended, grad, hidden, late, through):
    total = query.shape[0]
    steps = total // LONG
    part = pl.BlockSpec((LONG, GROUP), lambda s, *refs: (s, 0))
    block = (HALF, BLOCK, GROUP)
    return call_kernel(
        functools.partial(backward_body, steps),
        [where, query, key, value, extra, attended, grad, hidden, late],
        through,
        [part] * 5
        + [
            pl.BlockSpec((LONG, GROUP), lambda s, *refs: (s, group)),
            pl.BlockSpec((LONG, D), lambda s, *refs: (s, 0)),
            pl.BlockSpec((late.shape[0], GROUP), lambda s, *refs: (0, group), pipeline_mode=pl.Buffered(1)),
        ],
        [part] * 3 + [whole(block)] * 2,
        [jax.ShapeDtypeStruct((total, GROUP), BF16)] * 3 + [jax.ShapeDtypeStruct(block, BF16)] * 2,
        (steps,),
        "backward_group",
        (14e9, 16e6, 4e6),
        scratch=[
            pltpu.VMEM((D, 3 * GROUP), F32),
            pltpu.VMEM((ROW_OUT + late.shape[0], GROUP), BF16),
        ],
    )


MID_ROWS = 512
HALF_ROWS = 256
CHUNKS = FF // D
TANH_SCALE = math.sqrt(2.0 / math.pi)


def spread_matrix(size):
    quarter = size // CHUNKS
    to = lax.broadcasted_iota(jnp.int32, (size, size), 0)
    source = lax.broadcasted_iota(jnp.int32, (size, size), 1)
    return (source == CHUNKS * (to % quarter) + to // quarter).astype(BF16)


def interleave(parts):
    started, live = 0, []
    while started < len(parts) or live:
        if started < len(parts):
            live.append(parts[started])
            started += 1
        live = [part for part in live if next(part, True) is None]


def middle_body(steps, pieces, where, tok, grad_out, hidden_a, *refs):
    att_refs, wo_refs, refs = refs[:GROUPS], refs[GROUPS : 2 * GROUPS], refs[2 * GROUPS :]
    sources, refs = refs[: len(pieces)], refs[len(pieces) :]
    (outputs, grad_middle_ref, grad_za_ref, grad_attended, hid_f_ref, chunks_ref, grad_f_ref) = refs[:7]
    (grad_zf_ref, grad_a_ref, d_vec, gate_copy, weights, wide, slope, s_vec) = refs[7:]
    step = pl.program_id(0)
    base = ROW_OUT

    @pl.when(step == 0)
    def _():
        weights[...] = jnp.zeros_like(weights)
        for group in range(GROUPS):
            weights[: PLANE_END[0] - ROW_OUT, group * GROUP : (group + 1) * GROUP] = wo_refs[group][...]
        for piece, source in zip(pieces, sources):
            place_piece(weights, base, where, piece, source, False)
        shuffle = spread_matrix(256)
        for block in range(FF // 256):
            at = ROW_IN - base + block * 256
            part = dot_nn(shuffle, weights[at : at + 256, :]).astype(BF16)
            for chunk in range(CHUNKS):
                wide[chunk, block * 64 : (block + 1) * 64, :] = part[chunk * 64 : (chunk + 1) * 64]
        gate_copy[...] = weights[ROW_GATE_A - base : ROW_GATE_A - base + D, :]
        s_vec[...] = jnp.zeros_like(s_vec)

    w_out = weights.at[ROW_OUT - base : ROW_OUT - base + D]
    gate_attn = weights.at[ROW_GATE_A - base : ROW_GATE_A - base + D]
    gate_ffn = weights.at[ROW_GATE_F - base : ROW_GATE_F - base + D]
    w_down = weights.at[ROW_DOWN - base : ROW_DOWN - base + FF]
    vecs = weights[ROW_VEC - base : ROW_VEC - base + VEC_ROWS, :].astype(F32)
    chunks = [slice(chunk * D, (chunk + 1) * D) for chunk in range(CHUNKS)]

    def part(here):
        hid_a = hidden_a[here, :]
        att = jnp.concatenate([ref[here, :] for ref in att_refs], 1)
        grad = grad_out[here, :].astype(F32)
        branch_a = dot_nn(att, w_out[...])
        gate_a = dot_nn(hid_a, gate_attn[...])
        yield
        branch_a = branch_a + vecs[2:3]
        gate_a = sigmoid(gate_a + vecs[3:4])
        middle = tok[here, :].astype(F32) + gate_a * branch_a
        normed, inv_std = layer_stats(middle)
        hid_f = (normed * vecs[4:5] + vecs[5:6]).astype(BF16)
        hid_f_ref[here, :] = hid_f
        yield
        gate_f = dot_nn(hid_f, gate_ffn[...])
        pre = dot_nn(hid_f, wide[0])
        yield
        branch_f = vecs[6:7]
        for chunk, cols in enumerate(chunks):
            pre = pre + vecs[8 + chunk : 9 + chunk]
            square = pre * pre
            bend = jnp.tanh(pre * (TANH_SCALE + (TANH_SCALE * 0.044715) * square))
            half = 0.5 * (1.0 + bend)
            active = (pre * half).astype(BF16)
            slope[here, cols] = half + (0.5 * pre) * (1.0 - bend * bend) * (
                TANH_SCALE + (3.0 * 0.044715 * TANH_SCALE) * square
            )
            chunks_ref[chunk, here, :] = active
            yield
            if chunk + 1 < CHUNKS:
                pre = dot_nn(hid_f, wide[chunk + 1])
            branch_f = branch_f + dot_nn(active, w_down[cols, :])
            yield
        gate_f = sigmoid(gate_f + vecs[7:8])
        outputs[here, :] = (middle + gate_f * branch_f).astype(BF16)
        grad_branch_f = (grad * gate_f).astype(BF16)
        grad_zf = (grad * branch_f * gate_f * (1.0 - gate_f)).astype(BF16)
        grad_f_ref[here, :] = grad_branch_f
        grad_zf_ref[here, :] = grad_zf
        s_vec[6] += fold_rows(grad_branch_f.astype(F32))
        s_vec[7] += fold_rows(grad_zf.astype(F32))
        yield
        grad_hidden = dot_nt(grad_zf, gate_ffn[...])
        grad_active = dot_nt(grad_branch_f, w_down[chunks[0], :])
        yield
        for chunk, cols in enumerate(chunks):
            grad_pre = (grad_active * slope[here, cols]).astype(BF16)
            chunks_ref[CHUNKS + chunk, here, :] = grad_pre
            s_vec[8 + chunk] += fold_rows(grad_pre.astype(F32))
            yield
            if chunk + 1 < CHUNKS:
                grad_active = dot_nt(grad_branch_f, w_down[chunks[chunk + 1], :])
            grad_hidden = grad_hidden + dot_nt(grad_pre, wide[chunk])
            yield
        s_vec[4] += fold_rows(grad_hidden * normed)
        s_vec[5] += fold_rows(grad_hidden)
        grad_middle = grad + norm_back(grad_hidden * vecs[4:5], normed, inv_std)
        grad_middle_ref[here, :] = grad_middle
        grad_branch_a = (grad_middle * gate_a).astype(BF16)
        grad_za = (grad_middle * branch_a * gate_a * (1.0 - gate_a)).astype(BF16)
        grad_za_ref[here, :] = grad_za
        grad_a_ref[here, :] = grad_branch_a
        s_vec[2] += fold_rows(grad_branch_a.astype(F32))
        s_vec[3] += fold_rows(grad_za.astype(F32))
        yield
        grad_attended[here, :] = dot_nt(grad_branch_a, w_out[...]).astype(BF16)
        yield

    interleave([part(slice(at, at + HALF_ROWS)) for at in range(0, MID_ROWS, HALF_ROWS)])

    @pl.when(step == steps - 1)
    def _():
        d_vec[...] = jnp.sum(s_vec[...], 1).astype(BF16)


def middle_part(where, tokens, grad_out, hidden_a, attended, w_outs, pieces):
    total = tokens.shape[0]
    steps = total // MID_ROWS
    rows_at = lambda width: pl.BlockSpec((MID_ROWS, width), lambda i, *refs: (i, 0))
    shape = lambda width, kind=BF16: jax.ShapeDtypeStruct((total, width), kind)
    results, unused = call_kernel(
        functools.partial(middle_body, steps, pieces),
        [where, tokens, grad_out, hidden_a, *attended, *w_outs, *[piece.array for piece in pieces]],
        [],
        [rows_at(D)] * 3
        + [rows_at(GROUP)] * GROUPS
        + [whole(w_outs[0].shape)] * GROUPS
        + [whole(piece.array.shape) for piece in pieces],
        [rows_at(D)] * 5
        + [pl.BlockSpec((2 * CHUNKS, MID_ROWS, D), lambda i, *refs: (0, i, 0))]
        + [rows_at(D)] * 3
        + [whole((VEC_ROWS, D)), whole((D, D))],
        [shape(D), shape(D, F32), shape(D), shape(D), shape(D)]
        + [jax.ShapeDtypeStruct((2 * CHUNKS, total, D), BF16)]
        + [shape(D)] * 3
        + [jax.ShapeDtypeStruct((VEC_ROWS, D), BF16), jax.ShapeDtypeStruct((D, D), BF16)],
        (steps,),
        "middle_part",
        (24e9, 50e6, 4e6),
        scratch=[
            pltpu.VMEM((ALL_ROWS - ROW_OUT, D), BF16),
            pltpu.VMEM((CHUNKS, D, D), BF16),
            pltpu.VMEM((MID_ROWS, FF), F32),
            pltpu.VMEM((VEC_ROWS, 8, D), F32),
        ],
    )
    return results


PLANE_OUT = [jax.ShapeDtypeStruct((HALF, BLOCK, D), BF16)] * 2
PLANE_SPEC = [whole((HALF, BLOCK, D))] * 2


def ffn_body(where, chunk, grad_f, hidden_f, d_vec, keep_three, send_three, keep_two, send_two, carry, rows, wide):
    step = pl.program_id(0)

    @pl.when(step < CHUNKS)
    def _():
        at = pl.multiple_of(ROW_DOWN - ROW_IN + step * D, D)
        rows[pl.ds(at, D), :] = dot_tn(chunk[...], grad_f[...]).astype(BF16)

    @pl.when(step >= CHUNKS)
    def _():
        wide[step - CHUNKS] = dot_tn(hidden_f[...], chunk[...]).astype(BF16)

    @pl.when(step == CHUNKS - 1)
    def _():
        rows[ROW_VEC - ROW_IN :, :] = d_vec[...]
        emit_blocks(rows, ROW_IN, 3, where, keep_three, send_three)

    @pl.when(step == 2 * CHUNKS - 1)
    def _():
        shuffle = spread_matrix(256)

        @pl.loop(0, FF // 256)
        def _(block):
            quarter = pl.ds(pl.multiple_of(block * 64, 64), 64)
            parts = [wide[chunk, quarter, :] for chunk in range(CHUNKS)]
            to = pl.ds(pl.multiple_of(block * 256, 256), 256)
            rows[to, :] = dot_tn(shuffle, jnp.concatenate(parts, 0)).astype(BF16)

        emit_blocks(rows, ROW_IN, 2, where, keep_two, send_two)
        carry[...] = rows[: PLANE_END[1] - ROW_IN, :]


def ffn_gradient(where, chunks, grad_f, hidden_f, d_vec):
    total = chunks.shape[1]
    carry = PLANE_END[1] - ROW_IN
    results, unused = call_kernel(
        ffn_body,
        [where, chunks, grad_f, hidden_f, d_vec],
        [],
        [
            pl.BlockSpec((pl.Squeezed(), total, D), lambda i, *refs: (i, 0, 0)),
            whole((total, D)),
            whole((total, D)),
            whole((VEC_ROWS, D)),
        ],
        PLANE_SPEC * 2 + [whole((carry, D))],
        PLANE_OUT * 2 + [jax.ShapeDtypeStruct((carry, D), BF16)],
        (2 * CHUNKS,),
        "ffn_gradient",
        (8.6e9, 24e6, 0),
        scratch=[
            pltpu.VMEM((ALL_ROWS - ROW_IN, D), BF16),
            pltpu.VMEM((CHUNKS, D, D), BF16),
        ],
    )
    return results


def gates_body(where, *refs):
    att_refs, refs = refs[:GROUPS], refs[GROUPS:]
    hidden_a, hidden_f, grad_a, grad_za, grad_zf, late, keep, send, carry, rows = refs
    att = jnp.concatenate([ref[...] for ref in att_refs], 1)
    rows[:D, :] = dot_tn(att, grad_a[...]).astype(BF16)
    rows[D : 2 * D, :] = dot_tn(hidden_a[...], grad_za[...]).astype(BF16)
    rows[2 * D : 3 * D, :] = dot_tn(hidden_f[...], grad_zf[...]).astype(BF16)
    rows[3 * D :, :] = late[...]
    emit_blocks(rows, ROW_OUT, 1, where, keep, send)
    carry[...] = rows[: PLANE_END[0] - ROW_OUT, :]


def gates_gradient(where, attended, hidden_a, hidden_f, grad_a, grad_za, grad_zf, late, through):
    total = hidden_a.shape[0]
    carry = PLANE_END[0] - ROW_OUT
    return call_kernel(
        gates_body,
        [where, *attended, hidden_a, hidden_f, grad_a, grad_za, grad_zf, late],
        through,
        [whole((total, GROUP))] * GROUPS + [whole((total, D))] * 5 + [whole(late.shape)],
        PLANE_SPEC + [whole((carry, D))],
        PLANE_OUT + [jax.ShapeDtypeStruct((carry, D), BF16)],
        (1,),
        "gates_gradient",
        (3.2e9, 14e6, 0),
        scratch=[pltpu.VMEM((3 * D + late.shape[0], D), BF16)],
    )


LAST_ROWS = 512


def last_body(steps, tok, grad_middle, grad_za, *refs):
    grads, refs = refs[: 3 * GROUPS], refs[3 * GROUPS :]
    w_three, refs = refs[:GROUPS], refs[GROUPS:]
    gate_attn, vec, input_grad, d_vec, factors, s_vec = refs
    step = pl.program_id(0)

    @pl.when(step == 0)
    def _():
        s_vec[...] = jnp.zeros_like(s_vec)
        for group in range(GROUPS):
            factors[:, group * GROUP : (group + 1) * GROUP] = w_three[group][...]

    vecs = vec[...].astype(F32)
    normed, inv_std = layer_stats(tok[...].astype(F32))
    grad_hidden = dot_nt(grad_za[...], gate_attn[...])
    for part, at in enumerate((ROW_QUERY, ROW_KEY, ROW_VALUE)):
        grad = jnp.concatenate([grads[3 * group + part][...] for group in range(GROUPS)], 1)
        grad_hidden += dot_nt(grad, factors[at : at + D, :])
    s_vec[0] += fold_rows(grad_hidden * normed)
    s_vec[1] += fold_rows(grad_hidden)
    input_grad[...] = (grad_middle[...] + norm_back(grad_hidden * vecs[0:1], normed, inv_std)).astype(BF16)

    @pl.when(step == steps - 1)
    def _():
        d_vec[...] = jnp.sum(s_vec[...], 1)


def last_part(tokens, grad_middle, grad_za, grads, w_three, gate_attn, vec, through):
    total = tokens.shape[0]
    steps = total // LAST_ROWS
    rows_at = lambda width: pl.BlockSpec((LAST_ROWS, width), lambda i, *refs: (i, 0))
    return call_kernel(
        functools.partial(last_body, steps),
        [tokens, grad_middle, grad_za, *grads, *w_three, gate_attn, vec],
        through,
        [rows_at(D)] * 3
        + [rows_at(GROUP)] * (3 * GROUPS)
        + [whole((ROW_OUT, GROUP))] * GROUPS
        + [whole((D, D)), whole((VEC_ROWS, D))],
        [rows_at(D), whole((VEC_ROWS, D))],
        [jax.ShapeDtypeStruct((total, D), BF16), jax.ShapeDtypeStruct((VEC_ROWS, D), F32)],
        (steps,),
        "last_part",
        (4.3e9, 20e6, 0),
        scalars=0,
        scratch=[pltpu.VMEM((ROW_OUT, D), BF16), pltpu.VMEM((VEC_ROWS, 8, D), F32)],
    )


def local_part(where, longs, tokens, out_grad, first_pieces, middle_pieces, before, later, collect):
    subs, length, unused = tokens.shape
    rows = tokens.reshape(subs * length, D)
    grads_in = out_grad.reshape(subs * length, D)
    (*kept, hidden_a, vec), passed = forward_group(0, longs, where, rows, first_pieces, before("forward0"))
    later("forward0", passed)
    second, passed = forward_group(1, longs, where, hidden_a, first_pieces, before("forward1"))
    later("forward1", passed)
    groups = [kept, second]
    attended = [group[3] for group in groups]
    (outputs, grad_middle, grad_za, grad_attended, hidden_f, chunks, grad_f, grad_zf, grad_a, d_vec, gate_attn) = (
        middle_part(where, rows, grads_in, hidden_a, attended, [group[6] for group in groups], middle_pieces())
    )
    keep, send, *plane, carry = ffn_gradient(where, chunks, grad_f, hidden_f, d_vec)
    collect(3, keep, send)
    collect(2, *plane)
    (*plane, carry), passed = gates_gradient(
        where, attended, hidden_a, hidden_f, grad_a, grad_za, grad_zf, carry, before("gates")
    )
    later("gates", passed)
    collect(1, *plane)
    grads = []
    for group, (query, key, value, att, extra, *unused_two) in enumerate(groups):
        (*three, keep, send), passed = backward_group(
            group, where, query, key, value, extra, att, grad_attended, hidden_a, carry, before(f"back{group}")
        )
        later(f"back{group}", passed)
        grads += three
        collect(("first", group), keep, send)
    w_three = [group[5] for group in groups]
    (input_grad, d_vec), passed = last_part(
        rows, grad_middle, grad_za, grads, w_three, gate_attn, vec, before("last")
    )
    later("last", passed)
    return outputs.reshape(tokens.shape), input_grad.reshape(tokens.shape), d_vec


def own_block(params, start, rows):
    share = params.shape[0]
    room = jnp.pad(params, (TILE, rows * D - share))
    return lax.dynamic_slice(room, (TILE - start % TILE,), (rows * D,)).reshape(rows, D).astype(BF16)


def move(axis, count, step):
    perm = [(i, step(i)) for i in range(count) if step(i) is not None]
    return lambda value: lax.ppermute(value, axis, perm)


def on_slice(tokens, out_grad, long_count, params):
    z, x, y, c = (lax.axis_index(axis) for axis in ("z", "x", "y", "c"))
    me = ((z * 2 + x) * 2 + y) * 2 + c
    share = params.shape[0]
    block = own_block(params, me * share, BLOCK)
    odd = z % 2 == 1
    ends = (z == 0) | (z == 3)
    swap_c = move("c", 2, lambda i: 1 - i)
    swap_x = move("x", 2, lambda i: 1 - i)
    swap_y = move("y", 2, lambda i: 1 - i)
    swap_xy = move(("x", "y"), 4, lambda i: 3 - i)
    z_one = move("z", 4, lambda i: i ^ 1)
    z_two = move("z", 4, lambda i: i ^ 2)
    z_ends = move("z", 4, lambda i: {0: 2, 3: 1}.get(i))
    z_mid = move("z", 4, lambda i: {1: 2, 2: 1}.get(i))
    z_out = move("z", 4, lambda i: {1: 0, 2: 3}.get(i))

    inside = z < 4
    vec = block[VEC_AT : VEC_AT + VEC_ROWS]
    mine = jnp.concatenate([block, jnp.where(me == SHARES - 1, vec, jnp.zeros_like(vec))], 0)
    held = jnp.where(ends, mine, z_ends(mine))
    out_first, got_mid = z_out(block), z_mid(block)
    got = z_one(jnp.concatenate([held, jnp.where(inside, got_mid, out_first)], 0))
    other, out_second = got[: BLOCK + VEC_ROWS], got[BLOCK + VEC_ROWS :]
    vec = jnp.where(odd, held, other)[BLOCK:]
    first = jnp.concatenate([jnp.where(z == 2, held, other)[:BLOCK], vec], 0)[None]
    one = jnp.where(z == 0, out_first, jnp.where(z == 1, held[:BLOCK], jnp.where(z == 2, got_mid, out_second)))
    two = jnp.where(z == 0, out_second, jnp.where(z == 1, got_mid, jnp.where(z == 2, other[:BLOCK], out_first)))
    both = jnp.stack([one, two])

    def in_plane(parts, planes):
        near = jnp.concatenate(parts, 0)
        blocks = [(plane, spot) for spot in range(HALF) for plane in planes]
        return [Piece(near, blocks, False, 0), Piece(swap_c(near), blocks, True, 0)]

    own = block[None]
    pieces = in_plane([own, swap_y(own), swap_x(own), swap_xy(own)], ((0,),))
    pieces += in_plane([first, swap_y(first), swap_x(first), swap_xy(first)], ((4,),))
    around = {"both": [swap_y(both), swap_x(both), swap_xy(both)]}
    top = {"both": both[:, :TILE_ROWS]}

    def middle_pieces():
        mine = jnp.concatenate([top["both"], both[:, TILE_ROWS:]], 1)
        return pieces + in_plane([mine] + around["both"], ((5,), (6,)))

    early, late = ("first", 0), ("first", 1)
    arrived, at_chip, held = {}, {}, {}
    z_up = move("z", 4, lambda i: {0: 2, 1: 3}.get(i))
    z_down = move("z", 4, lambda i: {2: 0, 3: 1}.get(i))

    def collect(plane, keep, send):
        arrived[plane] = [keep, swap_c(send)]

    def send_around(name, planes, first=None):
        part = []
        for spot in range(HALF):
            sides = [[arrived[plane][side][spot].astype(F32) for plane in planes] for side in range(2)]
            keep, got = (jnp.concatenate(side, 1) for side in sides)
            if first is not None:
                keep = jnp.where(inside, keep, first[:, : keep.shape[1]])
            part.append((keep + got).astype(BF16))
        at_chip[name] = part[0]
        around[name] = (swap_y(part[1]), swap_x(part[2]), swap_xy(part[3]))

    def plane_sum(name):
        total = at_chip[name].astype(F32)
        for got in around[name]:
            total = total + got.astype(F32)
        return total

    def before(name):
        if name == "forward0":
            return []
        if name == "forward1":
            return [top["both"]]
        if name == "gates":
            return [arrived[2][0], arrived[3][0]]
        if name == "back0":
            send_around("upper", (2, 3))
            return [at_chip["upper"]]
        if name == "back1":
            held["upper"] = plane_sum("upper")
            held["up"] = z_up(held["upper"].astype(BF16))
            send_around("lower", (1, early), held["upper"])
            return [held["upper"], at_chip["lower"]]
        if name == "last":
            held["lower"] = plane_sum("lower")
            held["down"] = z_down(held["lower"].astype(BF16))
            send_around("late", (late,), held["lower"])
            upper = jnp.where(inside, held["upper"][:, : D + GROUP], held["lower"])
            upper = jnp.concatenate([upper, held["upper"][:, D + GROUP :]], 1) + held["up"].astype(F32)
            two, three = upper[:, :D], upper[:, D:]
            held["give"] = jnp.where(z == 2, three, two).astype(BF16)
            held["mine"] = jnp.where(z == 2, two, three)
            return [held["give"], held["mine"], held["lower"], at_chip["late"]]
        return []

    def later(name, passed):
        if name == "forward1":
            top["both"] = passed[0]
        if name == "gates":
            arrived[2][0], arrived[3][0] = passed
        if name == "back0":
            at_chip["upper"] = passed[0]
        if name == "back1":
            held["upper"], at_chip["lower"] = passed
        if name == "last":
            held["give"], held["mine"], held["lower"], at_chip["late"] = passed

    planes = [jnp.where(z == 0, 3, 0), jnp.where(z == 1, 3, 1), jnp.where(z == 2, 3, 2)]
    where = jnp.stack([z, x, y, c, *planes]).astype(jnp.int32)
    outputs, input_grad, d_vec = local_part(
        where,
        long_count.reshape(-1),
        tokens,
        out_grad,
        pieces,
        middle_pieces,
        before,
        later,
        collect,
    )
    low = plane_sum("late")
    lower = jnp.where(inside, held["lower"], jnp.concatenate([low] * 3, 1)) + held["down"].astype(F32)
    one, zero = lower[:, :D], jnp.concatenate([lower[:, D:]] * 2, 1)
    give = jnp.where(z == 0, one.astype(BF16), jnp.where(z == 1, zero.astype(BF16), held["give"]))
    given = z_one(give).astype(F32)
    total = jnp.where(z == 0, zero, jnp.where(z == 1, one, held["mine"])) + given
    gains = jnp.where(inside, d_vec[:2], jnp.concatenate([low[:2]] * 2, 1))
    gains = gains + swap_c(gains)
    gains = (gains + swap_x(gains) + swap_y(gains) + swap_xy(gains)).reshape(2 * GROUPS, GROUP)
    lines = jnp.pad(gains.astype(BF16), ((0, TILE_ROWS - 2 * GROUPS), (0, 0)))
    message = jnp.concatenate([low.astype(BF16), lines], 0)
    for step in ({3: 0, 0: 3}, {2: 0, 1: 3}, {1: 0, 2: 3}):
        got = move("z", 4, step.get)(message).astype(F32)
        low = low + got[:BLOCK]
        gains = gains + got[BLOCK : BLOCK + 2 * GROUPS]
    total = jnp.where(z == 0, jnp.concatenate([total[:, :GROUP], low], 1), total)
    gains = jnp.where(me == SHARES - 1, gains.reshape(2, D), jnp.zeros((2, D), F32))
    total = total + jnp.pad(gains, ((VEC_AT, BLOCK - VEC_AT - 2), (0, 0)))
    param_grad = lax.dynamic_slice(total.reshape(-1), ((me * share) % TILE,), (share,))
    return (outputs, input_grad, param_grad)


def on_any(axes, count, tokens, out_grad, long_count, params):
    share = params.shape[0]
    me = lax.axis_index(axes)
    starts = [index * share // TILE * TILE_ROWS for index in range(count)]
    rows = max(-(-((index + 1) * share) // TILE) * TILE_ROWS - starts[index] for index in range(count))
    gathered = lax.all_gather(own_block(params, me * share, rows), axes, axis=0)
    merged = jnp.zeros((starts[-1] + rows, D), BF16)
    for index in range(count):
        merged = merged.at[starts[index] : starts[index] + rows].add(gathered[index])
    merged = merged[:ALL_ROWS]
    near, far = [], []
    for plane in range(PLANES):
        blocks = []
        for index in range(plane * IN_PLANE, (plane + 1) * IN_PLANE):
            end = STARTS[index + 1] if index + 1 < SHARES else ALL_ROWS
            piece = merged[STARTS[index] : end]
            blocks.append(jnp.pad(piece, ((0, BLOCK - piece.shape[0]), (0, 0))))
        spots = [(plane, spot) for spot in range(HALF)]
        near.append(Piece(jnp.stack(blocks[0::2]), spots, False, 0))
        far.append(Piece(jnp.stack(blocks[1::2]), spots, True, 0))
    vec = merged[ROW_VEC : ROW_VEC + VEC_ROWS]
    first_pieces = []
    for piece in (near[0], far[0]):
        lines = jnp.zeros((HALF, VEC_ROWS, D), BF16)
        if piece is near[0]:
            lines = lines.at[0].set(vec)
        first_pieces.append(Piece(jnp.concatenate([piece.array, lines], 1), piece.blocks, piece.other, 0))
    by_share = [None] * SHARES

    halves = []

    def collect(plane, keep, send):
        if isinstance(plane, tuple):
            halves.append((keep, send))
            if len(halves) < GROUPS:
                return
            keep, send = (jnp.concatenate([half[side] for half in halves], 2) for side in range(2))
            plane = 0
        for spot in range(HALF):
            by_share[plane * IN_PLANE + 2 * spot] = keep[spot]
            by_share[plane * IN_PLANE + 2 * spot + 1] = send[spot]

    outputs, input_grad, d_vec = local_part(
        jnp.zeros((7,), jnp.int32),
        long_count.reshape(-1),
        tokens,
        out_grad,
        first_pieces,
        lambda: near[1:] + far[1:],
        lambda name: [],
        lambda name, passed: None,
        collect,
    )
    ends = STARTS[1:] + [ALL_ROWS]
    gradient = jnp.concatenate([part[: ends[i] - STARTS[i]] for i, part in enumerate(by_share)], 0)
    gradient = gradient.at[ROW_VEC : ROW_VEC + VEC_ROWS].add(d_vec.astype(BF16))
    gradient = jnp.pad(gradient, ((0, max(0, starts[-1] + rows - ALL_ROWS)), (0, 0)))
    spread = jnp.stack([gradient[start : start + rows] for start in starts])
    summed = lax.psum_scatter(spread, axes, scatter_dimension=0)
    param_grad = lax.dynamic_slice(summed.astype(F32).reshape(-1), ((me * share) % TILE,), (share,))
    return (outputs, input_grad, param_grad)


def solution(mesh):
    axes = ("wide", "narrow")
    count = math.prod(mesh.shape[axis] for axis in axes)
    step = functools.partial(on_any, axes, count)
    if mesh.shape["wide"] == 8 and mesh.shape["narrow"] == 4:
        axes = ("z", "x", "y", "c")
        mesh = Mesh(mesh.devices.reshape(4, 2, 2, 2), axes)
        step = on_slice
    return jax.shard_map(
        step,
        mesh=mesh,
        in_specs=(P(None, axes, None), P(None, axes, None), P(None, axes), P(axes)),
        out_specs=(P(None, axes, None), P(None, axes, None), P(axes)),
        check_vma=False,
    )
```

```python
import functools
import math

import jax
import jax.numpy as jnp
from jax import lax
from jax.experimental import pallas as pl
from jax.experimental.pallas import tpu as pltpu
from jax.sharding import Mesh, PartitionSpec as P

D = 512
FF = 2048
HEADS = 8
HD = 64
SHORT = 512
LONG = 1024
PAIR = 2 * HD
GROUP = 2 * PAIR
GROUPS = D // GROUP
STRIP = 256

TILE_ROWS = 16
TILE = TILE_ROWS * D

layer_eps = 1e-05
far_below = -1e30

F32 = jnp.float32
BF16 = jnp.bfloat16
MB = 1024 * 1024


def dot_nn(left, right):
    return lax.dot_general(left, right, (((1,), (0,)), ((), ())), preferred_element_type=F32)


def dot_nt(left, right):
    return lax.dot_general(left, right, (((1,), (1,)), ((), ())), preferred_element_type=F32)


def dot_tn(left, right):
    return lax.dot_general(left, right, (((0,), (0,)), ((), ())), preferred_element_type=F32)


def layer_stats(values):
    average = jnp.mean(values, -1, keepdims=True)
    centred = values - average
    variance = jnp.mean(centred * centred, -1, keepdims=True)
    inv_std = lax.rsqrt(variance + layer_eps)
    return (centred * inv_std, inv_std)


def norm_back(grad_hat, normed, inv_std):
    return inv_std * (
        grad_hat
        - jnp.mean(grad_hat, -1, keepdims=True)
        - normed * jnp.mean(grad_hat * normed, -1, keepdims=True)
    )


def sigmoid(values):
    return 0.5 * jnp.tanh(0.5 * values) + 0.5


def fold_rows(values):
    return jnp.sum(values.reshape(values.shape[0] // 8, 8, values.shape[1]), 0)


ROW_QUERY = 0
ROW_KEY = 512
ROW_VALUE = 1024
ROW_OUT = 1536
ROW_GATE_A = 2048
ROW_GATE_F = 2560
ROW_IN = 3072
ROW_DOWN = 5120
ROW_VEC = 7168
ALL_ROWS = 7184
VEC_ROWS = 16
ENTRIES = 6 * D * D + 2 * D * FF + 8 * D + FF

SHARES = 32
PLANES = 4
IN_PLANE = SHARES // PLANES
HALF = IN_PLANE // 2
STARTS = [index * (ENTRIES // SHARES) // TILE * TILE_ROWS for index in range(SHARES)]
BLOCK = max(
    -(-((index + 1) * (ENTRIES // SHARES)) // TILE) * TILE_ROWS - STARTS[index] for index in range(SHARES)
)
PLANE_END = [STARTS[(plane + 1) * IN_PLANE - 1] + BLOCK for plane in range(PLANES)]
VEC_AT = ROW_VEC - STARTS[-1]

VMEM = pltpu.CompilerParams(vmem_limit_bytes=62 * MB)


def whole(shape, single=True):
    rank = len(shape)
    kwargs = {"pipeline_mode": pl.Buffered(1)} if single else {}
    return pl.BlockSpec(shape, lambda *unused: (0,) * rank, **kwargs)


def share_row(where, plane, spot, other):
    core = 1 - where[3] if other else where[3]
    share = 2 * ((where[1] * 2 + where[2]) ^ spot) + core
    return ((plane * IN_PLANE + share) * (ENTRIES // SHARES)) // TILE * TILE_ROWS


class Piece:
    def __init__(self, array, blocks, other):
        self.array, self.blocks, self.other = array, blocks, other


def place_piece(target, base, where, piece, block_of, lowest):
    def place(index, plane, spot):
        at = share_row(where, plane, spot, piece.other) - base
        rows = pl.ds(pl.multiple_of(at, TILE_ROWS), BLOCK)
        target[rows, :] = target[rows, :] + block_of(index)

    for index, (plane, spot) in enumerate(piece.blocks):
        if not isinstance(plane, tuple):
            if (plane == 0) == lowest:
                place(index, plane, spot)
            continue
        plane = where[plane[0]]
        pl.when((plane == 0) == lowest)(functools.partial(place, index, plane, spot))


UNREAD = pl.BlockSpec(memory_space=pl.ANY)


def call_kernel(body, arguments, through, in_specs, out_specs, out_shape, grid, name, cost, scalars=1, scratch=(), alias=None):
    inputs, outputs, passed = len(arguments), len(out_specs), len(through)
    aliases = {inputs + index: outputs + index for index in range(passed)}
    aliases.update(alias or {})

    def run(*refs):
        at = inputs + passed
        body(*refs[:inputs], *refs[at : at + outputs], *refs[at + outputs + passed :])

    results = pl.pallas_call(
        run,
        name=name,
        grid_spec=pltpu.PrefetchScalarGridSpec(
            num_scalar_prefetch=scalars,
            grid=grid,
            in_specs=list(in_specs) + [UNREAD] * passed,
            out_specs=list(out_specs) + [UNREAD] * passed,
            scratch_shapes=list(scratch),
        ),
        out_shape=list(out_shape) + [jax.ShapeDtypeStruct(array.shape, array.dtype) for array in through],
        input_output_aliases=aliases,
        compiler_params=VMEM,
        cost_estimate=pl.CostEstimate(flops=int(cost[0]), bytes_accessed=int(cost[1]), transcendentals=int(cost[2])),
    )(*arguments, *through)
    return results[:outputs], results[outputs:]


def emit_copies(source, base, plane, where, keep, send, sems):
    copies = []
    for spot in range(HALF):
        for out, other in ((keep, False), (send, True)):
            at = pl.multiple_of(share_row(where, plane, spot, other) - base, TILE_ROWS)
            copy = pltpu.make_async_copy(source.at[pl.ds(at, BLOCK), :], out.at[spot], sems.at[len(copies)])
            copies.append(copy)
    return copies


def start_all(copies):
    for copy in copies:
        copy.start()


def wait_all(copies):
    for copy in copies:
        copy.wait()


COPY_SEMS = pltpu.SemaphoreType.DMA((IN_PLANE,))


def split_three(values):
    high = values.astype(BF16)
    rest = values - high.astype(F32)
    middle = rest.astype(BF16)
    low = (rest - middle.astype(F32)).astype(BF16)
    return high, middle, low


def pick_lanes(base, lane, first, columns):
    out = base
    for offset, column in enumerate(columns):
        out = jnp.where(lane == first + offset, column, out)
    return out


def pipeline(units, *stages):
    held, results = {}, {}
    count = len(units)
    for turn in range(count + len(stages) - 1):
        for at in range(len(stages)):
            stage = (0, *range(len(stages) - 1, 0, -1))[at]
            unit = turn - stage
            if 0 <= unit < count:
                value = stages[stage](units[unit], *(held.pop(unit) if stage else ()))
                if stage + 1 < len(stages):
                    held[unit] = value
                else:
                    results[units[unit]] = value
    return results


def attend_columns(is_long, query, key, value, attended, extra):
    strips = LONG // STRIP
    key_ids = lax.broadcasted_iota(jnp.int32, (STRIP, STRIP), 0)
    query_ids = lax.broadcasted_iota(jnp.int32, (STRIP, STRIP), 1)
    causal = query_ids >= key_ids
    cut = jnp.where(is_long, 0.0, far_below)
    late = jnp.where(is_long, 0.0, 1.0)
    lane = lax.broadcasted_iota(jnp.int32, (LONG, PAIR), 1)
    ones = jnp.ones((TILE_ROWS, LONG), BF16)
    q_heads, k_pairs, v_heads = [], [], []
    for pair in range(query.shape[1] // PAIR):
        cols = slice(pair * PAIR, (pair + 1) * PAIR)
        rows = query[:, cols]
        zero = jnp.zeros_like(rows)
        q_heads += [jnp.where(lane < HD, rows, zero), jnp.where(lane >= HD, rows, zero)]
        k_pairs.append(key[:, cols])
        turned = value[:, cols].astype(F32).T.astype(BF16)
        v_heads += [jnp.concatenate([turned[:HD], ones], 0), jnp.concatenate([turned[HD:], ones], 0)]

    def scores_of(unit):
        strip, head = unit
        lo, reach = strip * STRIP, (strip + 1) * STRIP
        return (dot_nt(k_pairs[head // 2][:reach], q_heads[head][lo:reach]),)

    def soften(unit, scores):
        strip, unused = unit
        lo = strip * STRIP
        parts = []
        if lo >= SHORT:
            parts.append(scores[:SHORT] + cut)
            if lo > SHORT:
                parts.append(scores[SHORT:lo])
        elif strip:
            parts.append(scores[:lo])
        parts.append(jnp.where(causal, scores[lo:], far_below))
        scores = jnp.concatenate(parts, 0)
        largest = jnp.max(scores, 0, keepdims=True)
        return jnp.exp(scores - largest).astype(BF16), largest

    def finish(unit, shifted, largest):
        strip, head = unit
        out = dot_nn(v_heads[head][:, : (strip + 1) * STRIP], shifted)
        sum_exp = out[HD : HD + 1]
        return out[:HD] * (1.0 / sum_exp), largest + jnp.log(sum_exp)

    units = [(strip, head) for strip in range(strips) for head in range(len(q_heads))]
    results = pipeline(units, scores_of, soften, finish)
    for strip in range(strips):
        rows = slice(strip * STRIP, (strip + 1) * STRIP)
        for pair in range(len(k_pairs)):
            cols = slice(pair * PAIR, (pair + 1) * PAIR)
            two = [results[(strip, 2 * pair + side)] for side in range(2)]
            attended[rows, cols] = jnp.concatenate([out for out, unused in two], 0).T.astype(BF16)
            lines = [part.astype(F32) for unused, logsum in two for part in split_three(-logsum)]
            lines.append(jnp.broadcast_to(late if strip * STRIP >= SHORT else 0.0, (1, STRIP)))
            lines.append(jnp.zeros((PAIR - 7, STRIP), F32))
            extra[rows, cols] = jnp.concatenate(lines, 0).T.astype(BF16)


def block_columns(source, index):
    return source[index, :BLOCK, :GROUP]


def forward_body(first, pieces, longs, where, rows_in, *rest):
    sources, rest = rest[: len(pieces)], rest[len(pieces) :]
    if first:
        query, key, value, attended, extra, w_three, w_out, hidden, vec, weights = rest
    else:
        query, key, value, attended, extra, w_three, w_out, weights = rest
    sub = pl.program_id(0)

    @pl.when(sub == 0)
    def _():
        weights[...] = jnp.zeros_like(weights)
        for piece, source in zip(pieces, sources):
            place_piece(weights, 0, where, piece, functools.partial(block_columns, source), True)
        w_three[...] = weights[:ROW_OUT, :]
        w_out[...] = weights[ROW_OUT:, :]
        if first:
            total = jnp.zeros((VEC_ROWS, D), BF16)
            for source in sources:
                if source.shape[1] > BLOCK:
                    for index in range(source.shape[0]):
                        total = total + source[index, BLOCK:, :]
            vec[...] = total

    if first:
        normed, unused = layer_stats(rows_in[...].astype(F32))
        lines = vec[...].astype(F32)
        hid = (normed * lines[0:1] + lines[1:2]).astype(BF16)
        hidden[...] = hid
    else:
        hid = rows_in[...]
    q_rows = (dot_nn(hid, weights[ROW_QUERY : ROW_QUERY + D, :]) * (1.0 / math.sqrt(HD))).astype(BF16)
    k_rows = dot_nn(hid, weights[ROW_KEY : ROW_KEY + D, :]).astype(BF16)
    v_rows = dot_nn(hid, weights[ROW_VALUE : ROW_VALUE + D, :]).astype(BF16)
    query[...] = q_rows
    key[...] = k_rows
    value[...] = v_rows
    attend_columns(longs[sub] > 0, q_rows, k_rows, v_rows, attended, extra)


def forward_group(group, longs, where, rows_in, pieces, through):
    first = group == 0
    total = rows_in.shape[0]
    rows = pl.BlockSpec((LONG, D), lambda s, *refs: (s, 0))
    part = pl.BlockSpec((LONG, GROUP), lambda s, *refs: (s, 0))
    width = D if first else GROUP
    blocks = [
        pl.BlockSpec(piece.array.shape[:2] + (width,), lambda s, *refs: (0, 0, group), pipeline_mode=pl.Buffered(1))
        for piece in pieces
    ]
    tail = PLANE_END[0] - ROW_OUT
    out_specs = [part] * 5 + [whole((ROW_OUT, GROUP)), whole((tail, GROUP))]
    out_shape = [jax.ShapeDtypeStruct((total, GROUP), BF16)] * 5 + [
        jax.ShapeDtypeStruct((ROW_OUT, GROUP), BF16),
        jax.ShapeDtypeStruct((tail, GROUP), BF16),
    ]
    if first:
        out_specs += [rows, whole((VEC_ROWS, D))]
        out_shape += [jax.ShapeDtypeStruct((total, D), BF16), jax.ShapeDtypeStruct((VEC_ROWS, D), BF16)]
    return call_kernel(
        functools.partial(forward_body, first, pieces),
        [longs, where, rows_in, *[piece.array for piece in pieces]],
        through,
        [rows] + blocks,
        out_specs,
        out_shape,
        (total // LONG,),
        "forward_group",
        (8e9, 12e6, 4e6) if first else (0, 0, 0),
        scalars=2,
        scratch=[pltpu.VMEM((PLANE_END[0], GROUP), BF16)],
    )


def attend_back_rows(query, key, value, extra, attended, grad, grad_query, grad_key, grad_value):
    strips = LONG // STRIP
    lane = lax.broadcasted_iota(jnp.int32, (LONG, PAIR), 1)
    row = lax.broadcasted_iota(jnp.int32, (LONG, PAIR), 0)
    row_ids = lax.broadcasted_iota(jnp.int32, (STRIP, STRIP), 0)
    col_ids = lax.broadcasted_iota(jnp.int32, (STRIP, STRIP), 1)
    causal = col_ids >= row_ids
    early = jnp.where((lane == 6) & (row < SHORT), far_below, 0.0)
    v_tail = jnp.where(lane < 3, 1.0, 0.0).astype(BF16)
    heads, pairs = [], query.shape[1] // PAIR
    for pair in range(pairs):
        cols = slice(pair * PAIR, (pair + 1) * PAIR)
        q_all, k_all, v_all, g_all, x_all = (ref[:, cols] for ref in (query, key, value, grad, extra))
        product = g_all.astype(F32) * attended[:, cols].astype(F32)
        zero = jnp.zeros_like(q_all)
        v_wide = jnp.concatenate([v_all, v_tail], 1)
        turned = k_all.astype(F32).T.astype(BF16)
        for side in range(2):
            mine = (lane < HD) if side == 0 else (lane >= HD)
            delta = jnp.sum(jnp.where(mine, product, 0.0), -1, keepdims=True)
            d_tail = pick_lanes(
                jnp.zeros((LONG, PAIR), F32), lane, 0, [part.astype(F32) for part in split_three(-delta)]
            )
            q_head = jnp.where(mine, q_all, zero)
            g_head = jnp.where(mine, g_all, zero)
            ones = jnp.where((lane >= 3 * side) & (lane < 3 * side + 3), 1.0, early).astype(BF16)
            heads.append(
                (
                    q_head,
                    g_head,
                    turned[side * HD : (side + 1) * HD],
                    jnp.concatenate([q_head, x_all], 1),
                    jnp.concatenate([g_head, d_tail.astype(BF16)], 1),
                    jnp.concatenate([k_all, ones], 1),
                    v_wide,
                )
            )

    def products(unit):
        block, head = unit
        lo, hi = block * STRIP, (block + 1) * STRIP
        unused, unused, unused, q_wide, g_wide, k_wide, v_wide = heads[head]
        return dot_nt(k_wide[lo:hi], q_wide[lo:]), dot_nt(v_wide[lo:hi], g_wide[lo:])

    def soften(unit, scores, slope):
        soft = jnp.exp(scores)
        first = jnp.where(causal, soft[:, :STRIP], 0.0)
        soft = first if soft.shape[1] == STRIP else jnp.concatenate([first, soft[:, STRIP:]], 1)
        return soft.astype(BF16), (soft * slope).astype(BF16)

    query_sum = {}

    def gradients(unit, soft, scores):
        block, head = unit
        lo, hi = block * STRIP, (block + 1) * STRIP
        q_head, g_head, k_turned, *unused = heads[head]
        part = dot_nn(k_turned[:, lo:hi], scores)
        for later in range(block, strips):
            piece = part[:, (later - block) * STRIP : (later - block + 1) * STRIP]
            at = (later, head)
            query_sum[at] = query_sum[at] + piece if at in query_sum else piece
        return dot_nn(soft, g_head[lo:]), dot_nn(scores, q_head[lo:])

    units = [(block, head) for block in range(strips) for head in range(len(heads))]
    results = pipeline(units, products, soften, gradients)
    for block in range(strips):
        rows = slice(block * STRIP, (block + 1) * STRIP)
        for pair in range(pairs):
            cols = slice(pair * PAIR, (pair + 1) * PAIR)
            (value_a, key_a), (value_b, key_b) = results[(block, 2 * pair)], results[(block, 2 * pair + 1)]
            grad_value[rows, cols] = (value_a + value_b).astype(BF16)
            grad_key[rows, cols] = (key_a + key_b).astype(BF16)
            two = jnp.concatenate([query_sum[(block, 2 * pair + side)] for side in range(2)], 0)
            grad_query[rows, cols] = (two * (1.0 / math.sqrt(HD))).T.astype(BF16)


def backward_body(steps, where, query, key, value, extra, attended, grad, hidden, late, *refs):
    grad_query, grad_key, grad_value, keep, send, total, rows, sems = refs
    step = pl.program_id(0)
    attend_back_rows(query, key, value, extra, attended, grad, grad_query, grad_key, grad_value)
    three = jnp.concatenate([grad_query[...], grad_key[...], grad_value[...]], 1)
    now = dot_tn(hidden[...], three)

    @pl.when(step == 0)
    def _():
        total[...] = now

    @pl.when(step > 0)
    def _():
        total[...] = total[...] + now

    @pl.when(step == steps - 1)
    def _():
        for part, at in enumerate((ROW_QUERY, ROW_KEY, ROW_VALUE)):
            rows[at : at + D, :] = total[:, part * GROUP : (part + 1) * GROUP].astype(BF16)
        rows[ROW_OUT:, :] = late[...]
        copies = emit_copies(rows, 0, 0, where, keep, send, sems)
        start_all(copies)
        wait_all(copies)


def backward_group(group, where, query, key, value, extra, attended, grad, hidden, late, through):
    total = query.shape[0]
    steps = total // LONG
    part = pl.BlockSpec((LONG, GROUP), lambda s, *refs: (s, 0))
    block = (HALF, BLOCK, GROUP)
    return call_kernel(
        functools.partial(backward_body, steps),
        [where, query, key, value, extra, attended, grad, hidden, late],
        through,
        [part] * 5
        + [
            pl.BlockSpec((LONG, GROUP), lambda s, *refs: (s, group)),
            pl.BlockSpec((LONG, D), lambda s, *refs: (s, 0)),
            pl.BlockSpec((late.shape[0], GROUP), lambda s, *refs: (0, group), pipeline_mode=pl.Buffered(1)),
        ],
        [part] * 3 + [UNREAD] * 2,
        [jax.ShapeDtypeStruct((total, GROUP), BF16)] * 3 + [jax.ShapeDtypeStruct(block, BF16)] * 2,
        (steps,),
        "backward_group",
        (14e9, 16e6, 4e6),
        scratch=[
            pltpu.VMEM((D, 3 * GROUP), F32),
            pltpu.VMEM((ROW_OUT + late.shape[0], GROUP), BF16),
            COPY_SEMS,
        ],
    )


MID_ROWS = 512
HALF_ROWS = 256
STAGE_ROWS = 256
STAGE = 8
CHUNKS = FF // D
TANH_SCALE = math.sqrt(2.0 / math.pi)


def spread_matrix(size):
    quarter = size // CHUNKS
    to = lax.broadcasted_iota(jnp.int32, (size, size), 0)
    source = lax.broadcasted_iota(jnp.int32, (size, size), 1)
    return (source == CHUNKS * (to % quarter) + to // quarter).astype(BF16)


def interleave(parts):
    started, live = 0, []
    while started < len(parts) or live:
        if started < len(parts):
            live.append(parts[started])
            started += 1
        live = [part for part in live if next(part, True) is None]


def middle_body(steps, pieces, where, tok, grad_out, hidden_a, *refs):
    att_refs, wo_refs, refs = refs[:GROUPS], refs[GROUPS : 2 * GROUPS], refs[2 * GROUPS :]
    sources, refs = refs[: len(pieces)], refs[len(pieces) :]
    (outputs, grad_middle_ref, grad_za_ref, grad_attended, hid_f_ref, grad_zf_ref, grad_a_ref, gate_copy) = refs[:8]
    (keep_three, send_three, keep_two, send_two, carry, weights, wide, slope, s_vec, kept, s_hid_f, s_grad_f) = refs[8:-3]
    load_sems, sems_three, sems_two = refs[-3:]
    step = pl.program_id(0)
    base = ROW_OUT

    @pl.when(step == 0)
    def _():
        staged = []
        for piece, source in zip(pieces, sources):
            for index in range(len(piece.blocks)):
                slot = len(staged)
                to = kept.at[slot // STAGE, pl.ds(slot % STAGE * STAGE_ROWS, BLOCK), :]
                staged.append((to, pltpu.make_async_copy(source.at[index, pl.ds(0, BLOCK), :], to, load_sems.at[slot])))
                staged[-1][1].start()
        weights[...] = jnp.zeros_like(weights)
        for group in range(GROUPS):
            weights[: PLANE_END[0] - ROW_OUT, group * GROUP : (group + 1) * GROUP] = wo_refs[group][...]
        at_slot = 0
        for piece in pieces:
            count = len(piece.blocks)
            here = staged[at_slot : at_slot + count]
            wait_all([copy for unused, copy in here])
            place_piece(weights, base, where, piece, lambda index, here=here: here[index][0][...], False)
            at_slot += count
        shuffle = spread_matrix(256)
        for block in range(FF // 256):
            at = ROW_IN - base + block * 256
            part = dot_nn(shuffle, weights[at : at + 256, :]).astype(BF16)
            for chunk in range(CHUNKS):
                wide[chunk, block * 64 : (block + 1) * 64, :] = part[chunk * 64 : (chunk + 1) * 64]
        gate_copy[...] = weights[ROW_GATE_A - base : ROW_GATE_A - base + D, :]
        s_vec[...] = jnp.zeros_like(s_vec)

    w_out = weights.at[ROW_OUT - base : ROW_OUT - base + D]
    gate_attn = weights.at[ROW_GATE_A - base : ROW_GATE_A - base + D]
    gate_ffn = weights.at[ROW_GATE_F - base : ROW_GATE_F - base + D]
    w_down = weights.at[ROW_DOWN - base : ROW_DOWN - base + FF]
    vecs = weights[ROW_VEC - base : ROW_VEC - base + VEC_ROWS, :].astype(F32)
    chunks = [slice(chunk * D, (chunk + 1) * D) for chunk in range(CHUNKS)]

    first_row = pl.multiple_of(step * MID_ROWS, MID_ROWS)

    def part(at):
        here = slice(at, at + HALF_ROWS)
        there = pl.ds(first_row + at, HALF_ROWS)
        hid_a = hidden_a[here, :]
        att = jnp.concatenate([ref[here, :] for ref in att_refs], 1)
        grad = grad_out[here, :].astype(F32)
        branch_a = dot_nn(att, w_out[...])
        gate_a = dot_nn(hid_a, gate_attn[...])
        yield
        branch_a = branch_a + vecs[2:3]
        gate_a = sigmoid(gate_a + vecs[3:4])
        middle = tok[here, :].astype(F32) + gate_a * branch_a
        normed, inv_std = layer_stats(middle)
        hid_f = (normed * vecs[4:5] + vecs[5:6]).astype(BF16)
        hid_f_ref[here, :] = hid_f
        s_hid_f[there, :] = hid_f
        yield
        gate_f = dot_nn(hid_f, gate_ffn[...])
        pre = dot_nn(hid_f, wide[0])
        yield
        branch_f = vecs[6:7]
        for chunk, cols in enumerate(chunks):
            pre = pre + vecs[8 + chunk : 9 + chunk]
            square = pre * pre
            bend = jnp.tanh(pre * (TANH_SCALE + (TANH_SCALE * 0.044715) * square))
            half = 0.5 * (1.0 + bend)
            active = (pre * half).astype(BF16)
            slope[here, cols] = half + (0.5 * pre) * (1.0 - bend * bend) * (
                TANH_SCALE + (3.0 * 0.044715 * TANH_SCALE) * square
            )
            kept[chunk, there, :] = active
            yield
            if chunk + 1 < CHUNKS:
                pre = dot_nn(hid_f, wide[chunk + 1])
            branch_f = branch_f + dot_nn(active, w_down[cols, :])
            yield
        gate_f = sigmoid(gate_f + vecs[7:8])
        outputs[here, :] = (middle + gate_f * branch_f).astype(BF16)
        grad_branch_f = (grad * gate_f).astype(BF16)
        grad_zf = (grad * branch_f * gate_f * (1.0 - gate_f)).astype(BF16)
        s_grad_f[there, :] = grad_branch_f
        grad_zf_ref[here, :] = grad_zf
        s_vec[6] += fold_rows(grad_branch_f.astype(F32))
        s_vec[7] += fold_rows(grad_zf.astype(F32))
        yield
        grad_hidden = dot_nt(grad_zf, gate_ffn[...])
        grad_active = dot_nt(grad_branch_f, w_down[chunks[0], :])
        yield
        for chunk, cols in enumerate(chunks):
            grad_pre = (grad_active * slope[here, cols]).astype(BF16)
            kept[CHUNKS + chunk, there, :] = grad_pre
            s_vec[8 + chunk] += fold_rows(grad_pre.astype(F32))
            yield
            if chunk + 1 < CHUNKS:
                grad_active = dot_nt(grad_branch_f, w_down[chunks[chunk + 1], :])
            grad_hidden = grad_hidden + dot_nt(grad_pre, wide[chunk])
            yield
        s_vec[4] += fold_rows(grad_hidden * normed)
        s_vec[5] += fold_rows(grad_hidden)
        grad_middle = grad + norm_back(grad_hidden * vecs[4:5], normed, inv_std)
        grad_middle_ref[here, :] = grad_middle
        grad_branch_a = (grad_middle * gate_a).astype(BF16)
        grad_za = (grad_middle * branch_a * gate_a * (1.0 - gate_a)).astype(BF16)
        grad_za_ref[here, :] = grad_za
        grad_a_ref[here, :] = grad_branch_a
        s_vec[2] += fold_rows(grad_branch_a.astype(F32))
        s_vec[3] += fold_rows(grad_za.astype(F32))
        yield
        grad_attended[here, :] = dot_nt(grad_branch_a, w_out[...]).astype(BF16)
        yield

    interleave([part(at) for at in range(0, MID_ROWS, HALF_ROWS)])

    @pl.when(step == steps - 1)
    def _():
        for chunk in range(CHUNKS):
            at = ROW_DOWN - base + chunk * D
            weights[at : at + D, :] = dot_tn(kept[chunk], s_grad_f[...]).astype(BF16)
        weights[ROW_VEC - base :, :] = jnp.sum(s_vec[...], 1).astype(BF16)
        copies = emit_copies(weights, base, 3, where, keep_three, send_three, sems_three)
        start_all(copies)
        for chunk in range(CHUNKS):
            wide[chunk] = dot_tn(s_hid_f[...], kept[CHUNKS + chunk]).astype(BF16)
        shuffle = spread_matrix(256)
        for block in range(FF // 256):
            parts = [wide[chunk, block * 64 : (block + 1) * 64, :] for chunk in range(CHUNKS)]
            at = ROW_IN - base + block * 256
            weights[at : at + 256, :] = dot_tn(shuffle, jnp.concatenate(parts, 0)).astype(BF16)
        last = emit_copies(weights, base, 2, where, keep_two, send_two, sems_two)
        start_all(last)
        carry[...] = weights[ROW_IN - base : PLANE_END[1] - base, :]
        wait_all(copies)
        wait_all(last)


def middle_part(where, tokens, grad_out, hidden_a, attended, w_outs, pieces):
    total = tokens.shape[0]
    steps = total // MID_ROWS
    carry = PLANE_END[1] - ROW_IN
    rows_at = lambda width: pl.BlockSpec((MID_ROWS, width), lambda i, *refs: (i, 0))
    shape = lambda kind=BF16: jax.ShapeDtypeStruct((total, D), kind)
    results, unused = call_kernel(
        functools.partial(middle_body, steps, pieces),
        [where, tokens, grad_out, hidden_a, *attended, *w_outs, *[piece.array for piece in pieces]],
        [],
        [rows_at(D)] * 3
        + [rows_at(GROUP)] * GROUPS
        + [whole(w_outs[0].shape)] * GROUPS
        + [UNREAD] * len(pieces),
        [rows_at(D)] * 7 + [whole((D, D))] + PLANE_SPEC * 2 + [whole((carry, D))],
        [shape(), shape(F32)]
        + [shape()] * 5
        + [jax.ShapeDtypeStruct((D, D), BF16)]
        + PLANE_OUT * 2
        + [jax.ShapeDtypeStruct((carry, D), BF16)],
        (steps,),
        "middle_part",
        (33e9, 50e6, 4e6),
        scratch=[
            pltpu.VMEM((ALL_ROWS - ROW_OUT, D), BF16),
            pltpu.VMEM((CHUNKS, D, D), BF16),
            pltpu.VMEM((MID_ROWS, FF), F32),
            pltpu.VMEM((VEC_ROWS, 8, D), F32),
            pltpu.VMEM((2 * CHUNKS, total, D), BF16),
            pltpu.VMEM((total, D), BF16),
            pltpu.VMEM((total, D), BF16),
            pltpu.SemaphoreType.DMA((SHARES,)),
            COPY_SEMS,
            COPY_SEMS,
        ],
    )
    return results


PLANE_OUT = [jax.ShapeDtypeStruct((HALF, BLOCK, D), BF16)] * 2
PLANE_SPEC = [UNREAD] * 2


def gates_body(where, *refs):
    att_refs, refs = refs[:GROUPS], refs[GROUPS:]
    hidden_a, hidden_f, grad_a, grad_za, grad_zf, late, keep, send, carry, rows, sems = refs
    att = jnp.concatenate([ref[...] for ref in att_refs], 1)
    rows[:D, :] = dot_tn(att, grad_a[...]).astype(BF16)
    rows[D : 2 * D, :] = dot_tn(hidden_a[...], grad_za[...]).astype(BF16)
    rows[2 * D : 3 * D, :] = dot_tn(hidden_f[...], grad_zf[...]).astype(BF16)
    rows[3 * D :, :] = late[...]
    copies = emit_copies(rows, ROW_OUT, 1, where, keep, send, sems)
    start_all(copies)
    carry[...] = rows[: PLANE_END[0] - ROW_OUT, :]
    wait_all(copies)


def gates_gradient(where, attended, hidden_a, hidden_f, grad_a, grad_za, grad_zf, late, through):
    total = hidden_a.shape[0]
    carry = PLANE_END[0] - ROW_OUT
    return call_kernel(
        gates_body,
        [where, *attended, hidden_a, hidden_f, grad_a, grad_za, grad_zf, late],
        through,
        [whole((total, GROUP))] * GROUPS + [whole((total, D))] * 5 + [whole(late.shape)],
        PLANE_SPEC + [whole((carry, D))],
        PLANE_OUT + [jax.ShapeDtypeStruct((carry, D), BF16)],
        (1,),
        "gates_gradient",
        (3.2e9, 14e6, 0),
        scratch=[pltpu.VMEM((3 * D + late.shape[0], D), BF16), COPY_SEMS],
    )


LAST_ROWS = 512


def last_body(steps, tok, grad_middle, grad_za, *refs):
    grads, refs = refs[: 3 * GROUPS], refs[3 * GROUPS :]
    w_three, refs = refs[:GROUPS], refs[GROUPS:]
    gate_attn, vec, input_grad, d_vec, factors, s_vec = refs
    step = pl.program_id(0)

    @pl.when(step == 0)
    def _():
        s_vec[...] = jnp.zeros_like(s_vec)
        for group in range(GROUPS):
            factors[:, group * GROUP : (group + 1) * GROUP] = w_three[group][...]

    vecs = vec[...].astype(F32)
    normed, inv_std = layer_stats(tok[...].astype(F32))
    grad_hidden = dot_nt(grad_za[...], gate_attn[...])
    for part, at in enumerate((ROW_QUERY, ROW_KEY, ROW_VALUE)):
        grad = jnp.concatenate([grads[3 * group + part][...] for group in range(GROUPS)], 1)
        grad_hidden += dot_nt(grad, factors[at : at + D, :])
    s_vec[0] += fold_rows(grad_hidden * normed)
    s_vec[1] += fold_rows(grad_hidden)
    input_grad[...] = (grad_middle[...] + norm_back(grad_hidden * vecs[0:1], normed, inv_std)).astype(BF16)

    @pl.when(step == steps - 1)
    def _():
        d_vec[...] = jnp.sum(s_vec[...], 1)


def last_part(tokens, grad_middle, grad_za, grads, w_three, gate_attn, vec, through):
    total = tokens.shape[0]
    steps = total // LAST_ROWS
    rows_at = lambda width: pl.BlockSpec((LAST_ROWS, width), lambda i, *refs: (i, 0))
    return call_kernel(
        functools.partial(last_body, steps),
        [tokens, grad_middle, grad_za, *grads, *w_three, gate_attn, vec],
        through,
        [rows_at(D)] * 3
        + [rows_at(GROUP)] * (3 * GROUPS)
        + [whole((ROW_OUT, GROUP))] * GROUPS
        + [whole((D, D)), whole((VEC_ROWS, D))],
        [rows_at(D), whole((VEC_ROWS, D))],
        [jax.ShapeDtypeStruct((total, D), BF16), jax.ShapeDtypeStruct((VEC_ROWS, D), F32)],
        (steps,),
        "last_part",
        (4.3e9, 20e6, 0),
        scalars=0,
        scratch=[pltpu.VMEM((ROW_OUT, D), BF16), pltpu.VMEM((VEC_ROWS, 8, D), F32)],
    )


def local_part(where, longs, tokens, out_grad, first_pieces, middle_pieces, before, later, collect):
    subs, length, unused = tokens.shape
    rows = tokens.reshape(subs * length, D)
    grads_in = out_grad.reshape(subs * length, D)
    (*kept, hidden_a, vec), passed = forward_group(0, longs, where, rows, first_pieces, before("forward0"))
    later("forward0", passed)
    second, passed = forward_group(1, longs, where, hidden_a, first_pieces, before("forward1"))
    later("forward1", passed)
    groups = [kept, second]
    attended = [group[3] for group in groups]
    (outputs, grad_middle, grad_za, grad_attended, hidden_f, grad_zf, grad_a, gate_attn, keep, send, *plane, carry) = (
        middle_part(where, rows, grads_in, hidden_a, attended, [group[6] for group in groups], middle_pieces())
    )
    collect(3, keep, send)
    collect(2, *plane)
    (*plane, carry), passed = gates_gradient(
        where, attended, hidden_a, hidden_f, grad_a, grad_za, grad_zf, carry, before("gates")
    )
    later("gates", passed)
    collect(1, *plane)
    grads = []
    for group, (query, key, value, att, extra, *unused_two) in enumerate(groups):
        (*three, keep, send), passed = backward_group(
            group, where, query, key, value, extra, att, grad_attended, hidden_a, carry, before(f"back{group}")
        )
        later(f"back{group}", passed)
        grads += three
        collect(("first", group), keep, send)
    w_three = [group[5] for group in groups]
    (input_grad, d_vec), passed = last_part(
        rows, grad_middle, grad_za, grads, w_three, gate_attn, vec, before("last")
    )
    later("last", passed)
    return outputs.reshape(tokens.shape), input_grad.reshape(tokens.shape), d_vec


def own_block(params, start, rows):
    share = params.shape[0]
    room = jnp.pad(params, (TILE, rows * D - share))
    return lax.dynamic_slice(room, (TILE - start % TILE,), (rows * D,)).reshape(rows, D).astype(BF16)


def move(axis, count, step):
    perm = [(i, step(i)) for i in range(count) if step(i) is not None]
    return lambda value: lax.ppermute(value, axis, perm)


def on_slice(tokens, out_grad, long_count, params):
    z, x, y, c = (lax.axis_index(axis) for axis in ("z", "x", "y", "c"))
    me = ((z * 2 + x) * 2 + y) * 2 + c
    share = params.shape[0]
    block = own_block(params, me * share, BLOCK)
    odd = z % 2 == 1
    ends = (z == 0) | (z == 3)
    swap_c = move("c", 2, lambda i: 1 - i)
    swap_x = move("x", 2, lambda i: 1 - i)
    swap_y = move("y", 2, lambda i: 1 - i)
    swap_xy = move(("x", "y"), 4, lambda i: 3 - i)
    z_one = move("z", 4, lambda i: i ^ 1)
    z_two = move("z", 4, lambda i: i ^ 2)
    inside = z < 4
    vec = block[VEC_AT : VEC_AT + VEC_ROWS]
    mine = jnp.concatenate([block, jnp.where(me == SHARES - 1, vec, jnp.zeros_like(vec))], 0)
    step_one = move("z", 4, {0: 2, 1: 0, 2: 3, 3: 1}.get)(mine)
    held = jnp.where(ends, mine, step_one)
    step_two = z_one(held)
    step_three = z_two(jnp.where(ends, step_one[:BLOCK], block))
    vec = jnp.where(odd, held, step_two)[BLOCK:]
    first = jnp.where(inside, jnp.where(z == 2, step_one, step_two)[:BLOCK], step_three)
    first = jnp.concatenate([first, vec], 0)[None]
    both = jnp.stack([jnp.where(z == 2, step_two, step_one)[:BLOCK], step_three])

    def in_plane(parts, planes):
        near = jnp.concatenate(parts, 0)
        blocks = [(plane, spot) for spot in range(HALF) for plane in planes]
        return [Piece(near, blocks, False), Piece(swap_c(near), blocks, True)]

    own = block[None]
    pieces = in_plane([own, swap_y(own), swap_x(own), swap_xy(own)], ((0,),))
    pieces += in_plane([first, swap_y(first), swap_x(first), swap_xy(first)], ((4,),))
    around = {"both": [swap_y(both), swap_x(both), swap_xy(both)]}
    top = {"both": both[:, :TILE_ROWS]}
    pair = ((5,), (6,))
    blocks = [(plane, 0) for plane in pair]
    both_pieces = [Piece(both, blocks, False), Piece(swap_c(both), blocks, True)]

    def middle_pieces():
        late = jnp.pad(top["both"], ((0, 0), (0, BLOCK - TILE_ROWS), (0, 0)))
        parts = around["both"]
        near = jnp.concatenate([jnp.where(inside, parts[0], late), *parts[1:]], 0)
        blocks = [(plane, spot) for spot in range(1, HALF) for plane in pair]
        return pieces + both_pieces + [Piece(near, blocks, False), Piece(swap_c(near), blocks, True)]

    early, late = ("first", 0), ("first", 1)
    arrived, at_chip, held = {}, {}, {}
    z_up = move("z", 4, lambda i: {0: 2, 1: 3}.get(i))
    z_down = move("z", 4, lambda i: {2: 0, 3: 1}.get(i))

    def collect(plane, keep, send):
        arrived[plane] = [keep, swap_c(send)]

    def send_around(name, planes, first=None):
        part = []
        for spot in range(HALF):
            sides = [[arrived[plane][side][spot].astype(F32) for plane in planes] for side in range(2)]
            keep, got = (jnp.concatenate(side, 1) for side in sides)
            if first is not None:
                keep = jnp.where(inside, keep, first[:, : keep.shape[1]])
            part.append((keep + got).astype(BF16))
        at_chip[name] = part[0]
        around[name] = (swap_y(part[1]), swap_x(part[2]), swap_xy(part[3]))

    def plane_sum(name):
        total = at_chip[name].astype(F32)
        for got in around[name]:
            total = total + got.astype(F32)
        return total

    def before(name):
        if name == "forward0":
            return []
        if name == "forward1":
            return [top["both"]]
        if name == "gates":
            return [arrived[2][0], arrived[3][0]]
        if name == "back0":
            send_around("upper", (2, 3))
            return [at_chip["upper"]]
        if name == "back1":
            held["upper"] = plane_sum("upper")
            held["up"] = z_up(held["upper"].astype(BF16))
            send_around("lower", (1, early), held["upper"])
            return [held["upper"], at_chip["lower"]]
        if name == "last":
            held["lower"] = plane_sum("lower")
            held["down"] = z_down(held["lower"].astype(BF16))
            send_around("late", (late,), held["lower"])
            upper = jnp.where(inside, held["upper"][:, : D + GROUP], held["lower"])
            upper = jnp.concatenate([upper, held["upper"][:, D + GROUP :]], 1) + held["up"].astype(F32)
            two, three = upper[:, :D], upper[:, D:]
            held["give"] = jnp.where(z == 2, three, two).astype(BF16)
            held["mine"] = jnp.where(z == 2, two, three)
            return [held["give"], held["mine"], held["lower"], at_chip["late"]]
        return []

    def later(name, passed):
        if name == "forward1":
            top["both"] = passed[0]
        if name == "gates":
            arrived[2][0], arrived[3][0] = passed
        if name == "back0":
            at_chip["upper"] = passed[0]
        if name == "back1":
            held["upper"], at_chip["lower"] = passed
        if name == "last":
            held["give"], held["mine"], held["lower"], at_chip["late"] = passed

    planes = [jnp.where(z == 0, 3, 0), jnp.where(z == 0, 1, jnp.where(z == 3, 2, 3)), jnp.where(z < 2, 2, 1)]
    where = jnp.stack([z, x, y, c, *planes]).astype(jnp.int32)
    outputs, input_grad, d_vec = local_part(
        where,
        long_count.reshape(-1),
        tokens,
        out_grad,
        pieces,
        middle_pieces,
        before,
        later,
        collect,
    )
    low = plane_sum("late")
    lower = jnp.where(inside, held["lower"], jnp.concatenate([low] * 3, 1)) + held["down"].astype(F32)
    one, zero = lower[:, :D], jnp.concatenate([lower[:, D:]] * 2, 1)
    give = jnp.where(z == 0, one.astype(BF16), jnp.where(z == 1, zero.astype(BF16), held["give"]))
    given = z_one(give).astype(F32)
    total = jnp.where(z == 0, zero, jnp.where(z == 1, one, held["mine"])) + given
    gains = jnp.where(inside, d_vec[:2], jnp.concatenate([low[:2]] * 2, 1))
    gains = gains + swap_c(gains)
    gains = (gains + swap_x(gains) + swap_y(gains) + swap_xy(gains)).reshape(2 * GROUPS, GROUP)
    lines = jnp.pad(gains.astype(BF16), ((0, TILE_ROWS - 2 * GROUPS), (0, 0)))
    message = jnp.concatenate([jnp.where(inside, low, given[:, :GROUP]).astype(BF16), lines], 0)
    for step in ({3: 0, 0: 3}, {2: 0, 1: 3}, {1: 0, 2: 3}):
        got = move("z", 4, step.get)(message).astype(F32)
        low = low + got[:BLOCK]
        gains = gains + got[BLOCK : BLOCK + 2 * GROUPS]
    total = jnp.where(z == 0, jnp.concatenate([total[:, :GROUP], low], 1), total)
    gains = jnp.where(me == SHARES - 1, gains.reshape(2, D), jnp.zeros((2, D), F32))
    total = total + jnp.pad(gains, ((VEC_AT, BLOCK - VEC_AT - 2), (0, 0)))
    param_grad = lax.dynamic_slice(total.reshape(-1), ((me * share) % TILE,), (share,))
    return (outputs, input_grad, param_grad)


def on_any(axes, count, tokens, out_grad, long_count, params):
    share = params.shape[0]
    me = lax.axis_index(axes)
    starts = [index * share // TILE * TILE_ROWS for index in range(count)]
    rows = max(-(-((index + 1) * share) // TILE) * TILE_ROWS - starts[index] for index in range(count))
    gathered = lax.all_gather(own_block(params, me * share, rows), axes, axis=0)
    merged = jnp.zeros((starts[-1] + rows, D), BF16)
    for index in range(count):
        merged = merged.at[starts[index] : starts[index] + rows].add(gathered[index])
    merged = merged[:ALL_ROWS]
    near, far = [], []
    for plane in range(PLANES):
        blocks = []
        for index in range(plane * IN_PLANE, (plane + 1) * IN_PLANE):
            end = STARTS[index + 1] if index + 1 < SHARES else ALL_ROWS
            piece = merged[STARTS[index] : end]
            blocks.append(jnp.pad(piece, ((0, BLOCK - piece.shape[0]), (0, 0))))
        spots = [(plane, spot) for spot in range(HALF)]
        near.append(Piece(jnp.stack(blocks[0::2]), spots, False))
        far.append(Piece(jnp.stack(blocks[1::2]), spots, True))
    vec = merged[ROW_VEC : ROW_VEC + VEC_ROWS]
    first_pieces = []
    for piece in (near[0], far[0]):
        lines = jnp.zeros((HALF, VEC_ROWS, D), BF16)
        if piece is near[0]:
            lines = lines.at[0].set(vec)
        first_pieces.append(Piece(jnp.concatenate([piece.array, lines], 1), piece.blocks, piece.other))
    by_share = [None] * SHARES

    halves = []

    def collect(plane, keep, send):
        if isinstance(plane, tuple):
            halves.append((keep, send))
            if len(halves) < GROUPS:
                return
            keep, send = (jnp.concatenate([half[side] for half in halves], 2) for side in range(2))
            plane = 0
        for spot in range(HALF):
            by_share[plane * IN_PLANE + 2 * spot] = keep[spot]
            by_share[plane * IN_PLANE + 2 * spot + 1] = send[spot]

    outputs, input_grad, d_vec = local_part(
        jnp.zeros((7,), jnp.int32),
        long_count.reshape(-1),
        tokens,
        out_grad,
        first_pieces,
        lambda: near[1:] + far[1:],
        lambda name: [],
        lambda name, passed: None,
        collect,
    )
    ends = STARTS[1:] + [ALL_ROWS]
    gradient = jnp.concatenate([part[: ends[i] - STARTS[i]] for i, part in enumerate(by_share)], 0)
    gradient = gradient.at[ROW_VEC : ROW_VEC + VEC_ROWS].add(d_vec.astype(BF16))
    gradient = jnp.pad(gradient, ((0, max(0, starts[-1] + rows - ALL_ROWS)), (0, 0)))
    spread = jnp.stack([gradient[start : start + rows] for start in starts])
    summed = lax.psum_scatter(spread, axes, scatter_dimension=0)
    param_grad = lax.dynamic_slice(summed.astype(F32).reshape(-1), ((me * share) % TILE,), (share,))
    return (outputs, input_grad, param_grad)


def solution(mesh):
    axes = ("wide", "narrow")
    count = math.prod(mesh.shape[axis] for axis in axes)
    step = functools.partial(on_any, axes, count)
    if mesh.shape["wide"] == 8 and mesh.shape["narrow"] == 4:
        axes = ("z", "x", "y", "c")
        mesh = Mesh(mesh.devices.reshape(4, 2, 2, 2), axes)
        step = on_slice
    return jax.shard_map(
        step,
        mesh=mesh,
        in_specs=(P(None, axes, None), P(None, axes, None), P(None, axes), P(axes)),
        out_specs=(P(None, axes, None), P(None, axes, None), P(axes)),
        check_vma=False,
    )
```

```python
import functools
import math

import jax
import jax.numpy as jnp
from jax import lax
from jax.experimental import pallas as pl
from jax.experimental.pallas import tpu as pltpu
from jax.sharding import Mesh, PartitionSpec as P

D = 512
FF = 2048
HEADS = 8
HD = 64
SHORT = 512
LONG = 1024
PAIR = 2 * HD
GROUP = 2 * PAIR
GROUPS = D // GROUP
STRIP = 256

TILE_ROWS = 16
TILE = TILE_ROWS * D

layer_eps = 1e-05
far_below = -1e30

F32 = jnp.float32
BF16 = jnp.bfloat16
MB = 1024 * 1024


def dot_nn(left, right):
    return lax.dot_general(left, right, (((1,), (0,)), ((), ())), preferred_element_type=F32)


def dot_nt(left, right):
    return lax.dot_general(left, right, (((1,), (1,)), ((), ())), preferred_element_type=F32)


def dot_tn(left, right):
    return lax.dot_general(left, right, (((0,), (0,)), ((), ())), preferred_element_type=F32)


def layer_stats(values):
    average = jnp.mean(values, -1, keepdims=True)
    centred = values - average
    variance = jnp.mean(centred * centred, -1, keepdims=True)
    inv_std = lax.rsqrt(variance + layer_eps)
    return (centred * inv_std, inv_std)


def norm_back(grad_hat, normed, inv_std):
    return inv_std * (
        grad_hat
        - jnp.mean(grad_hat, -1, keepdims=True)
        - normed * jnp.mean(grad_hat * normed, -1, keepdims=True)
    )


def sigmoid(values):
    return 0.5 * jnp.tanh(0.5 * values) + 0.5


def fold_rows(values):
    return jnp.sum(values.reshape(values.shape[0] // 8, 8, values.shape[1]), 0)


ROW_QUERY = 0
ROW_KEY = 512
ROW_VALUE = 1024
ROW_OUT = 1536
ROW_GATE_A = 2048
ROW_GATE_F = 2560
ROW_IN = 3072
ROW_DOWN = 5120
ROW_VEC = 7168
ALL_ROWS = 7184
VEC_ROWS = 16
ENTRIES = 6 * D * D + 2 * D * FF + 8 * D + FF

SHARES = 32
PLANES = 4
IN_PLANE = SHARES // PLANES
HALF = IN_PLANE // 2
STARTS = [index * (ENTRIES // SHARES) // TILE * TILE_ROWS for index in range(SHARES)]
BLOCK = max(
    -(-((index + 1) * (ENTRIES // SHARES)) // TILE) * TILE_ROWS - STARTS[index] for index in range(SHARES)
)
PLANE_END = [STARTS[(plane + 1) * IN_PLANE - 1] + BLOCK for plane in range(PLANES)]
VEC_AT = ROW_VEC - STARTS[-1]

VMEM = pltpu.CompilerParams(vmem_limit_bytes=62 * MB)


def whole(shape, single=True):
    rank = len(shape)
    kwargs = {"pipeline_mode": pl.Buffered(1)} if single else {}
    return pl.BlockSpec(shape, lambda *unused: (0,) * rank, **kwargs)


def share_row(where, plane, spot, other):
    core = 1 - where[3] if other else where[3]
    share = 2 * ((where[1] * 2 + where[2]) ^ spot) + core
    return ((plane * IN_PLANE + share) * (ENTRIES // SHARES)) // TILE * TILE_ROWS


class Piece:
    def __init__(self, array, blocks, other):
        self.array, self.blocks, self.other = array, blocks, other


def place_piece(target, base, where, piece, block_of, lowest):
    def place(index, plane, spot):
        at = share_row(where, plane, spot, piece.other) - base
        rows = pl.ds(pl.multiple_of(at, TILE_ROWS), BLOCK)
        target[rows, :] = target[rows, :] + block_of(index)

    for index, (plane, spot) in enumerate(piece.blocks):
        if not isinstance(plane, tuple):
            if (plane == 0) == lowest:
                place(index, plane, spot)
            continue
        plane = where[plane[0]]
        pl.when((plane == 0) == lowest)(functools.partial(place, index, plane, spot))


UNREAD = pl.BlockSpec(memory_space=pl.ANY)


def call_kernel(body, arguments, through, in_specs, out_specs, out_shape, grid, name, cost, scalars=1, scratch=(), alias=None):
    inputs, outputs, passed = len(arguments), len(out_specs), len(through)
    aliases = {inputs + index: outputs + index for index in range(passed)}
    aliases.update(alias or {})

    def run(*refs):
        at = inputs + passed
        body(*refs[:inputs], *refs[at : at + outputs], *refs[at + outputs + passed :])

    results = pl.pallas_call(
        run,
        name=name,
        grid_spec=pltpu.PrefetchScalarGridSpec(
            num_scalar_prefetch=scalars,
            grid=grid,
            in_specs=list(in_specs) + [UNREAD] * passed,
            out_specs=list(out_specs) + [UNREAD] * passed,
            scratch_shapes=list(scratch),
        ),
        out_shape=list(out_shape) + [jax.ShapeDtypeStruct(array.shape, array.dtype) for array in through],
        input_output_aliases=aliases,
        compiler_params=VMEM,
        cost_estimate=pl.CostEstimate(flops=int(cost[0]), bytes_accessed=int(cost[1]), transcendentals=int(cost[2])),
    )(*arguments, *through)
    return results[:outputs], results[outputs:]


def emit_copies(source, base, plane, where, keep, send, sems, column=0):
    copies = []
    cols = pl.ds(column, source.shape[1])
    for spot in range(HALF):
        for out, other in ((keep[spot], False), (send.at[spot], True)):
            at = pl.multiple_of(share_row(where, plane, spot, other) - base, TILE_ROWS)
            source_rows = source.at[pl.ds(at, BLOCK), :]
            copies.append(pltpu.make_async_copy(source_rows, out.at[:, cols], sems.at[len(copies)]))
    return copies


def start_all(copies):
    for copy in copies:
        copy.start()


def wait_all(copies):
    for copy in copies:
        copy.wait()


COPY_SEMS = pltpu.SemaphoreType.DMA((IN_PLANE,))


def plane_out(width):
    return [jax.ShapeDtypeStruct((BLOCK, width), BF16)] * HALF + [jax.ShapeDtypeStruct((HALF, BLOCK, width), BF16)]


PLANE_SPEC = [UNREAD] * (HALF + 1)


def split_three(values):
    high = values.astype(BF16)
    rest = values - high.astype(F32)
    middle = rest.astype(BF16)
    low = (rest - middle.astype(F32)).astype(BF16)
    return high, middle, low


def pick_lanes(base, lane, first, columns):
    out = base
    for offset, column in enumerate(columns):
        out = jnp.where(lane == first + offset, column, out)
    return out


def pipeline(units, lag, *stages):
    held, results = {}, {}
    last = len(stages) - 1
    for turn in range(len(units) + last * lag):
        for stage in (0, *range(last, 0, -1)):
            unit = turn - stage * lag
            if 0 <= unit < len(units):
                value = stages[stage](units[unit], *(held.pop(unit) if stage else ()))
                if stage < last:
                    held[unit] = value
                else:
                    results[units[unit]] = value
    return results


def attend_columns(is_long, query, key, value, attended, extra):
    strips = LONG // STRIP
    key_ids = lax.broadcasted_iota(jnp.int32, (STRIP, STRIP), 0)
    query_ids = lax.broadcasted_iota(jnp.int32, (STRIP, STRIP), 1)
    causal = query_ids >= key_ids
    cut = jnp.where(is_long, 0.0, far_below)
    late = jnp.where(is_long, 0.0, 1.0)
    lane = lax.broadcasted_iota(jnp.int32, (LONG, PAIR), 1)
    ones = jnp.ones((TILE_ROWS, LONG), BF16)
    q_heads, k_pairs, v_heads = [], [], []
    for pair in range(query.shape[1] // PAIR):
        cols = slice(pair * PAIR, (pair + 1) * PAIR)
        rows = query[:, cols]
        zero = jnp.zeros_like(rows)
        q_heads += [jnp.where(lane < HD, rows, zero), jnp.where(lane >= HD, rows, zero)]
        k_pairs.append(key[:, cols])
        turned = value[:, cols].astype(F32).T.astype(BF16)
        v_heads += [jnp.concatenate([turned[:HD], ones], 0), jnp.concatenate([turned[HD:], ones], 0)]

    def scores_of(unit):
        strip, head = unit
        lo, reach = strip * STRIP, (strip + 1) * STRIP
        return (dot_nt(k_pairs[head // 2][:reach], q_heads[head][lo:reach]),)

    def soften(unit, scores):
        strip, unused = unit
        lo = strip * STRIP
        parts = []
        if lo >= SHORT:
            parts.append(scores[:SHORT] + cut)
            if lo > SHORT:
                parts.append(scores[SHORT:lo])
        elif strip:
            parts.append(scores[:lo])
        parts.append(jnp.where(causal, scores[lo:], far_below))
        scores = jnp.concatenate(parts, 0)
        largest = jnp.max(scores, 0, keepdims=True)
        return jnp.exp(scores - largest).astype(BF16), largest

    def finish(unit, shifted, largest):
        strip, head = unit
        out = dot_nn(v_heads[head][:, : (strip + 1) * STRIP], shifted)
        sum_exp = out[HD : HD + 1]
        return out[:HD] * (1.0 / sum_exp), largest + jnp.log(sum_exp)

    units = [(strip, head) for strip in range(strips) for head in range(len(q_heads))]
    results = pipeline(units, 2, scores_of, soften, finish)
    for strip in range(strips):
        rows = slice(strip * STRIP, (strip + 1) * STRIP)
        for pair in range(len(k_pairs)):
            cols = slice(pair * PAIR, (pair + 1) * PAIR)
            two = [results[(strip, 2 * pair + side)] for side in range(2)]
            attended[rows, cols] = jnp.concatenate([out for out, unused in two], 0).T.astype(BF16)
            lines = [part.astype(F32) for unused, logsum in two for part in split_three(-logsum)]
            lines.append(jnp.broadcast_to(late if strip * STRIP >= SHORT else 0.0, (1, STRIP)))
            lines.append(jnp.zeros((PAIR - 7, STRIP), F32))
            extra[rows, cols] = jnp.concatenate(lines, 0).T.astype(BF16)


def block_columns(source, index):
    return source[index, :BLOCK, :GROUP]


def forward_body(first, pieces, longs, where, rows_in, *rest):
    sources, rest = rest[: len(pieces)], rest[len(pieces) :]
    if first:
        query, key, value, attended, extra, w_three, w_out, hidden, vec, weights = rest
    else:
        query, key, value, attended, extra, w_three, w_out, weights = rest
    sub = pl.program_id(0)

    @pl.when(sub == 0)
    def _():
        weights[...] = jnp.zeros_like(weights)
        for piece, source in zip(pieces, sources):
            place_piece(weights, 0, where, piece, functools.partial(block_columns, source), True)
        w_three[...] = weights[:ROW_OUT, :]
        w_out[...] = weights[ROW_OUT:, :]
        if first:
            total = jnp.zeros((VEC_ROWS, D), BF16)
            for source in sources:
                if source.shape[1] > BLOCK:
                    for index in range(source.shape[0]):
                        total = total + source[index, BLOCK:, :]
            vec[...] = total

    if first:
        normed, unused = layer_stats(rows_in[...].astype(F32))
        lines = vec[...].astype(F32)
        hid = (normed * lines[0:1] + lines[1:2]).astype(BF16)
        hidden[...] = hid
    else:
        hid = rows_in[...]
    q_rows = (dot_nn(hid, weights[ROW_QUERY : ROW_QUERY + D, :]) * (1.0 / math.sqrt(HD))).astype(BF16)
    k_rows = dot_nn(hid, weights[ROW_KEY : ROW_KEY + D, :]).astype(BF16)
    v_rows = dot_nn(hid, weights[ROW_VALUE : ROW_VALUE + D, :]).astype(BF16)
    query[...] = q_rows
    key[...] = k_rows
    value[...] = v_rows
    attend_columns(longs[sub] > 0, q_rows, k_rows, v_rows, attended, extra)


def forward_group(group, longs, where, rows_in, pieces, through):
    first = group == 0
    total = rows_in.shape[0]
    rows = pl.BlockSpec((LONG, D), lambda s, *refs: (s, 0))
    part = pl.BlockSpec((LONG, GROUP), lambda s, *refs: (s, 0))
    width = D if first else GROUP
    blocks = [
        pl.BlockSpec(piece.array.shape[:2] + (width,), lambda s, *refs: (0, 0, group), pipeline_mode=pl.Buffered(1))
        for piece in pieces
    ]
    tail = PLANE_END[0] - ROW_OUT
    out_specs = [part] * 5 + [whole((ROW_OUT, GROUP)), whole((tail, GROUP))]
    out_shape = [jax.ShapeDtypeStruct((total, GROUP), BF16)] * 5 + [
        jax.ShapeDtypeStruct((ROW_OUT, GROUP), BF16),
        jax.ShapeDtypeStruct((tail, GROUP), BF16),
    ]
    if first:
        out_specs += [rows, whole((VEC_ROWS, D))]
        out_shape += [jax.ShapeDtypeStruct((total, D), BF16), jax.ShapeDtypeStruct((VEC_ROWS, D), BF16)]
    return call_kernel(
        functools.partial(forward_body, first, pieces),
        [longs, where, rows_in, *[piece.array for piece in pieces]],
        through,
        [rows] + blocks,
        out_specs,
        out_shape,
        (total // LONG,),
        "forward_group",
        (8e9, 12e6, 4e6) if first else (0, 0, 0),
        scalars=2,
        scratch=[pltpu.VMEM((PLANE_END[0], GROUP), BF16)],
    )


def attend_back_rows(query, key, value, extra, attended, grad, grad_query, grad_key, grad_value):
    strips = LONG // STRIP
    lane = lax.broadcasted_iota(jnp.int32, (LONG, PAIR), 1)
    row = lax.broadcasted_iota(jnp.int32, (LONG, PAIR), 0)
    row_ids = lax.broadcasted_iota(jnp.int32, (STRIP, STRIP), 0)
    col_ids = lax.broadcasted_iota(jnp.int32, (STRIP, STRIP), 1)
    causal = row_ids >= col_ids
    early = jnp.where((lane == 6) & (row < SHORT), far_below, 0.0)
    v_tail = jnp.where(lane < 3, 1.0, 0.0).astype(BF16)
    heads, pairs = [], query.shape[1] // PAIR
    for pair in range(pairs):
        cols = slice(pair * PAIR, (pair + 1) * PAIR)
        q_all, k_all, v_all, g_all, x_all = (ref[:, cols] for ref in (query, key, value, grad, extra))
        product = g_all.astype(F32) * attended[:, cols].astype(F32)
        zero = jnp.zeros_like(q_all)
        v_wide = jnp.concatenate([v_all, v_tail], 1)
        q_turned = q_all.astype(F32).T.astype(BF16)
        g_turned = g_all.astype(F32).T.astype(BF16)
        for side in range(2):
            mine = (lane < HD) if side == 0 else (lane >= HD)
            own = slice(side * HD, (side + 1) * HD)
            delta = jnp.sum(jnp.where(mine, product, 0.0), -1, keepdims=True)
            d_tail = pick_lanes(
                jnp.zeros((LONG, PAIR), F32), lane, 0, [part.astype(F32) for part in split_three(-delta)]
            )
            ones = jnp.where((lane >= 3 * side) & (lane < 3 * side + 3), 1.0, early).astype(BF16)
            heads.append(
                (
                    jnp.where(mine, k_all, zero),
                    q_turned[own],
                    g_turned[own],
                    jnp.concatenate([jnp.where(mine, q_all, zero), x_all], 1),
                    jnp.concatenate([jnp.where(mine, g_all, zero), d_tail.astype(BF16)], 1),
                    jnp.concatenate([k_all, ones], 1),
                    v_wide,
                )
            )

    def products(unit):
        strip, head = unit
        lo, hi = strip * STRIP, (strip + 1) * STRIP
        unused, unused, unused, q_wide, g_wide, k_wide, v_wide = heads[head]
        return dot_nt(q_wide[lo:hi], k_wide[:hi]), dot_nt(g_wide[lo:hi], v_wide[:hi])

    def soften(unit, scores, slope):
        lo = unit[0] * STRIP
        soft = jnp.exp(scores)
        last = jnp.where(causal, soft[:, lo:], 0.0)
        soft = jnp.concatenate([soft[:, :lo], last], 1) if lo else last
        return soft.astype(BF16), (soft * slope).astype(BF16)

    key_sum, value_sum = {}, {}

    def gradients(unit, soft, scores):
        strip, head = unit
        lo, hi = strip * STRIP, (strip + 1) * STRIP
        k_head, q_turned, g_turned, *unused = heads[head]
        value_part = dot_nn(g_turned[:, lo:hi], soft)
        key_part = dot_nn(q_turned[:, lo:hi], scores)
        for block in range(strip + 1):
            cols, at = slice(block * STRIP, (block + 1) * STRIP), (block, head)
            for total, part in ((value_sum, value_part), (key_sum, key_part)):
                total[at] = total[at] + part[:, cols] if at in total else part[:, cols]
        return dot_nn(scores, k_head[:hi])

    units = [(strip, head) for strip in range(strips) for head in range(len(heads))]
    results = pipeline(units, 1, products, soften, gradients)
    for block in range(strips):
        rows = slice(block * STRIP, (block + 1) * STRIP)
        for pair in range(pairs):
            cols = slice(pair * PAIR, (pair + 1) * PAIR)
            ends = [(block, 2 * pair), (block, 2 * pair + 1)]
            two = results[ends[0]] + results[ends[1]]
            grad_query[rows, cols] = (two * (1.0 / math.sqrt(HD))).astype(BF16)
            grad_key[rows, cols] = jnp.concatenate([key_sum[at] for at in ends], 0).T.astype(BF16)
            grad_value[rows, cols] = jnp.concatenate([value_sum[at] for at in ends], 0).T.astype(BF16)


def backward_body(steps, where, query, key, value, extra, attended, grad, hidden, late, *refs):
    (grad_query, grad_key, grad_value), keep = refs[:3], refs[3 : 3 + HALF]
    send, total, rows, sems = refs[3 + HALF :]
    step = pl.program_id(0)
    attend_back_rows(query, key, value, extra, attended, grad, grad_query, grad_key, grad_value)
    three = jnp.concatenate([grad_query[...], grad_key[...], grad_value[...]], 1)
    now = dot_tn(hidden[...], three)

    @pl.when(step == 0)
    def _():
        total[...] = now

    @pl.when(step > 0)
    def _():
        total[...] = total[...] + now

    @pl.when(step == steps - 1)
    def _():
        for part, at in enumerate((ROW_QUERY, ROW_KEY, ROW_VALUE)):
            rows[at : at + D, :] = total[:, part * GROUP : (part + 1) * GROUP].astype(BF16)
        rows[ROW_OUT:, :] = late[...]
        copies = emit_copies(rows, 0, 0, where, keep, send, sems)
        start_all(copies)
        wait_all(copies)


def backward_group(group, where, query, key, value, extra, attended, grad, hidden, late, through):
    total = query.shape[0]
    steps = total // LONG
    part = pl.BlockSpec((LONG, GROUP), lambda s, *refs: (s, 0))
    return call_kernel(
        functools.partial(backward_body, steps),
        [where, query, key, value, extra, attended, grad, hidden, late],
        through,
        [part] * 5
        + [
            pl.BlockSpec((LONG, GROUP), lambda s, *refs: (s, group)),
            pl.BlockSpec((LONG, D), lambda s, *refs: (s, 0)),
            pl.BlockSpec((late.shape[0], GROUP), lambda s, *refs: (0, group), pipeline_mode=pl.Buffered(1)),
        ],
        [part] * 3 + PLANE_SPEC,
        [jax.ShapeDtypeStruct((total, GROUP), BF16)] * 3 + plane_out(GROUP),
        (steps,),
        "backward_group",
        (14e9, 16e6, 4e6),
        scratch=[
            pltpu.VMEM((D, 3 * GROUP), F32),
            pltpu.VMEM((ROW_OUT + late.shape[0], GROUP), BF16),
            COPY_SEMS,
        ],
    )


MID_ROWS = 512
HALF_ROWS = 256
STAGE_ROWS = 256
STAGE = 8
CHUNKS = FF // D
TANH_SCALE = math.sqrt(2.0 / math.pi)


def spread_matrix(size):
    quarter = size // CHUNKS
    to = lax.broadcasted_iota(jnp.int32, (size, size), 0)
    source = lax.broadcasted_iota(jnp.int32, (size, size), 1)
    return (source == CHUNKS * (to % quarter) + to // quarter).astype(BF16)


def interleave(parts):
    started, live = 0, []
    while started < len(parts) or live:
        if started < len(parts):
            live.append(parts[started])
            started += 1
        live = [part for part in live if next(part, True) is None]


def middle_body(steps, pieces, where, tok, grad_out, hidden_a, *refs):
    att_refs, wo_refs, refs = refs[:GROUPS], refs[GROUPS : 2 * GROUPS], refs[2 * GROUPS :]
    sources, refs = refs[: len(pieces)], refs[len(pieces) :]
    (outputs, grad_middle_ref, grad_za_ref, grad_attended, hid_f_ref, grad_zf_ref, grad_a_ref, gate_copy) = refs[:8]
    keep, send = refs[8 : 8 + HALF], refs[8 + HALF]
    carry, weights, wide, slope, s_vec, kept, s_hid_f, s_grad_f = refs[9 + HALF : -3]
    load_sems, sems_three, sems_two = refs[-3:]
    step = pl.program_id(0)
    base = ROW_OUT

    @pl.when(step == 0)
    def _():
        staged = []
        for piece, source in zip(pieces, sources):
            for index in range(len(piece.blocks)):
                slot = len(staged)
                to = kept.at[slot // STAGE, pl.ds(slot % STAGE * STAGE_ROWS, BLOCK), :]
                staged.append((to, pltpu.make_async_copy(source.at[index, pl.ds(0, BLOCK), :], to, load_sems.at[slot])))
                staged[-1][1].start()
        weights[...] = jnp.zeros_like(weights)
        for group in range(GROUPS):
            weights[: PLANE_END[0] - ROW_OUT, group * GROUP : (group + 1) * GROUP] = wo_refs[group][...]
        at_slot = 0
        for piece in pieces:
            count = len(piece.blocks)
            here = staged[at_slot : at_slot + count]
            wait_all([copy for unused, copy in here])
            place_piece(weights, base, where, piece, lambda index, here=here: here[index][0][...], False)
            at_slot += count
        shuffle = spread_matrix(256)
        for block in range(FF // 256):
            at = ROW_IN - base + block * 256
            part = dot_nn(shuffle, weights[at : at + 256, :]).astype(BF16)
            for chunk in range(CHUNKS):
                wide[chunk, block * 64 : (block + 1) * 64, :] = part[chunk * 64 : (chunk + 1) * 64]
        gate_copy[...] = weights[ROW_GATE_A - base : ROW_GATE_A - base + D, :]
        s_vec[...] = jnp.zeros_like(s_vec)

    w_out = weights.at[ROW_OUT - base : ROW_OUT - base + D]
    gate_attn = weights.at[ROW_GATE_A - base : ROW_GATE_A - base + D]
    gate_ffn = weights.at[ROW_GATE_F - base : ROW_GATE_F - base + D]
    w_down = weights.at[ROW_DOWN - base : ROW_DOWN - base + FF]
    vecs = weights[ROW_VEC - base : ROW_VEC - base + VEC_ROWS, :].astype(F32)
    chunks = [slice(chunk * D, (chunk + 1) * D) for chunk in range(CHUNKS)]

    first_row = pl.multiple_of(step * MID_ROWS, MID_ROWS)

    def part(at):
        here = slice(at, at + HALF_ROWS)
        there = pl.ds(first_row + at, HALF_ROWS)
        hid_a = hidden_a[here, :]
        att = jnp.concatenate([ref[here, :] for ref in att_refs], 1)
        grad = grad_out[here, :].astype(F32)
        branch_a = dot_nn(att, w_out[...])
        gate_a = dot_nn(hid_a, gate_attn[...])
        yield
        branch_a = branch_a + vecs[2:3]
        gate_a = sigmoid(gate_a + vecs[3:4])
        middle = tok[here, :].astype(F32) + gate_a * branch_a
        normed, inv_std = layer_stats(middle)
        hid_f = (normed * vecs[4:5] + vecs[5:6]).astype(BF16)
        hid_f_ref[here, :] = hid_f
        s_hid_f[there, :] = hid_f
        yield
        gate_f = dot_nn(hid_f, gate_ffn[...])
        pre = dot_nn(hid_f, wide[0])
        yield
        branch_f = vecs[6:7]
        for chunk, cols in enumerate(chunks):
            pre = pre + vecs[8 + chunk : 9 + chunk]
            square = pre * pre
            bend = jnp.tanh(pre * (TANH_SCALE + (TANH_SCALE * 0.044715) * square))
            half = 0.5 * (1.0 + bend)
            active = (pre * half).astype(BF16)
            slope[here, cols] = half + (0.5 * pre) * (1.0 - bend * bend) * (
                TANH_SCALE + (3.0 * 0.044715 * TANH_SCALE) * square
            )
            kept[chunk, there, :] = active
            yield
            if chunk + 1 < CHUNKS:
                pre = dot_nn(hid_f, wide[chunk + 1])
            branch_f = branch_f + dot_nn(active, w_down[cols, :])
            yield
        gate_f = sigmoid(gate_f + vecs[7:8])
        outputs[here, :] = (middle + gate_f * branch_f).astype(BF16)
        grad_branch_f = (grad * gate_f).astype(BF16)
        grad_zf = (grad * branch_f * gate_f * (1.0 - gate_f)).astype(BF16)
        s_grad_f[there, :] = grad_branch_f
        grad_zf_ref[here, :] = grad_zf
        s_vec[6] += fold_rows(grad_branch_f.astype(F32))
        s_vec[7] += fold_rows(grad_zf.astype(F32))
        yield
        grad_hidden = dot_nt(grad_zf, gate_ffn[...])
        grad_active = dot_nt(grad_branch_f, w_down[chunks[0], :])
        yield
        for chunk, cols in enumerate(chunks):
            grad_pre = (grad_active * slope[here, cols]).astype(BF16)
            kept[CHUNKS + chunk, there, :] = grad_pre
            s_vec[8 + chunk] += fold_rows(grad_pre.astype(F32))
            yield
            if chunk + 1 < CHUNKS:
                grad_active = dot_nt(grad_branch_f, w_down[chunks[chunk + 1], :])
            grad_hidden = grad_hidden + dot_nt(grad_pre, wide[chunk])
            yield
        s_vec[4] += fold_rows(grad_hidden * normed)
        s_vec[5] += fold_rows(grad_hidden)
        grad_middle = grad + norm_back(grad_hidden * vecs[4:5], normed, inv_std)
        grad_middle_ref[here, :] = grad_middle
        grad_branch_a = (grad_middle * gate_a).astype(BF16)
        grad_za = (grad_middle * branch_a * gate_a * (1.0 - gate_a)).astype(BF16)
        grad_za_ref[here, :] = grad_za
        grad_a_ref[here, :] = grad_branch_a
        s_vec[2] += fold_rows(grad_branch_a.astype(F32))
        s_vec[3] += fold_rows(grad_za.astype(F32))
        yield
        grad_attended[here, :] = dot_nt(grad_branch_a, w_out[...]).astype(BF16)
        yield

    interleave([part(at) for at in range(0, MID_ROWS, HALF_ROWS)])

    @pl.when(step == steps - 1)
    def _():
        for chunk in range(CHUNKS):
            at = ROW_DOWN - base + chunk * D
            weights[at : at + D, :] = dot_tn(kept[chunk], s_grad_f[...]).astype(BF16)
        weights[ROW_VEC - base :, :] = jnp.sum(s_vec[...], 1).astype(BF16)
        copies = emit_copies(weights, base, 3, where, keep, send, sems_three, D)
        start_all(copies)
        for chunk in range(CHUNKS):
            wide[chunk] = dot_tn(s_hid_f[...], kept[CHUNKS + chunk]).astype(BF16)
        shuffle = spread_matrix(256)
        for block in range(FF // 256):
            parts = [wide[chunk, block * 64 : (block + 1) * 64, :] for chunk in range(CHUNKS)]
            at = ROW_IN - base + block * 256
            weights[at : at + 256, :] = dot_tn(shuffle, jnp.concatenate(parts, 0)).astype(BF16)
        last = emit_copies(weights, base, 2, where, keep, send, sems_two)
        start_all(last)
        carry[...] = weights[ROW_IN - base : PLANE_END[1] - base, :]
        wait_all(copies)
        wait_all(last)


def middle_part(where, tokens, grad_out, hidden_a, attended, w_outs, pieces):
    total = tokens.shape[0]
    steps = total // MID_ROWS
    carry = PLANE_END[1] - ROW_IN
    rows_at = lambda width: pl.BlockSpec((MID_ROWS, width), lambda i, *refs: (i, 0))
    shape = lambda kind=BF16: jax.ShapeDtypeStruct((total, D), kind)
    results, unused = call_kernel(
        functools.partial(middle_body, steps, pieces),
        [where, tokens, grad_out, hidden_a, *attended, *w_outs, *[piece.array for piece in pieces]],
        [],
        [rows_at(D)] * 3
        + [rows_at(GROUP)] * GROUPS
        + [whole(w_outs[0].shape)] * GROUPS
        + [UNREAD] * len(pieces),
        [rows_at(D)] * 7 + [whole((D, D))] + PLANE_SPEC + [whole((carry, D))],
        [shape(), shape(F32)]
        + [shape()] * 5
        + [jax.ShapeDtypeStruct((D, D), BF16)]
        + plane_out(2 * D)
        + [jax.ShapeDtypeStruct((carry, D), BF16)],
        (steps,),
        "middle_part",
        (33e9, 50e6, 4e6),
        scratch=[
            pltpu.VMEM((ALL_ROWS - ROW_OUT, D), BF16),
            pltpu.VMEM((CHUNKS, D, D), BF16),
            pltpu.VMEM((MID_ROWS, FF), F32),
            pltpu.VMEM((VEC_ROWS, 8, D), F32),
            pltpu.VMEM((2 * CHUNKS, total, D), BF16),
            pltpu.VMEM((total, D), BF16),
            pltpu.VMEM((total, D), BF16),
            pltpu.SemaphoreType.DMA((SHARES,)),
            COPY_SEMS,
            COPY_SEMS,
        ],
    )
    return results


def gates_body(where, *refs):
    att_refs, refs = refs[:GROUPS], refs[GROUPS:]
    hidden_a, hidden_f, grad_a, grad_za, grad_zf, late, *refs = refs
    keep, send, carry, sides, rows, load_sems, sems = refs[:HALF], *refs[HALF:]
    loads = []

    def load(source, to):
        loads.append(pltpu.make_async_copy(source, to, load_sems.at[len(loads)]))
        loads[-1].start()

    for group, ref in enumerate(att_refs):
        load(ref, sides.at[0, :, pl.ds(group * GROUP, GROUP)])
    for slot, ref in enumerate((grad_a, hidden_a, grad_za, hidden_f, grad_zf)):
        load(ref, sides.at[1 + slot])
    rows[3 * D :, :] = late[...]
    for at in range(3):
        wait_all(loads[: GROUPS + 1] if at == 0 else loads[GROUPS + 2 * at - 1 : GROUPS + 2 * at + 1])
        rows[at * D : (at + 1) * D, :] = dot_tn(sides[2 * at], sides[2 * at + 1]).astype(BF16)
    copies = emit_copies(rows, ROW_OUT, 1, where, keep, send, sems)
    start_all(copies)
    carry[...] = rows[: PLANE_END[0] - ROW_OUT, :]
    wait_all(copies)


def gates_gradient(where, attended, hidden_a, hidden_f, grad_a, grad_za, grad_zf, late, through):
    total = hidden_a.shape[0]
    carry = PLANE_END[0] - ROW_OUT
    return call_kernel(
        gates_body,
        [where, *attended, hidden_a, hidden_f, grad_a, grad_za, grad_zf, late],
        through,
        [UNREAD] * (GROUPS + 5) + [whole(late.shape)],
        PLANE_SPEC + [whole((carry, D))],
        plane_out(D) + [jax.ShapeDtypeStruct((carry, D), BF16)],
        (1,),
        "gates_gradient",
        (3.2e9, 14e6, 0),
        scratch=[
            pltpu.VMEM((6, total, D), BF16),
            pltpu.VMEM((3 * D + late.shape[0], D), BF16),
            pltpu.SemaphoreType.DMA((GROUPS + 5,)),
            COPY_SEMS,
        ],
    )


LAST_ROWS = 512


def last_body(steps, tok, grad_middle, grad_za, *refs):
    grads, refs = refs[: 3 * GROUPS], refs[3 * GROUPS :]
    w_three, refs = refs[:GROUPS], refs[GROUPS:]
    gate_attn, vec, input_grad, d_vec, factors, s_vec = refs
    step = pl.program_id(0)

    @pl.when(step == 0)
    def _():
        s_vec[...] = jnp.zeros_like(s_vec)
        for group in range(GROUPS):
            factors[:, group * GROUP : (group + 1) * GROUP] = w_three[group][...]

    vecs = vec[...].astype(F32)

    def part(at):
        here = slice(at, at + HALF_ROWS)
        grad_hidden = dot_nt(grad_za[here, :], gate_attn[...])
        for side, row in enumerate((ROW_QUERY, ROW_KEY, ROW_VALUE)):
            grad = jnp.concatenate([grads[3 * group + side][here, :] for group in range(GROUPS)], 1)
            grad_hidden += dot_nt(grad, factors[row : row + D, :])
        yield
        normed, inv_std = layer_stats(tok[here, :].astype(F32))
        s_vec[0] += fold_rows(grad_hidden * normed)
        s_vec[1] += fold_rows(grad_hidden)
        back = norm_back(grad_hidden * vecs[0:1], normed, inv_std)
        input_grad[here, :] = (grad_middle[here, :] + back).astype(BF16)
        yield

    interleave([part(at) for at in range(0, LAST_ROWS, HALF_ROWS)])

    @pl.when(step == steps - 1)
    def _():
        d_vec[...] = jnp.sum(s_vec[...], 1)


def last_part(tokens, grad_middle, grad_za, grads, w_three, gate_attn, vec, through):
    total = tokens.shape[0]
    steps = total // LAST_ROWS
    rows_at = lambda width: pl.BlockSpec((LAST_ROWS, width), lambda i, *refs: (i, 0))
    return call_kernel(
        functools.partial(last_body, steps),
        [tokens, grad_middle, grad_za, *grads, *w_three, gate_attn, vec],
        through,
        [rows_at(D)] * 3
        + [rows_at(GROUP)] * (3 * GROUPS)
        + [whole((ROW_OUT, GROUP))] * GROUPS
        + [whole((D, D)), whole((VEC_ROWS, D))],
        [rows_at(D), whole((VEC_ROWS, D))],
        [jax.ShapeDtypeStruct((total, D), BF16), jax.ShapeDtypeStruct((VEC_ROWS, D), F32)],
        (steps,),
        "last_part",
        (4.3e9, 20e6, 0),
        scalars=0,
        scratch=[pltpu.VMEM((ROW_OUT, D), BF16), pltpu.VMEM((VEC_ROWS, 8, D), F32)],
    )


def local_part(where, longs, tokens, out_grad, first_pieces, middle_pieces, before, later, collect):
    subs, length, unused = tokens.shape
    rows = tokens.reshape(subs * length, D)
    grads_in = out_grad.reshape(subs * length, D)
    (*kept, hidden_a, vec), passed = forward_group(0, longs, where, rows, first_pieces, before("forward0"))
    later("forward0", passed)
    second, passed = forward_group(1, longs, where, hidden_a, first_pieces, before("forward1"))
    later("forward1", passed)
    groups = [kept, second]
    attended = [group[3] for group in groups]
    (outputs, grad_middle, grad_za, grad_attended, hidden_f, grad_zf, grad_a, gate_attn, *plane, carry) = (
        middle_part(where, rows, grads_in, hidden_a, attended, [group[6] for group in groups], middle_pieces())
    )
    collect("upper", plane)
    (*plane, carry), passed = gates_gradient(
        where, attended, hidden_a, hidden_f, grad_a, grad_za, grad_zf, carry, before("gates")
    )
    later("gates", passed)
    collect(1, plane)
    grads = []
    for group, (query, key, value, att, extra, *unused_two) in enumerate(groups):
        results, passed = backward_group(
            group, where, query, key, value, extra, att, grad_attended, hidden_a, carry, before(f"back{group}")
        )
        later(f"back{group}", passed)
        grads += results[:3]
        collect(("first", group), results[3:])
    w_three = [group[5] for group in groups]
    (input_grad, d_vec), passed = last_part(
        rows, grad_middle, grad_za, grads, w_three, gate_attn, vec, before("last")
    )
    later("last", passed)
    return outputs.reshape(tokens.shape), input_grad.reshape(tokens.shape), d_vec


def own_block(params, start, rows):
    share = params.shape[0]
    room = jnp.pad(params, (TILE, rows * D - share))
    return lax.dynamic_slice(room, (TILE - start % TILE,), (rows * D,)).reshape(rows, D).astype(BF16)


def move(axis, count, step):
    perm = [(i, step(i)) for i in range(count) if step(i) is not None]
    return lambda value: lax.ppermute(value, axis, perm)


def on_slice(tokens, out_grad, long_count, params):
    z, x, y, c = (lax.axis_index(axis) for axis in ("z", "x", "y", "c"))
    me = ((z * 2 + x) * 2 + y) * 2 + c
    share = params.shape[0]
    block = own_block(params, me * share, BLOCK)
    odd = z % 2 == 1
    ends = (z == 0) | (z == 3)
    swap_c = move("c", 2, lambda i: 1 - i)
    swap_x = move("x", 2, lambda i: 1 - i)
    swap_y = move("y", 2, lambda i: 1 - i)
    swap_xy = move(("x", "y"), 4, lambda i: 3 - i)
    z_one = move("z", 4, lambda i: i ^ 1)
    z_two = move("z", 4, lambda i: i ^ 2)
    inside = z < 4
    vec = block[VEC_AT : VEC_AT + VEC_ROWS]
    mine = jnp.concatenate([block, jnp.where(me == SHARES - 1, vec, jnp.zeros_like(vec))], 0)
    step_one = move("z", 4, {0: 2, 1: 0, 2: 3, 3: 1}.get)(mine)
    held = jnp.where(ends, mine, step_one)
    step_two = z_one(held)
    step_three = z_two(jnp.where(ends, step_one[:BLOCK], block))
    vec = jnp.where(odd, held, step_two)[BLOCK:]
    first = jnp.where(inside, jnp.where(z == 2, step_one, step_two)[:BLOCK], step_three)
    first = jnp.concatenate([first, vec], 0)[None]
    both = jnp.stack([jnp.where(z == 2, step_two, step_one)[:BLOCK], step_three])

    def in_plane(parts, planes):
        near = jnp.concatenate(parts, 0)
        blocks = [(plane, spot) for spot in range(HALF) for plane in planes]
        return [Piece(near, blocks, False), Piece(swap_c(near), blocks, True)]

    own = block[None]
    pieces = in_plane([own, swap_y(own), swap_x(own), swap_xy(own)], ((0,),))
    pieces += in_plane([first, swap_y(first), swap_x(first), swap_xy(first)], ((4,),))
    around = {"both": [swap_y(both), swap_x(both), swap_xy(both)]}
    top = {"both": both[:, :TILE_ROWS]}
    pair = ((5,), (6,))
    blocks = [(plane, 0) for plane in pair]
    both_pieces = [Piece(both, blocks, False), Piece(swap_c(both), blocks, True)]

    def middle_pieces():
        late = jnp.pad(top["both"], ((0, 0), (0, BLOCK - TILE_ROWS), (0, 0)))
        parts = around["both"]
        near = jnp.concatenate([jnp.where(inside, parts[0], late), *parts[1:]], 0)
        blocks = [(plane, spot) for spot in range(1, HALF) for plane in pair]
        return pieces + both_pieces + [Piece(near, blocks, False), Piece(swap_c(near), blocks, True)]

    early, late = ("first", 0), ("first", 1)
    arrived, at_chip, held = {}, {}, {}
    z_up = move("z", 4, lambda i: {0: 2, 1: 3}.get(i))
    z_down = move("z", 4, lambda i: {2: 0, 3: 1}.get(i))

    def collect(plane, blocks):
        arrived[plane] = [list(blocks[:HALF]), swap_c(blocks[HALF])]

    def send_around(name, planes, first=None):
        part = []
        for spot in range(HALF):
            sides = [[arrived[plane][side][spot].astype(F32) for plane in planes] for side in range(2)]
            keep, got = (jnp.concatenate(side, 1) for side in sides)
            if first is not None:
                keep = jnp.where(inside, keep, first[:, : keep.shape[1]])
            part.append((keep + got).astype(BF16))
        at_chip[name] = part[0]
        around[name] = (swap_y(part[1]), swap_x(part[2]), swap_xy(part[3]))

    def plane_sum(name):
        total = at_chip[name].astype(F32)
        for got in around[name]:
            total = total + got.astype(F32)
        return total

    def before(name):
        if name == "forward0":
            return []
        if name == "forward1":
            return [top["both"]]
        if name == "gates":
            return arrived["upper"][0]
        if name == "back0":
            send_around("upper", ("upper",))
            return [at_chip["upper"]]
        if name == "back1":
            held["upper"] = plane_sum("upper")
            held["up"] = z_up(held["upper"].astype(BF16))
            send_around("lower", (1, early), held["upper"])
            return [held["upper"], at_chip["lower"]]
        if name == "last":
            held["lower"] = plane_sum("lower")
            held["down"] = z_down(held["lower"].astype(BF16))
            send_around("late", (late,), held["lower"])
            upper = jnp.where(inside, held["upper"][:, : D + GROUP], held["lower"])
            upper = jnp.concatenate([upper, held["upper"][:, D + GROUP :]], 1) + held["up"].astype(F32)
            two, three = upper[:, :D], upper[:, D:]
            held["give"] = jnp.where(z == 2, three, two).astype(BF16)
            held["mine"] = jnp.where(z == 2, two, three)
            return [held["give"], held["mine"], held["lower"], at_chip["late"]]
        return []

    def later(name, passed):
        if name == "forward1":
            top["both"] = passed[0]
        if name == "gates":
            arrived["upper"][0] = passed
        if name == "back0":
            at_chip["upper"] = passed[0]
        if name == "back1":
            held["upper"], at_chip["lower"] = passed
        if name == "last":
            held["give"], held["mine"], held["lower"], at_chip["late"] = passed

    planes = [jnp.where(z == 0, 3, 0), jnp.where(z == 0, 1, jnp.where(z == 3, 2, 3)), jnp.where(z < 2, 2, 1)]
    where = jnp.stack([z, x, y, c, *planes]).astype(jnp.int32)
    outputs, input_grad, d_vec = local_part(
        where,
        long_count.reshape(-1),
        tokens,
        out_grad,
        pieces,
        middle_pieces,
        before,
        later,
        collect,
    )
    low = plane_sum("late")
    lower = jnp.where(inside, held["lower"], jnp.concatenate([low] * 3, 1)) + held["down"].astype(F32)
    one, zero = lower[:, :D], jnp.concatenate([lower[:, D:]] * 2, 1)
    give = jnp.where(z == 0, one.astype(BF16), jnp.where(z == 1, zero.astype(BF16), held["give"]))
    given = z_one(give).astype(F32)
    total = jnp.where(z == 0, zero, jnp.where(z == 1, one, held["mine"])) + given
    gains = jnp.where(inside, d_vec[:2], jnp.concatenate([low[:2]] * 2, 1))
    gains = gains + swap_c(gains)
    gains = (gains + swap_x(gains) + swap_y(gains) + swap_xy(gains)).reshape(2 * GROUPS, GROUP)
    lines = jnp.pad(gains.astype(BF16), ((0, TILE_ROWS - 2 * GROUPS), (0, 0)))
    message = jnp.concatenate([jnp.where(inside, low, given[:, :GROUP]).astype(BF16), lines], 0)
    for step in ({3: 0, 0: 3}, {2: 0, 1: 3}, {1: 0, 2: 3}):
        got = move("z", 4, step.get)(message).astype(F32)
        low = low + got[:BLOCK]
        gains = gains + got[BLOCK : BLOCK + 2 * GROUPS]
    total = jnp.where(z == 0, jnp.concatenate([total[:, :GROUP], low], 1), total)
    gains = jnp.where(me == SHARES - 1, gains.reshape(2, D), jnp.zeros((2, D), F32))
    total = total + jnp.pad(gains, ((VEC_AT, BLOCK - VEC_AT - 2), (0, 0)))
    param_grad = lax.dynamic_slice(total.reshape(-1), ((me * share) % TILE,), (share,))
    return (outputs, input_grad, param_grad)


def on_any(axes, count, tokens, out_grad, long_count, params):
    share = params.shape[0]
    me = lax.axis_index(axes)
    starts = [index * share // TILE * TILE_ROWS for index in range(count)]
    rows = max(-(-((index + 1) * share) // TILE) * TILE_ROWS - starts[index] for index in range(count))
    gathered = lax.all_gather(own_block(params, me * share, rows), axes, axis=0)
    merged = jnp.zeros((starts[-1] + rows, D), BF16)
    for index in range(count):
        merged = merged.at[starts[index] : starts[index] + rows].add(gathered[index])
    merged = merged[:ALL_ROWS]
    near, far = [], []
    for plane in range(PLANES):
        blocks = []
        for index in range(plane * IN_PLANE, (plane + 1) * IN_PLANE):
            end = STARTS[index + 1] if index + 1 < SHARES else ALL_ROWS
            piece = merged[STARTS[index] : end]
            blocks.append(jnp.pad(piece, ((0, BLOCK - piece.shape[0]), (0, 0))))
        spots = [(plane, spot) for spot in range(HALF)]
        near.append(Piece(jnp.stack(blocks[0::2]), spots, False))
        far.append(Piece(jnp.stack(blocks[1::2]), spots, True))
    vec = merged[ROW_VEC : ROW_VEC + VEC_ROWS]
    first_pieces = []
    for piece in (near[0], far[0]):
        lines = jnp.zeros((HALF, VEC_ROWS, D), BF16)
        if piece is near[0]:
            lines = lines.at[0].set(vec)
        first_pieces.append(Piece(jnp.concatenate([piece.array, lines], 1), piece.blocks, piece.other))
    by_share = [None] * SHARES

    halves = []

    def collect(plane, blocks):
        if isinstance(plane, tuple):
            halves.append(blocks)
            if len(halves) < GROUPS:
                return
            blocks = [jnp.concatenate(parts, parts[0].ndim - 1) for parts in zip(*halves)]
            plane = 0
        places = (2, 3) if plane == "upper" else (plane,)
        for at, plane in enumerate(places):
            cols = slice(at * D, (at + 1) * D)
            for spot in range(HALF):
                by_share[plane * IN_PLANE + 2 * spot] = blocks[spot][:, cols]
                by_share[plane * IN_PLANE + 2 * spot + 1] = blocks[HALF][spot][:, cols]

    outputs, input_grad, d_vec = local_part(
        jnp.zeros((7,), jnp.int32),
        long_count.reshape(-1),
        tokens,
        out_grad,
        first_pieces,
        lambda: near[1:] + far[1:],
        lambda name: [],
        lambda name, passed: None,
        collect,
    )
    ends = STARTS[1:] + [ALL_ROWS]
    gradient = jnp.concatenate([part[: ends[i] - STARTS[i]] for i, part in enumerate(by_share)], 0)
    gradient = gradient.at[ROW_VEC : ROW_VEC + VEC_ROWS].add(d_vec.astype(BF16))
    gradient = jnp.pad(gradient, ((0, max(0, starts[-1] + rows - ALL_ROWS)), (0, 0)))
    spread = jnp.stack([gradient[start : start + rows] for start in starts])
    summed = lax.psum_scatter(spread, axes, scatter_dimension=0)
    param_grad = lax.dynamic_slice(summed.astype(F32).reshape(-1), ((me * share) % TILE,), (share,))
    return (outputs, input_grad, param_grad)


def solution(mesh):
    axes = ("wide", "narrow")
    count = math.prod(mesh.shape[axis] for axis in axes)
    step = functools.partial(on_any, axes, count)
    if mesh.shape["wide"] == 8 and mesh.shape["narrow"] == 4:
        axes = ("z", "x", "y", "c")
        mesh = Mesh(mesh.devices.reshape(4, 2, 2, 2), axes)
        step = on_slice
    return jax.shard_map(
        step,
        mesh=mesh,
        in_specs=(P(None, axes, None), P(None, axes, None), P(None, axes), P(axes)),
        out_specs=(P(None, axes, None), P(None, axes, None), P(axes)),
        check_vma=False,
    )
```

```python
import functools
import math

import jax
import jax.numpy as jnp
from jax import lax
from jax.experimental import pallas as pl
from jax.experimental.pallas import tpu as pltpu
from jax.sharding import Mesh, PartitionSpec as P

D = 512
FF = 2048
HEADS = 8
HD = 64
SHORT = 512
LONG = 1024
PAIR = 2 * HD
GROUP = 2 * PAIR
GROUPS = D // GROUP
STRIP = 256

TILE_ROWS = 16
TILE = TILE_ROWS * D

layer_eps = 1e-05
far_below = -1e30

F32 = jnp.float32
BF16 = jnp.bfloat16
MB = 1024 * 1024


def dot_nn(left, right):
    return lax.dot_general(left, right, (((1,), (0,)), ((), ())), preferred_element_type=F32)


def dot_nt(left, right):
    return lax.dot_general(left, right, (((1,), (1,)), ((), ())), preferred_element_type=F32)


def dot_tn(left, right):
    return lax.dot_general(left, right, (((0,), (0,)), ((), ())), preferred_element_type=F32)


def layer_stats(values):
    average = jnp.mean(values, -1, keepdims=True)
    centred = values - average
    variance = jnp.mean(centred * centred, -1, keepdims=True)
    inv_std = lax.rsqrt(variance + layer_eps)
    return (centred * inv_std, inv_std)


def norm_back(grad_hat, normed, inv_std):
    return inv_std * (
        grad_hat
        - jnp.mean(grad_hat, -1, keepdims=True)
        - normed * jnp.mean(grad_hat * normed, -1, keepdims=True)
    )


def sigmoid(values):
    return 0.5 * jnp.tanh(0.5 * values) + 0.5


def fold_rows(values):
    return jnp.sum(values.reshape(values.shape[0] // 8, 8, values.shape[1]), 0)


ROW_QUERY = 0
ROW_KEY = 512
ROW_VALUE = 1024
ROW_OUT = 1536
ROW_GATE_A = 2048
ROW_GATE_F = 2560
ROW_IN = 3072
ROW_DOWN = 5120
ROW_VEC = 7168
ALL_ROWS = 7184
VEC_ROWS = 16
ENTRIES = 6 * D * D + 2 * D * FF + 8 * D + FF

SHARES = 32
PLANES = 4
IN_PLANE = SHARES // PLANES
HALF = IN_PLANE // 2
STARTS = [index * (ENTRIES // SHARES) // TILE * TILE_ROWS for index in range(SHARES)]
BLOCK = max(
    -(-((index + 1) * (ENTRIES // SHARES)) // TILE) * TILE_ROWS - STARTS[index] for index in range(SHARES)
)
PLANE_END = [STARTS[(plane + 1) * IN_PLANE - 1] + BLOCK for plane in range(PLANES)]
VEC_AT = ROW_VEC - STARTS[-1]

VMEM = pltpu.CompilerParams(vmem_limit_bytes=62 * MB)


def whole(shape, single=True):
    rank = len(shape)
    kwargs = {"pipeline_mode": pl.Buffered(1)} if single else {}
    return pl.BlockSpec(shape, lambda *unused: (0,) * rank, **kwargs)


def share_row(where, plane, spot, other):
    core = 1 - where[3] if other else where[3]
    share = 2 * ((where[1] * 2 + where[2]) ^ spot) + core
    return ((plane * IN_PLANE + share) * (ENTRIES // SHARES)) // TILE * TILE_ROWS


class Piece:
    def __init__(self, array, blocks, other):
        self.array, self.blocks, self.other = array, blocks, other


def place_piece(target, base, where, piece, block_of, lowest):
    def place(index, plane, spot):
        at = share_row(where, plane, spot, piece.other) - base
        rows = pl.ds(pl.multiple_of(at, TILE_ROWS), BLOCK)
        target[rows, :] = target[rows, :] + block_of(index)

    for index, (plane, spot) in enumerate(piece.blocks):
        if not isinstance(plane, tuple):
            if (plane == 0) == lowest:
                place(index, plane, spot)
            continue
        plane = where[plane[0]]
        pl.when((plane == 0) == lowest)(functools.partial(place, index, plane, spot))


UNREAD = pl.BlockSpec(memory_space=pl.ANY)


def call_kernel(body, arguments, through, in_specs, out_specs, out_shape, grid, name, cost, scalars=1, scratch=(), alias=None):
    inputs, outputs, passed = len(arguments), len(out_specs), len(through)
    aliases = {inputs + index: outputs + index for index in range(passed)}
    aliases.update(alias or {})

    def run(*refs):
        at = inputs + passed
        body(*refs[:inputs], *refs[at : at + outputs], *refs[at + outputs + passed :])

    results = pl.pallas_call(
        run,
        name=name,
        grid_spec=pltpu.PrefetchScalarGridSpec(
            num_scalar_prefetch=scalars,
            grid=grid,
            in_specs=list(in_specs) + [UNREAD] * passed,
            out_specs=list(out_specs) + [UNREAD] * passed,
            scratch_shapes=list(scratch),
        ),
        out_shape=list(out_shape) + [jax.ShapeDtypeStruct(array.shape, array.dtype) for array in through],
        input_output_aliases=aliases,
        compiler_params=VMEM,
        cost_estimate=pl.CostEstimate(flops=int(cost[0]), bytes_accessed=int(cost[1]), transcendentals=int(cost[2])),
    )(*arguments, *through)
    return results[:outputs], results[outputs:]


def emit_copies(source, base, plane, where, keep, send, sems, column=0):
    copies = []
    cols = pl.ds(column, source.shape[1])
    for spot in range(HALF):
        for out, other in ((keep[spot], False), (send.at[spot], True)):
            at = pl.multiple_of(share_row(where, plane, spot, other) - base, TILE_ROWS)
            source_rows = source.at[pl.ds(at, BLOCK), :]
            copies.append(pltpu.make_async_copy(source_rows, out.at[:, cols], sems.at[len(copies)]))
    return copies


def start_all(copies):
    for copy in copies:
        copy.start()


def wait_all(copies):
    for copy in copies:
        copy.wait()


COPY_SEMS = pltpu.SemaphoreType.DMA((IN_PLANE,))


def plane_out(width):
    return [jax.ShapeDtypeStruct((BLOCK, width), BF16)] * HALF + [jax.ShapeDtypeStruct((HALF, BLOCK, width), BF16)]


PLANE_SPEC = [UNREAD] * (HALF + 1)


def split_three(values):
    high = values.astype(BF16)
    rest = values - high.astype(F32)
    middle = rest.astype(BF16)
    low = (rest - middle.astype(F32)).astype(BF16)
    return high, middle, low


def pick_lanes(base, lane, first, columns):
    out = base
    for offset, column in enumerate(columns):
        out = jnp.where(lane == first + offset, column, out)
    return out


def pipeline(units, lag, *stages):
    held, results = {}, {}
    last = len(stages) - 1
    for turn in range(len(units) + last * lag):
        for stage in (0, *range(last, 0, -1)):
            unit = turn - stage * lag
            if 0 <= unit < len(units):
                value = stages[stage](units[unit], *(held.pop(unit) if stage else ()))
                if stage < last:
                    held[unit] = value
                else:
                    results[units[unit]] = value
    return results


def attend_columns(is_long, query, key, value, attended, extra):
    strips = LONG // STRIP
    key_ids = lax.broadcasted_iota(jnp.int32, (STRIP, STRIP), 0)
    query_ids = lax.broadcasted_iota(jnp.int32, (STRIP, STRIP), 1)
    causal = query_ids >= key_ids
    cut = jnp.where(is_long, 0.0, far_below)
    late = jnp.where(is_long, 0.0, 1.0)
    lane = lax.broadcasted_iota(jnp.int32, (LONG, PAIR), 1)
    ones = jnp.ones((TILE_ROWS, LONG), BF16)
    q_heads, k_pairs, v_heads = [], [], []
    for pair in range(query.shape[1] // PAIR):
        cols = slice(pair * PAIR, (pair + 1) * PAIR)
        rows = query[:, cols]
        zero = jnp.zeros_like(rows)
        q_heads += [jnp.where(lane < HD, rows, zero), jnp.where(lane >= HD, rows, zero)]
        k_pairs.append(key[:, cols])
        turned = value[:, cols].astype(F32).T.astype(BF16)
        v_heads += [jnp.concatenate([turned[:HD], ones], 0), jnp.concatenate([turned[HD:], ones], 0)]

    def scores_of(unit):
        strip, head = unit
        lo, reach = strip * STRIP, (strip + 1) * STRIP
        return (dot_nt(k_pairs[head // 2][:reach], q_heads[head][lo:reach]),)

    def soften(unit, scores):
        strip, unused = unit
        lo = strip * STRIP
        parts = []
        if lo >= SHORT:
            parts.append(scores[:SHORT] + cut)
            if lo > SHORT:
                parts.append(scores[SHORT:lo])
        elif strip:
            parts.append(scores[:lo])
        parts.append(jnp.where(causal, scores[lo:], far_below))
        scores = jnp.concatenate(parts, 0)
        largest = jnp.max(scores, 0, keepdims=True)
        return jnp.exp(scores - largest).astype(BF16), largest

    def finish(unit, shifted, largest):
        strip, head = unit
        out = dot_nn(v_heads[head][:, : (strip + 1) * STRIP], shifted)
        sum_exp = out[HD : HD + 1]
        return out[:HD] * (1.0 / sum_exp), largest + jnp.log(sum_exp)

    units = [(strip, head) for strip in range(strips) for head in range(len(q_heads))]
    results = pipeline(units, 2, scores_of, soften, finish)
    for strip in range(strips):
        rows = slice(strip * STRIP, (strip + 1) * STRIP)
        for pair in range(len(k_pairs)):
            cols = slice(pair * PAIR, (pair + 1) * PAIR)
            two = [results[(strip, 2 * pair + side)] for side in range(2)]
            attended[rows, cols] = jnp.concatenate([out for out, unused in two], 0).T.astype(BF16)
            lines = [part.astype(F32) for unused, logsum in two for part in split_three(-logsum)]
            lines.append(jnp.broadcast_to(late if strip * STRIP >= SHORT else 0.0, (1, STRIP)))
            lines.append(jnp.zeros((PAIR - 7, STRIP), F32))
            extra[rows, cols] = jnp.concatenate(lines, 0).T.astype(BF16)


def block_columns(source, index):
    return source[index, :BLOCK, :GROUP]


def forward_body(first, pieces, longs, where, rows_in, *rest):
    sources, rest = rest[: len(pieces)], rest[len(pieces) :]
    if first:
        query, key, value, attended, extra, w_three, w_out, hidden, vec, weights = rest
    else:
        query, key, value, attended, extra, w_three, w_out, weights = rest
    sub = pl.program_id(0)

    @pl.when(sub == 0)
    def _():
        weights[...] = jnp.zeros_like(weights)
        for piece, source in zip(pieces, sources):
            place_piece(weights, 0, where, piece, functools.partial(block_columns, source), True)
        w_three[...] = weights[:ROW_OUT, :]
        w_out[...] = weights[ROW_OUT:, :]
        if first:
            total = jnp.zeros((VEC_ROWS, D), BF16)
            for source in sources:
                if source.shape[1] > BLOCK:
                    for index in range(source.shape[0]):
                        total = total + source[index, BLOCK:, :]
            vec[...] = total

    if first:
        normed, unused = layer_stats(rows_in[...].astype(F32))
        lines = vec[...].astype(F32)
        hid = (normed * lines[0:1] + lines[1:2]).astype(BF16)
        hidden[...] = hid
    else:
        hid = rows_in[...]
    q_rows = (dot_nn(hid, weights[ROW_QUERY : ROW_QUERY + D, :]) * (1.0 / math.sqrt(HD))).astype(BF16)
    k_rows = dot_nn(hid, weights[ROW_KEY : ROW_KEY + D, :]).astype(BF16)
    v_rows = dot_nn(hid, weights[ROW_VALUE : ROW_VALUE + D, :]).astype(BF16)
    query[...] = q_rows
    key[...] = k_rows
    value[...] = v_rows
    attend_columns(longs[sub] > 0, q_rows, k_rows, v_rows, attended, extra)


def forward_group(group, longs, where, rows_in, pieces, through):
    first = group == 0
    total = rows_in.shape[0]
    rows = pl.BlockSpec((LONG, D), lambda s, *refs: (s, 0))
    part = pl.BlockSpec((LONG, GROUP), lambda s, *refs: (s, 0))
    width = D if first else GROUP
    blocks = [
        pl.BlockSpec(piece.array.shape[:2] + (width,), lambda s, *refs: (0, 0, group), pipeline_mode=pl.Buffered(1))
        for piece in pieces
    ]
    tail = PLANE_END[0] - ROW_OUT
    out_specs = [part] * 5 + [whole((ROW_OUT, GROUP)), whole((tail, GROUP))]
    out_shape = [jax.ShapeDtypeStruct((total, GROUP), BF16)] * 5 + [
        jax.ShapeDtypeStruct((ROW_OUT, GROUP), BF16),
        jax.ShapeDtypeStruct((tail, GROUP), BF16),
    ]
    if first:
        out_specs += [rows, whole((VEC_ROWS, D))]
        out_shape += [jax.ShapeDtypeStruct((total, D), BF16), jax.ShapeDtypeStruct((VEC_ROWS, D), BF16)]
    return call_kernel(
        functools.partial(forward_body, first, pieces),
        [longs, where, rows_in, *[piece.array for piece in pieces]],
        through,
        [rows] + blocks,
        out_specs,
        out_shape,
        (total // LONG,),
        "forward_group",
        (8e9, 12e6, 4e6) if first else (0, 0, 0),
        scalars=2,
        scratch=[pltpu.VMEM((PLANE_END[0], GROUP), BF16)],
    )


def attend_back_rows(query, key, value, extra, attended, grad, grad_query, grad_key, grad_value):
    strips = LONG // STRIP
    lane = lax.broadcasted_iota(jnp.int32, (LONG, PAIR), 1)
    row = lax.broadcasted_iota(jnp.int32, (LONG, PAIR), 0)
    row_ids = lax.broadcasted_iota(jnp.int32, (STRIP, STRIP), 0)
    col_ids = lax.broadcasted_iota(jnp.int32, (STRIP, STRIP), 1)
    causal = row_ids >= col_ids
    early = jnp.where((lane == 6) & (row < SHORT), far_below, 0.0)
    v_tail = jnp.where(lane < 3, 1.0, 0.0).astype(BF16)
    heads, pairs = [], query.shape[1] // PAIR
    for pair in range(pairs):
        cols = slice(pair * PAIR, (pair + 1) * PAIR)
        q_all, k_all, v_all, g_all, x_all = (ref[:, cols] for ref in (query, key, value, grad, extra))
        product = g_all.astype(F32) * attended[:, cols].astype(F32)
        zero = jnp.zeros_like(q_all)
        v_wide = jnp.concatenate([v_all, v_tail], 1)
        q_turned = q_all.astype(F32).T.astype(BF16)
        g_turned = g_all.astype(F32).T.astype(BF16)
        for side in range(2):
            mine = (lane < HD) if side == 0 else (lane >= HD)
            own = slice(side * HD, (side + 1) * HD)
            delta = jnp.sum(jnp.where(mine, product, 0.0), -1, keepdims=True)
            d_tail = pick_lanes(
                jnp.zeros((LONG, PAIR), F32), lane, 0, [part.astype(F32) for part in split_three(-delta)]
            )
            ones = jnp.where((lane >= 3 * side) & (lane < 3 * side + 3), 1.0, early).astype(BF16)
            heads.append(
                (
                    jnp.where(mine, k_all, zero),
                    q_turned[own],
                    g_turned[own],
                    jnp.concatenate([jnp.where(mine, q_all, zero), x_all], 1),
                    jnp.concatenate([jnp.where(mine, g_all, zero), d_tail.astype(BF16)], 1),
                    jnp.concatenate([k_all, ones], 1),
                    v_wide,
                )
            )

    def products(unit):
        strip, head = unit
        lo, hi = strip * STRIP, (strip + 1) * STRIP
        unused, unused, unused, q_wide, g_wide, k_wide, v_wide = heads[head]
        return dot_nt(q_wide[lo:hi], k_wide[:hi]), dot_nt(g_wide[lo:hi], v_wide[:hi])

    def soften(unit, scores, slope):
        lo = unit[0] * STRIP
        soft = jnp.exp(scores)
        last = jnp.where(causal, soft[:, lo:], 0.0)
        soft = jnp.concatenate([soft[:, :lo], last], 1) if lo else last
        return soft.astype(BF16), (soft * slope).astype(BF16)

    key_sum, value_sum = {}, {}

    def gradients(unit, soft, scores):
        strip, head = unit
        lo, hi = strip * STRIP, (strip + 1) * STRIP
        k_head, q_turned, g_turned, *unused = heads[head]
        value_part = dot_nn(g_turned[:, lo:hi], soft)
        key_part = dot_nn(q_turned[:, lo:hi], scores)
        for block in range(strip + 1):
            cols, at = slice(block * STRIP, (block + 1) * STRIP), (block, head)
            for total, part in ((value_sum, value_part), (key_sum, key_part)):
                total[at] = total[at] + part[:, cols] if at in total else part[:, cols]
        return dot_nn(scores, k_head[:hi])

    units = [(strip, head) for strip in range(strips) for head in range(len(heads))]
    results = pipeline(units, 1, products, soften, gradients)
    for block in range(strips):
        rows = slice(block * STRIP, (block + 1) * STRIP)
        for pair in range(pairs):
            cols = slice(pair * PAIR, (pair + 1) * PAIR)
            ends = [(block, 2 * pair), (block, 2 * pair + 1)]
            two = results[ends[0]] + results[ends[1]]
            grad_query[rows, cols] = (two * (1.0 / math.sqrt(HD))).astype(BF16)
            grad_key[rows, cols] = jnp.concatenate([key_sum[at] for at in ends], 0).T.astype(BF16)
            grad_value[rows, cols] = jnp.concatenate([value_sum[at] for at in ends], 0).T.astype(BF16)


def backward_body(steps, where, query, key, value, extra, attended, grad, hidden, late, *refs):
    (grad_query, grad_key, grad_value), keep = refs[:3], refs[3 : 3 + HALF]
    send, total, rows, sems = refs[3 + HALF :]
    step = pl.program_id(0)
    attend_back_rows(query, key, value, extra, attended, grad, grad_query, grad_key, grad_value)
    three = jnp.concatenate([grad_query[...], grad_key[...], grad_value[...]], 1)
    now = dot_tn(hidden[...], three)

    @pl.when(step == 0)
    def _():
        total[...] = now

    @pl.when(step > 0)
    def _():
        total[...] = total[...] + now

    @pl.when(step == steps - 1)
    def _():
        for part, at in enumerate((ROW_QUERY, ROW_KEY, ROW_VALUE)):
            rows[at : at + D, :] = total[:, part * GROUP : (part + 1) * GROUP].astype(BF16)
        rows[ROW_OUT:, :] = late[...]
        copies = emit_copies(rows, 0, 0, where, keep, send, sems)
        start_all(copies)
        wait_all(copies)


def backward_group(group, where, query, key, value, extra, attended, grad, hidden, late, through):
    total = query.shape[0]
    steps = total // LONG
    part = pl.BlockSpec((LONG, GROUP), lambda s, *refs: (s, 0))
    return call_kernel(
        functools.partial(backward_body, steps),
        [where, query, key, value, extra, attended, grad, hidden, late],
        through,
        [part] * 5
        + [
            pl.BlockSpec((LONG, GROUP), lambda s, *refs: (s, group)),
            pl.BlockSpec((LONG, D), lambda s, *refs: (s, 0)),
            pl.BlockSpec((late.shape[0], GROUP), lambda s, *refs: (0, group), pipeline_mode=pl.Buffered(1)),
        ],
        [part] * 3 + PLANE_SPEC,
        [jax.ShapeDtypeStruct((total, GROUP), BF16)] * 3 + plane_out(GROUP),
        (steps,),
        "backward_group",
        (14e9, 16e6, 4e6),
        scratch=[
            pltpu.VMEM((D, 3 * GROUP), F32),
            pltpu.VMEM((ROW_OUT + late.shape[0], GROUP), BF16),
            COPY_SEMS,
        ],
    )


MID_ROWS = 512
HALF_ROWS = 256
STAGE_ROWS = 256
STAGE = 8
CHUNKS = FF // D
TANH_SCALE = math.sqrt(2.0 / math.pi)


def spread_matrix(size):
    quarter = size // CHUNKS
    to = lax.broadcasted_iota(jnp.int32, (size, size), 0)
    source = lax.broadcasted_iota(jnp.int32, (size, size), 1)
    return (source == CHUNKS * (to % quarter) + to // quarter).astype(BF16)


def interleave(parts):
    started, live = 0, []
    while started < len(parts) or live:
        if started < len(parts):
            live.append(parts[started])
            started += 1
        live = [part for part in live if next(part, True) is None]


def middle_body(steps, pieces, where, tok, grad_out, hidden_a, *refs):
    att_refs, wo_refs, refs = refs[:GROUPS], refs[GROUPS : 2 * GROUPS], refs[2 * GROUPS :]
    sources, refs = refs[: len(pieces)], refs[len(pieces) :]
    (outputs, grad_middle_ref, grad_za_ref, grad_attended, hid_f_ref, grad_zf_ref, grad_a_ref, gate_copy) = refs[:8]
    keep, send = refs[8 : 8 + HALF], refs[8 + HALF]
    carry, weights, wide, slope, s_vec, kept, s_hid_f, s_grad_f = refs[9 + HALF : -3]
    load_sems, sems_three, sems_two = refs[-3:]
    step = pl.program_id(0)
    base = ROW_OUT

    @pl.when(step == 0)
    def _():
        staged = []
        for piece, source in zip(pieces, sources):
            for index in range(len(piece.blocks)):
                slot = len(staged)
                to = kept.at[slot // STAGE, pl.ds(slot % STAGE * STAGE_ROWS, BLOCK), :]
                staged.append((to, pltpu.make_async_copy(source.at[index, pl.ds(0, BLOCK), :], to, load_sems.at[slot])))
                staged[-1][1].start()
        weights[...] = jnp.zeros_like(weights)
        for group in range(GROUPS):
            weights[: PLANE_END[0] - ROW_OUT, group * GROUP : (group + 1) * GROUP] = wo_refs[group][...]
        at_slot = 0
        for piece in pieces:
            count = len(piece.blocks)
            here = staged[at_slot : at_slot + count]
            wait_all([copy for unused, copy in here])
            place_piece(weights, base, where, piece, lambda index, here=here: here[index][0][...], False)
            at_slot += count
        shuffle = spread_matrix(256)
        for block in range(FF // 256):
            at = ROW_IN - base + block * 256
            part = dot_nn(shuffle, weights[at : at + 256, :]).astype(BF16)
            for chunk in range(CHUNKS):
                wide[chunk, block * 64 : (block + 1) * 64, :] = part[chunk * 64 : (chunk + 1) * 64]
        gate_copy[...] = weights[ROW_GATE_A - base : ROW_GATE_A - base + D, :]
        s_vec[...] = jnp.zeros_like(s_vec)

    w_out = weights.at[ROW_OUT - base : ROW_OUT - base + D]
    gate_attn = weights.at[ROW_GATE_A - base : ROW_GATE_A - base + D]
    gate_ffn = weights.at[ROW_GATE_F - base : ROW_GATE_F - base + D]
    w_down = weights.at[ROW_DOWN - base : ROW_DOWN - base + FF]
    vecs = weights[ROW_VEC - base : ROW_VEC - base + VEC_ROWS, :].astype(F32)
    chunks = [slice(chunk * D, (chunk + 1) * D) for chunk in range(CHUNKS)]

    first_row = pl.multiple_of(step * MID_ROWS, MID_ROWS)

    def part(at):
        here = slice(at, at + HALF_ROWS)
        there = pl.ds(first_row + at, HALF_ROWS)
        hid_a = hidden_a[here, :]
        att = jnp.concatenate([ref[here, :] for ref in att_refs], 1)
        grad = grad_out[here, :].astype(F32)
        branch_a = dot_nn(att, w_out[...])
        gate_a = dot_nn(hid_a, gate_attn[...])
        yield
        branch_a = branch_a + vecs[2:3]
        gate_a = sigmoid(gate_a + vecs[3:4])
        middle = tok[here, :].astype(F32) + gate_a * branch_a
        normed, inv_std = layer_stats(middle)
        hid_f = (normed * vecs[4:5] + vecs[5:6]).astype(BF16)
        hid_f_ref[here, :] = hid_f
        s_hid_f[there, :] = hid_f
        yield
        gate_f = dot_nn(hid_f, gate_ffn[...])
        pre = dot_nn(hid_f, wide[0])
        yield
        branch_f = vecs[6:7]
        for chunk, cols in enumerate(chunks):
            pre = pre + vecs[8 + chunk : 9 + chunk]
            square = pre * pre
            bend = jnp.tanh(pre * (TANH_SCALE + (TANH_SCALE * 0.044715) * square))
            half = 0.5 * (1.0 + bend)
            active = (pre * half).astype(BF16)
            slope[here, cols] = half + (0.5 * pre) * (1.0 - bend * bend) * (
                TANH_SCALE + (3.0 * 0.044715 * TANH_SCALE) * square
            )
            kept[chunk, there, :] = active
            yield
            if chunk + 1 < CHUNKS:
                pre = dot_nn(hid_f, wide[chunk + 1])
            branch_f = branch_f + dot_nn(active, w_down[cols, :])
            yield
        gate_f = sigmoid(gate_f + vecs[7:8])
        outputs[here, :] = (middle + gate_f * branch_f).astype(BF16)
        grad_branch_f = (grad * gate_f).astype(BF16)
        grad_zf = (grad * branch_f * gate_f * (1.0 - gate_f)).astype(BF16)
        s_grad_f[there, :] = grad_branch_f
        grad_zf_ref[here, :] = grad_zf
        s_vec[6] += fold_rows(grad_branch_f.astype(F32))
        s_vec[7] += fold_rows(grad_zf.astype(F32))
        yield
        grad_hidden = dot_nt(grad_zf, gate_ffn[...])
        grad_active = dot_nt(grad_branch_f, w_down[chunks[0], :])
        yield
        for chunk, cols in enumerate(chunks):
            grad_pre = (grad_active * slope[here, cols]).astype(BF16)
            kept[CHUNKS + chunk, there, :] = grad_pre
            s_vec[8 + chunk] += fold_rows(grad_pre.astype(F32))
            yield
            if chunk + 1 < CHUNKS:
                grad_active = dot_nt(grad_branch_f, w_down[chunks[chunk + 1], :])
            grad_hidden = grad_hidden + dot_nt(grad_pre, wide[chunk])
            yield
        s_vec[4] += fold_rows(grad_hidden * normed)
        s_vec[5] += fold_rows(grad_hidden)
        grad_middle = grad + norm_back(grad_hidden * vecs[4:5], normed, inv_std)
        grad_middle_ref[here, :] = grad_middle
        grad_branch_a = (grad_middle * gate_a).astype(BF16)
        grad_za = (grad_middle * branch_a * gate_a * (1.0 - gate_a)).astype(BF16)
        grad_za_ref[here, :] = grad_za
        grad_a_ref[here, :] = grad_branch_a
        s_vec[2] += fold_rows(grad_branch_a.astype(F32))
        s_vec[3] += fold_rows(grad_za.astype(F32))
        yield
        grad_attended[here, :] = dot_nt(grad_branch_a, w_out[...]).astype(BF16)
        yield

    interleave([part(at) for at in range(0, MID_ROWS, HALF_ROWS)])

    @pl.when(step == steps - 1)
    def _():
        for chunk in range(CHUNKS):
            at = ROW_DOWN - base + chunk * D
            weights[at : at + D, :] = dot_tn(kept[chunk], s_grad_f[...]).astype(BF16)
        weights[ROW_VEC - base :, :] = jnp.sum(s_vec[...], 1).astype(BF16)
        copies = emit_copies(weights, base, 3, where, keep, send, sems_three, D)
        start_all(copies)
        for chunk in range(CHUNKS):
            wide[chunk] = dot_tn(s_hid_f[...], kept[CHUNKS + chunk]).astype(BF16)
        shuffle = spread_matrix(256)
        for block in range(FF // 256):
            parts = [wide[chunk, block * 64 : (block + 1) * 64, :] for chunk in range(CHUNKS)]
            at = ROW_IN - base + block * 256
            weights[at : at + 256, :] = dot_tn(shuffle, jnp.concatenate(parts, 0)).astype(BF16)
        last = emit_copies(weights, base, 2, where, keep, send, sems_two)
        start_all(last)
        carry[...] = weights[ROW_IN - base : PLANE_END[1] - base, :]
        wait_all(copies)
        wait_all(last)


def middle_part(where, tokens, grad_out, hidden_a, attended, w_outs, pieces):
    total = tokens.shape[0]
    steps = total // MID_ROWS
    carry = PLANE_END[1] - ROW_IN
    rows_at = lambda width: pl.BlockSpec((MID_ROWS, width), lambda i, *refs: (i, 0))
    shape = lambda kind=BF16: jax.ShapeDtypeStruct((total, D), kind)
    results, unused = call_kernel(
        functools.partial(middle_body, steps, pieces),
        [where, tokens, grad_out, hidden_a, *attended, *w_outs, *[piece.array for piece in pieces]],
        [],
        [rows_at(D)] * 3
        + [rows_at(GROUP)] * GROUPS
        + [whole(w_outs[0].shape)] * GROUPS
        + [UNREAD] * len(pieces),
        [rows_at(D)] * 7 + [whole((D, D))] + PLANE_SPEC + [whole((carry, D))],
        [shape(), shape(F32)]
        + [shape()] * 5
        + [jax.ShapeDtypeStruct((D, D), BF16)]
        + plane_out(2 * D)
        + [jax.ShapeDtypeStruct((carry, D), BF16)],
        (steps,),
        "middle_part",
        (33e9, 50e6, 4e6),
        scratch=[
            pltpu.VMEM((ALL_ROWS - ROW_OUT, D), BF16),
            pltpu.VMEM((CHUNKS, D, D), BF16),
            pltpu.VMEM((MID_ROWS, FF), F32),
            pltpu.VMEM((VEC_ROWS, 8, D), F32),
            pltpu.VMEM((2 * CHUNKS, total, D), BF16),
            pltpu.VMEM((total, D), BF16),
            pltpu.VMEM((total, D), BF16),
            pltpu.SemaphoreType.DMA((SHARES,)),
            COPY_SEMS,
            COPY_SEMS,
        ],
    )
    return results


def gates_body(where, *refs):
    att_refs, refs = refs[:GROUPS], refs[GROUPS:]
    hidden_a, hidden_f, grad_a, grad_za, grad_zf, late, *refs = refs
    keep, send, carry, sides, rows, load_sems, sems = refs[:HALF], *refs[HALF:]
    loads = []

    def load(source, to):
        loads.append(pltpu.make_async_copy(source, to, load_sems.at[len(loads)]))
        loads[-1].start()

    for group, ref in enumerate(att_refs):
        load(ref, sides.at[0, :, pl.ds(group * GROUP, GROUP)])
    for slot, ref in enumerate((grad_a, hidden_a, grad_za, hidden_f, grad_zf)):
        load(ref, sides.at[1 + slot])
    rows[3 * D :, :] = late[...]
    for at in range(3):
        wait_all(loads[: GROUPS + 1] if at == 0 else loads[GROUPS + 2 * at - 1 : GROUPS + 2 * at + 1])
        rows[at * D : (at + 1) * D, :] = dot_tn(sides[2 * at], sides[2 * at + 1]).astype(BF16)
    copies = emit_copies(rows, ROW_OUT, 1, where, keep, send, sems)
    start_all(copies)
    carry[...] = rows[: PLANE_END[0] - ROW_OUT, :]
    wait_all(copies)


def gates_gradient(where, attended, hidden_a, hidden_f, grad_a, grad_za, grad_zf, late, through):
    total = hidden_a.shape[0]
    carry = PLANE_END[0] - ROW_OUT
    return call_kernel(
        gates_body,
        [where, *attended, hidden_a, hidden_f, grad_a, grad_za, grad_zf, late],
        through,
        [UNREAD] * (GROUPS + 5) + [whole(late.shape)],
        PLANE_SPEC + [whole((carry, D))],
        plane_out(D) + [jax.ShapeDtypeStruct((carry, D), BF16)],
        (1,),
        "gates_gradient",
        (3.2e9, 14e6, 0),
        scratch=[
            pltpu.VMEM((6, total, D), BF16),
            pltpu.VMEM((3 * D + late.shape[0], D), BF16),
            pltpu.SemaphoreType.DMA((GROUPS + 5,)),
            COPY_SEMS,
        ],
    )


LAST_ROWS = 512


def last_body(steps, tok, grad_middle, grad_za, *refs):
    grads, refs = refs[: 3 * GROUPS], refs[3 * GROUPS :]
    w_three, refs = refs[:GROUPS], refs[GROUPS:]
    gate_attn, vec, input_grad, d_vec, factors, s_vec = refs
    step = pl.program_id(0)

    @pl.when(step == 0)
    def _():
        s_vec[...] = jnp.zeros_like(s_vec)
        for group in range(GROUPS):
            factors[:, group * GROUP : (group + 1) * GROUP] = w_three[group][...]

    vecs = vec[...].astype(F32)

    def part(at):
        here = slice(at, at + HALF_ROWS)
        grad_hidden = dot_nt(grad_za[here, :], gate_attn[...])
        for side, row in enumerate((ROW_QUERY, ROW_KEY, ROW_VALUE)):
            grad = jnp.concatenate([grads[3 * group + side][here, :] for group in range(GROUPS)], 1)
            grad_hidden += dot_nt(grad, factors[row : row + D, :])
        yield
        normed, inv_std = layer_stats(tok[here, :].astype(F32))
        s_vec[0] += fold_rows(grad_hidden * normed)
        s_vec[1] += fold_rows(grad_hidden)
        back = norm_back(grad_hidden * vecs[0:1], normed, inv_std)
        input_grad[here, :] = (grad_middle[here, :] + back).astype(BF16)
        yield

    interleave([part(at) for at in range(0, LAST_ROWS, HALF_ROWS)])

    @pl.when(step == steps - 1)
    def _():
        d_vec[...] = jnp.sum(s_vec[...], 1)


def last_part(tokens, grad_middle, grad_za, grads, w_three, gate_attn, vec, through):
    total = tokens.shape[0]
    steps = total // LAST_ROWS
    rows_at = lambda width: pl.BlockSpec((LAST_ROWS, width), lambda i, *refs: (i, 0))
    return call_kernel(
        functools.partial(last_body, steps),
        [tokens, grad_middle, grad_za, *grads, *w_three, gate_attn, vec],
        through,
        [rows_at(D)] * 3
        + [rows_at(GROUP)] * (3 * GROUPS)
        + [whole((ROW_OUT, GROUP))] * GROUPS
        + [whole((D, D)), whole((VEC_ROWS, D))],
        [rows_at(D), whole((VEC_ROWS, D))],
        [jax.ShapeDtypeStruct((total, D), BF16), jax.ShapeDtypeStruct((VEC_ROWS, D), F32)],
        (steps,),
        "last_part",
        (4.3e9, 20e6, 0),
        scalars=0,
        scratch=[pltpu.VMEM((ROW_OUT, D), BF16), pltpu.VMEM((VEC_ROWS, 8, D), F32)],
    )


def local_part(where, longs, tokens, out_grad, first_pieces, middle_pieces, before, later, collect):
    subs, length, unused = tokens.shape
    rows = tokens.reshape(subs * length, D)
    grads_in = out_grad.reshape(subs * length, D)
    (*kept, hidden_a, vec), passed = forward_group(0, longs, where, rows, first_pieces, before("forward0"))
    later("forward0", passed)
    second, passed = forward_group(1, longs, where, hidden_a, first_pieces, before("forward1"))
    later("forward1", passed)
    groups = [kept, second]
    attended = [group[3] for group in groups]
    (outputs, grad_middle, grad_za, grad_attended, hidden_f, grad_zf, grad_a, gate_attn, *plane, carry) = (
        middle_part(where, rows, grads_in, hidden_a, attended, [group[6] for group in groups], middle_pieces())
    )
    collect("upper", plane)
    (*plane, carry), passed = gates_gradient(
        where, attended, hidden_a, hidden_f, grad_a, grad_za, grad_zf, carry, before("gates")
    )
    later("gates", passed)
    collect(1, plane)
    grads = []
    for group, (query, key, value, att, extra, *unused_two) in enumerate(groups):
        results, passed = backward_group(
            group, where, query, key, value, extra, att, grad_attended, hidden_a, carry, before(f"back{group}")
        )
        later(f"back{group}", passed)
        grads += results[:3]
        collect(("first", group), results[3:])
    w_three = [group[5] for group in groups]
    (input_grad, d_vec), passed = last_part(
        rows, grad_middle, grad_za, grads, w_three, gate_attn, vec, before("last")
    )
    later("last", passed)
    return outputs.reshape(tokens.shape), input_grad.reshape(tokens.shape), d_vec


def own_block(params, start, rows):
    share = params.shape[0]
    room = jnp.pad(params, (TILE, rows * D - share))
    return lax.dynamic_slice(room, (TILE - start % TILE,), (rows * D,)).reshape(rows, D).astype(BF16)


def move(axis, count, step):
    perm = [(i, step(i)) for i in range(count) if step(i) is not None]
    return lambda value: lax.ppermute(value, axis, perm)


def on_slice(tokens, out_grad, long_count, params):
    z, x, y, c = (lax.axis_index(axis) for axis in ("z", "x", "y", "c"))
    me = ((z * 2 + x) * 2 + y) * 2 + c
    share = params.shape[0]
    block = own_block(params, me * share, BLOCK)
    odd = z % 2 == 1
    ends = (z == 0) | (z == 3)
    swap_c = move("c", 2, lambda i: 1 - i)
    swap_x = move("x", 2, lambda i: 1 - i)
    swap_y = move("y", 2, lambda i: 1 - i)
    swap_xy = move(("x", "y"), 4, lambda i: 3 - i)
    z_one = move("z", 4, lambda i: i ^ 1)
    z_two = move("z", 4, lambda i: i ^ 2)
    inside = z < 4
    vec = block[VEC_AT : VEC_AT + VEC_ROWS]
    mine = jnp.concatenate([block, jnp.where(me == SHARES - 1, vec, jnp.zeros_like(vec))], 0)
    step_one = move("z", 4, {0: 2, 1: 0, 2: 3, 3: 1}.get)(mine)
    held = jnp.where(ends, mine, step_one)
    step_two = z_one(held)
    step_three = z_two(jnp.where(ends, step_one[:BLOCK], block))
    vec = jnp.where(odd, held, step_two)[BLOCK:]
    first = jnp.where(inside, jnp.where(z == 2, step_one, step_two)[:BLOCK], step_three)
    first = jnp.concatenate([first, vec], 0)[None]
    both = jnp.stack([jnp.where(z == 2, step_two, step_one)[:BLOCK], step_three])

    def in_plane(parts, planes):
        near = jnp.concatenate(parts, 0)
        blocks = [(plane, spot) for spot in range(HALF) for plane in planes]
        return [Piece(near, blocks, False), Piece(swap_c(near), blocks, True)]

    own = block[None]
    pieces = in_plane([own, swap_y(own), swap_x(own), swap_xy(own)], ((0,),))
    pieces += in_plane([first, swap_y(first), swap_x(first), swap_xy(first)], ((4,),))
    around = {"both": [swap_y(both), swap_x(both), swap_xy(both)]}
    top = {"both": both[:, :TILE_ROWS]}
    pair = ((5,), (6,))
    blocks = [(plane, 0) for plane in pair]
    both_pieces = [Piece(both, blocks, False), Piece(swap_c(both), blocks, True)]

    def middle_pieces():
        late = jnp.pad(top["both"], ((0, 0), (0, BLOCK - TILE_ROWS), (0, 0)))
        parts = around["both"]
        near = jnp.concatenate([jnp.where(inside, parts[0], late), *parts[1:]], 0)
        blocks = [(plane, spot) for spot in range(1, HALF) for plane in pair]
        return pieces + both_pieces + [Piece(near, blocks, False), Piece(swap_c(near), blocks, True)]

    early, late = ("first", 0), ("first", 1)
    arrived, at_chip, held = {}, {}, {}
    z_up = move("z", 4, lambda i: {0: 2, 1: 3}.get(i))
    z_down = move("z", 4, lambda i: {2: 0, 3: 1}.get(i))

    def collect(plane, blocks):
        arrived[plane] = [list(blocks[:HALF]), swap_c(blocks[HALF])]

    def send_around(name, planes, first=None):
        part = []
        for spot in range(HALF):
            sums = [arrived[plane][0][spot].astype(F32) + arrived[plane][1][spot].astype(F32) for plane in planes]
            sums = jnp.concatenate(sums, 1)
            if first is not None:
                sums = jnp.where(inside, sums, first[:, : sums.shape[1]])
            part.append(sums.astype(BF16))
        at_chip[name] = part[0]
        around[name] = (swap_y(part[1]), swap_x(part[2]), swap_xy(part[3]))

    def plane_sum(name):
        total = at_chip[name].astype(F32)
        for got in around[name]:
            total = total + got.astype(F32)
        return total

    def before(name):
        if name == "forward0":
            return []
        if name == "forward1":
            return [top["both"]]
        if name == "gates":
            return arrived["upper"][0]
        if name == "back0":
            send_around("upper", ("upper",))
            return [at_chip["upper"]]
        if name == "back1":
            held["upper"] = plane_sum("upper")
            held["up"] = z_up(held["upper"].astype(BF16))
            send_around("lower", (1, early), held["upper"])
            return [held["upper"], at_chip["lower"]]
        if name == "last":
            held["lower"] = plane_sum("lower")
            held["down"] = z_down(held["lower"].astype(BF16))
            send_around("late", (late,), held["lower"])
            upper = held["upper"] + held["up"].astype(F32)
            two, three, last = upper[:, :D], upper[:, D:], held["lower"][:, :D]
            held["give"] = jnp.where(inside, jnp.where(z == 2, three, two), last).astype(BF16)
            held["mine"] = jnp.where(inside, jnp.where(z == 2, two, three), last)
            return [held["give"], held["mine"], held["lower"], at_chip["late"]]
        return []

    def later(name, passed):
        if name == "forward1":
            top["both"] = passed[0]
        if name == "gates":
            arrived["upper"][0] = passed
        if name == "back0":
            at_chip["upper"] = passed[0]
        if name == "back1":
            held["upper"], at_chip["lower"] = passed
        if name == "last":
            held["give"], held["mine"], held["lower"], at_chip["late"] = passed

    planes = [jnp.where(z == 0, 3, 0), jnp.where(z == 0, 1, jnp.where(z == 3, 2, 3)), jnp.where(z < 2, 2, 1)]
    where = jnp.stack([z, x, y, c, *planes]).astype(jnp.int32)
    outputs, input_grad, d_vec = local_part(
        where,
        long_count.reshape(-1),
        tokens,
        out_grad,
        pieces,
        middle_pieces,
        before,
        later,
        collect,
    )
    low = plane_sum("late")
    lower = jnp.where(inside, held["lower"], jnp.concatenate([low] * 3, 1)) + held["down"].astype(F32)
    one, zero = lower[:, :D], jnp.concatenate([lower[:, D:]] * 2, 1)
    give = jnp.where(z == 0, one.astype(BF16), jnp.where(z == 1, zero.astype(BF16), held["give"]))
    given = z_one(give).astype(F32)
    total = jnp.where(z == 0, zero, jnp.where(z == 1, one, held["mine"])) + given
    gains = jnp.where(inside, d_vec[:2], jnp.concatenate([low[:2]] * 2, 1))
    gains = gains + swap_c(gains)
    gains = (gains + swap_x(gains) + swap_y(gains) + swap_xy(gains)).reshape(2 * GROUPS, GROUP)
    lines = jnp.pad(gains.astype(BF16), ((0, TILE_ROWS - 2 * GROUPS), (0, 0)))
    message = jnp.concatenate([jnp.where(inside, low, given[:, :GROUP]).astype(BF16), lines], 0)
    for step in ({3: 0, 0: 3}, {2: 0, 1: 3}, {1: 0, 2: 3}):
        got = move("z", 4, step.get)(message).astype(F32)
        low = low + got[:BLOCK]
        gains = gains + got[BLOCK : BLOCK + 2 * GROUPS]
    total = jnp.where(z == 0, jnp.concatenate([total[:, :GROUP], low], 1), total)
    gains = jnp.where(me == SHARES - 1, gains.reshape(2, D), jnp.zeros((2, D), F32))
    total = total + jnp.pad(gains, ((VEC_AT, BLOCK - VEC_AT - 2), (0, 0)))
    param_grad = lax.dynamic_slice(total.reshape(-1), ((me * share) % TILE,), (share,))
    return (outputs, input_grad, param_grad)


def on_any(axes, count, tokens, out_grad, long_count, params):
    share = params.shape[0]
    me = lax.axis_index(axes)
    starts = [index * share // TILE * TILE_ROWS for index in range(count)]
    rows = max(-(-((index + 1) * share) // TILE) * TILE_ROWS - starts[index] for index in range(count))
    gathered = lax.all_gather(own_block(params, me * share, rows), axes, axis=0)
    merged = jnp.zeros((starts[-1] + rows, D), BF16)
    for index in range(count):
        merged = merged.at[starts[index] : starts[index] + rows].add(gathered[index])
    merged = merged[:ALL_ROWS]
    near, far = [], []
    for plane in range(PLANES):
        blocks = []
        for index in range(plane * IN_PLANE, (plane + 1) * IN_PLANE):
            end = STARTS[index + 1] if index + 1 < SHARES else ALL_ROWS
            piece = merged[STARTS[index] : end]
            blocks.append(jnp.pad(piece, ((0, BLOCK - piece.shape[0]), (0, 0))))
        spots = [(plane, spot) for spot in range(HALF)]
        near.append(Piece(jnp.stack(blocks[0::2]), spots, False))
        far.append(Piece(jnp.stack(blocks[1::2]), spots, True))
    vec = merged[ROW_VEC : ROW_VEC + VEC_ROWS]
    first_pieces = []
    for piece in (near[0], far[0]):
        lines = jnp.zeros((HALF, VEC_ROWS, D), BF16)
        if piece is near[0]:
            lines = lines.at[0].set(vec)
        first_pieces.append(Piece(jnp.concatenate([piece.array, lines], 1), piece.blocks, piece.other))
    by_share = [None] * SHARES

    halves = []

    def collect(plane, blocks):
        if isinstance(plane, tuple):
            halves.append(blocks)
            if len(halves) < GROUPS:
                return
            blocks = [jnp.concatenate(parts, parts[0].ndim - 1) for parts in zip(*halves)]
            plane = 0
        places = (2, 3) if plane == "upper" else (plane,)
        for at, plane in enumerate(places):
            cols = slice(at * D, (at + 1) * D)
            for spot in range(HALF):
                by_share[plane * IN_PLANE + 2 * spot] = blocks[spot][:, cols]
                by_share[plane * IN_PLANE + 2 * spot + 1] = blocks[HALF][spot][:, cols]

    outputs, input_grad, d_vec = local_part(
        jnp.zeros((7,), jnp.int32),
        long_count.reshape(-1),
        tokens,
        out_grad,
        first_pieces,
        lambda: near[1:] + far[1:],
        lambda name: [],
        lambda name, passed: None,
        collect,
    )
    ends = STARTS[1:] + [ALL_ROWS]
    gradient = jnp.concatenate([part[: ends[i] - STARTS[i]] for i, part in enumerate(by_share)], 0)
    gradient = gradient.at[ROW_VEC : ROW_VEC + VEC_ROWS].add(d_vec.astype(BF16))
    gradient = jnp.pad(gradient, ((0, max(0, starts[-1] + rows - ALL_ROWS)), (0, 0)))
    spread = jnp.stack([gradient[start : start + rows] for start in starts])
    summed = lax.psum_scatter(spread, axes, scatter_dimension=0)
    param_grad = lax.dynamic_slice(summed.astype(F32).reshape(-1), ((me * share) % TILE,), (share,))
    return (outputs, input_grad, param_grad)


def solution(mesh):
    axes = ("wide", "narrow")
    count = math.prod(mesh.shape[axis] for axis in axes)
    step = functools.partial(on_any, axes, count)
    if mesh.shape["wide"] == 8 and mesh.shape["narrow"] == 4:
        axes = ("z", "x", "y", "c")
        mesh = Mesh(mesh.devices.reshape(4, 2, 2, 2), axes)
        step = on_slice
    return jax.shard_map(
        step,
        mesh=mesh,
        in_specs=(P(None, axes, None), P(None, axes, None), P(None, axes), P(axes)),
        out_specs=(P(None, axes, None), P(None, axes, None), P(axes)),
        check_vma=False,
    )
```

```python
import functools
import math

import jax
import jax.numpy as jnp
from jax import lax
from jax.experimental import pallas as pl
from jax.experimental.pallas import tpu as pltpu
from jax.sharding import Mesh, PartitionSpec as P

D = 512
FF = 2048
HEADS = 8
HD = 64
SHORT = 512
LONG = 1024
PAIR = 2 * HD
GROUP = 2 * PAIR
GROUPS = D // GROUP
STRIP = 256

TILE_ROWS = 16
TILE = TILE_ROWS * D

layer_eps = 1e-05
far_below = -1e30

F32 = jnp.float32
BF16 = jnp.bfloat16
MB = 1024 * 1024


def dot_nn(left, right):
    return lax.dot_general(left, right, (((1,), (0,)), ((), ())), preferred_element_type=F32)


def dot_nt(left, right):
    return lax.dot_general(left, right, (((1,), (1,)), ((), ())), preferred_element_type=F32)


def dot_tn(left, right):
    return lax.dot_general(left, right, (((0,), (0,)), ((), ())), preferred_element_type=F32)


def layer_stats(values):
    average = jnp.mean(values, -1, keepdims=True)
    centred = values - average
    variance = jnp.mean(centred * centred, -1, keepdims=True)
    inv_std = lax.rsqrt(variance + layer_eps)
    return (centred * inv_std, inv_std)


def norm_back(grad_hat, normed, inv_std):
    return inv_std * (
        grad_hat
        - jnp.mean(grad_hat, -1, keepdims=True)
        - normed * jnp.mean(grad_hat * normed, -1, keepdims=True)
    )


def sigmoid(values):
    return 0.5 * jnp.tanh(0.5 * values) + 0.5


def fold_rows(values):
    return jnp.sum(values.reshape(values.shape[0] // 8, 8, values.shape[1]), 0)


ROW_QUERY = 0
ROW_KEY = 512
ROW_VALUE = 1024
ROW_OUT = 1536
ROW_GATE_A = 2048
ROW_GATE_F = 2560
ROW_IN = 3072
ROW_DOWN = 5120
ROW_VEC = 7168
ALL_ROWS = 7184
VEC_ROWS = 16
ENTRIES = 6 * D * D + 2 * D * FF + 8 * D + FF

SHARES = 32
PLANES = 4
IN_PLANE = SHARES // PLANES
HALF = IN_PLANE // 2
STARTS = [index * (ENTRIES // SHARES) // TILE * TILE_ROWS for index in range(SHARES)]
BLOCK = max(
    -(-((index + 1) * (ENTRIES // SHARES)) // TILE) * TILE_ROWS - STARTS[index] for index in range(SHARES)
)
PLANE_END = [STARTS[(plane + 1) * IN_PLANE - 1] + BLOCK for plane in range(PLANES)]
VEC_AT = ROW_VEC - STARTS[-1]

VMEM = pltpu.CompilerParams(vmem_limit_bytes=62 * MB)


def whole(shape, single=True):
    rank = len(shape)
    kwargs = {"pipeline_mode": pl.Buffered(1)} if single else {}
    return pl.BlockSpec(shape, lambda *unused: (0,) * rank, **kwargs)


def share_row(where, plane, spot, other):
    core = 1 - where[3] if other else where[3]
    share = 2 * ((where[1] * 2 + where[2]) ^ spot) + core
    return ((plane * IN_PLANE + share) * (ENTRIES // SHARES)) // TILE * TILE_ROWS


class Piece:
    def __init__(self, array, blocks, other):
        self.array, self.blocks, self.other = array, blocks, other


def place_piece(target, base, where, piece, block_of, lowest):
    def place(index, plane, spot):
        at = share_row(where, plane, spot, piece.other) - base
        rows = pl.ds(pl.multiple_of(at, TILE_ROWS), BLOCK)
        target[rows, :] = target[rows, :] + block_of(index)

    for index, (plane, spot) in enumerate(piece.blocks):
        if not isinstance(plane, tuple):
            if (plane == 0) == lowest:
                place(index, plane, spot)
            continue
        plane = where[plane[0]]
        pl.when((plane == 0) == lowest)(functools.partial(place, index, plane, spot))


UNREAD = pl.BlockSpec(memory_space=pl.ANY)


def call_kernel(body, arguments, through, in_specs, out_specs, out_shape, grid, name, cost, scalars=1, scratch=(), alias=None):
    inputs, outputs, passed = len(arguments), len(out_specs), len(through)
    aliases = {inputs + index: outputs + index for index in range(passed)}
    aliases.update(alias or {})

    def run(*refs):
        at = inputs + passed
        body(*refs[:inputs], *refs[at : at + outputs], *refs[at + outputs + passed :])

    results = pl.pallas_call(
        run,
        name=name,
        grid_spec=pltpu.PrefetchScalarGridSpec(
            num_scalar_prefetch=scalars,
            grid=grid,
            in_specs=list(in_specs) + [UNREAD] * passed,
            out_specs=list(out_specs) + [UNREAD] * passed,
            scratch_shapes=list(scratch),
        ),
        out_shape=list(out_shape) + [jax.ShapeDtypeStruct(array.shape, array.dtype) for array in through],
        input_output_aliases=aliases,
        compiler_params=VMEM,
        cost_estimate=pl.CostEstimate(flops=int(cost[0]), bytes_accessed=int(cost[1]), transcendentals=int(cost[2])),
    )(*arguments, *through)
    return results[:outputs], results[outputs:]


def emit_copies(source, base, plane, where, keep, send, sems, column=0):
    copies = []
    cols = pl.ds(column, source.shape[1])
    for spot in range(HALF):
        for out, other in ((keep[spot], False), (send.at[spot], True)):
            at = pl.multiple_of(share_row(where, plane, spot, other) - base, TILE_ROWS)
            source_rows = source.at[pl.ds(at, BLOCK), :]
            copies.append(pltpu.make_async_copy(source_rows, out.at[:, cols], sems.at[len(copies)]))
    return copies


def start_all(copies):
    for copy in copies:
        copy.start()


def wait_all(copies):
    for copy in copies:
        copy.wait()


COPY_SEMS = pltpu.SemaphoreType.DMA((IN_PLANE,))


def plane_out(width):
    return [jax.ShapeDtypeStruct((BLOCK, width), BF16)] * HALF + [jax.ShapeDtypeStruct((HALF, BLOCK, width), BF16)]


PLANE_SPEC = [UNREAD] * (HALF + 1)


def split_three(values):
    high = values.astype(BF16)
    rest = values - high.astype(F32)
    middle = rest.astype(BF16)
    low = (rest - middle.astype(F32)).astype(BF16)
    return high, middle, low


def pick_lanes(base, lane, first, columns):
    out = base
    for offset, column in enumerate(columns):
        out = jnp.where(lane == first + offset, column, out)
    return out


def pipeline(units, lag, *stages):
    held, results = {}, {}
    last = len(stages) - 1
    for turn in range(len(units) + last * lag):
        for stage in (0, *range(last, 0, -1)):
            unit = turn - stage * lag
            if 0 <= unit < len(units):
                value = stages[stage](units[unit], *(held.pop(unit) if stage else ()))
                if stage < last:
                    held[unit] = value
                else:
                    results[units[unit]] = value
    return results


def attend_columns(is_long, query, key, value, attended, extra):
    strips = LONG // STRIP
    key_ids = lax.broadcasted_iota(jnp.int32, (STRIP, STRIP), 0)
    query_ids = lax.broadcasted_iota(jnp.int32, (STRIP, STRIP), 1)
    causal = query_ids >= key_ids
    cut = jnp.where(is_long, 0.0, far_below)
    late = jnp.where(is_long, 0.0, 1.0)
    lane = lax.broadcasted_iota(jnp.int32, (LONG, PAIR), 1)
    ones = jnp.ones((TILE_ROWS, LONG), BF16)
    q_heads, k_pairs, v_heads = [], [], []
    for pair in range(query.shape[1] // PAIR):
        cols = slice(pair * PAIR, (pair + 1) * PAIR)
        rows = query[:, cols]
        zero = jnp.zeros_like(rows)
        q_heads += [jnp.where(lane < HD, rows, zero), jnp.where(lane >= HD, rows, zero)]
        k_pairs.append(key[:, cols])
        turned = value[:, cols].astype(F32).T.astype(BF16)
        v_heads += [jnp.concatenate([turned[:HD], ones], 0), jnp.concatenate([turned[HD:], ones], 0)]

    def scores_of(unit):
        strip, head = unit
        lo, reach = strip * STRIP, (strip + 1) * STRIP
        return (dot_nt(k_pairs[head // 2][:reach], q_heads[head][lo:reach]),)

    def soften(unit, scores):
        strip, unused = unit
        lo = strip * STRIP
        parts = []
        if lo >= SHORT:
            parts.append(scores[:SHORT] + cut)
            if lo > SHORT:
                parts.append(scores[SHORT:lo])
        elif strip:
            parts.append(scores[:lo])
        parts.append(jnp.where(causal, scores[lo:], far_below))
        scores = jnp.concatenate(parts, 0)
        largest = jnp.max(scores, 0, keepdims=True)
        return jnp.exp(scores - largest).astype(BF16), largest

    def finish(unit, shifted, largest):
        strip, head = unit
        out = dot_nn(v_heads[head][:, : (strip + 1) * STRIP], shifted)
        sum_exp = out[HD : HD + 1]
        return out[:HD] * (1.0 / sum_exp), largest + jnp.log(sum_exp)

    units = [(strip, head) for strip in range(strips) for head in range(len(q_heads))]
    results = pipeline(units, 2, scores_of, soften, finish)
    for strip in range(strips):
        rows = slice(strip * STRIP, (strip + 1) * STRIP)
        for pair in range(len(k_pairs)):
            cols = slice(pair * PAIR, (pair + 1) * PAIR)
            two = [results[(strip, 2 * pair + side)] for side in range(2)]
            attended[rows, cols] = jnp.concatenate([out for out, unused in two], 0).T.astype(BF16)
            lines = [part.astype(F32) for unused, logsum in two for part in split_three(-logsum)]
            lines.append(jnp.broadcast_to(late if strip * STRIP >= SHORT else 0.0, (1, STRIP)))
            lines.append(jnp.zeros((PAIR - 7, STRIP), F32))
            extra[rows, cols] = jnp.concatenate(lines, 0).T.astype(BF16)


def block_columns(source, index):
    return source[index, :BLOCK, :GROUP]


def forward_body(first, pieces, longs, where, rows_in, *rest):
    sources, rest = rest[: len(pieces)], rest[len(pieces) :]
    if first:
        query, key, value, attended, extra, w_three, w_out, hidden, vec, weights = rest
    else:
        query, key, value, attended, extra, w_three, w_out, weights = rest
    sub = pl.program_id(0)

    @pl.when(sub == 0)
    def _():
        weights[...] = jnp.zeros_like(weights)
        for piece, source in zip(pieces, sources):
            place_piece(weights, 0, where, piece, functools.partial(block_columns, source), True)
        w_three[...] = weights[:ROW_OUT, :]
        w_out[...] = weights[ROW_OUT:, :]
        if first:
            total = jnp.zeros((VEC_ROWS, D), BF16)
            for source in sources:
                if source.shape[1] > BLOCK:
                    for index in range(source.shape[0]):
                        total = total + source[index, BLOCK:, :]
            vec[...] = total

    if first:
        normed, unused = layer_stats(rows_in[...].astype(F32))
        lines = vec[...].astype(F32)
        hid = (normed * lines[0:1] + lines[1:2]).astype(BF16)
        hidden[...] = hid
    else:
        hid = rows_in[...]
    q_rows = (dot_nn(hid, weights[ROW_QUERY : ROW_QUERY + D, :]) * (1.0 / math.sqrt(HD))).astype(BF16)
    k_rows = dot_nn(hid, weights[ROW_KEY : ROW_KEY + D, :]).astype(BF16)
    v_rows = dot_nn(hid, weights[ROW_VALUE : ROW_VALUE + D, :]).astype(BF16)
    query[...] = q_rows
    key[...] = k_rows
    value[...] = v_rows
    attend_columns(longs[sub] > 0, q_rows, k_rows, v_rows, attended, extra)


def forward_group(group, longs, where, rows_in, pieces, through):
    first = group == 0
    total = rows_in.shape[0]
    rows = pl.BlockSpec((LONG, D), lambda s, *refs: (s, 0))
    part = pl.BlockSpec((LONG, GROUP), lambda s, *refs: (s, 0))
    width = D if first else GROUP
    blocks = [
        pl.BlockSpec(piece.array.shape[:2] + (width,), lambda s, *refs: (0, 0, group), pipeline_mode=pl.Buffered(1))
        for piece in pieces
    ]
    tail = PLANE_END[0] - ROW_OUT
    out_specs = [part] * 5 + [whole((ROW_OUT, GROUP)), whole((tail, GROUP))]
    out_shape = [jax.ShapeDtypeStruct((total, GROUP), BF16)] * 5 + [
        jax.ShapeDtypeStruct((ROW_OUT, GROUP), BF16),
        jax.ShapeDtypeStruct((tail, GROUP), BF16),
    ]
    if first:
        out_specs += [rows, whole((VEC_ROWS, D))]
        out_shape += [jax.ShapeDtypeStruct((total, D), BF16), jax.ShapeDtypeStruct((VEC_ROWS, D), BF16)]
    return call_kernel(
        functools.partial(forward_body, first, pieces),
        [longs, where, rows_in, *[piece.array for piece in pieces]],
        through,
        [rows] + blocks,
        out_specs,
        out_shape,
        (total // LONG,),
        "forward_group",
        (8e9, 12e6, 4e6) if first else (0, 0, 0),
        scalars=2,
        scratch=[pltpu.VMEM((PLANE_END[0], GROUP), BF16)],
    )


def attend_back_rows(query, key, value, extra, attended, grad, grad_query, grad_key, grad_value):
    strips = LONG // STRIP
    lane = lax.broadcasted_iota(jnp.int32, (LONG, PAIR), 1)
    row = lax.broadcasted_iota(jnp.int32, (LONG, PAIR), 0)
    row_ids = lax.broadcasted_iota(jnp.int32, (STRIP, STRIP), 0)
    col_ids = lax.broadcasted_iota(jnp.int32, (STRIP, STRIP), 1)
    causal = row_ids >= col_ids
    early = jnp.where((lane == 6) & (row < SHORT), far_below, 0.0)
    v_tail = jnp.where(lane < 3, 1.0, 0.0).astype(BF16)
    heads, pairs = [], query.shape[1] // PAIR
    for pair in range(pairs):
        cols = slice(pair * PAIR, (pair + 1) * PAIR)
        q_all, k_all, v_all, g_all, x_all = (ref[:, cols] for ref in (query, key, value, grad, extra))
        product = g_all.astype(F32) * attended[:, cols].astype(F32)
        zero = jnp.zeros_like(q_all)
        v_wide = jnp.concatenate([v_all, v_tail], 1)
        q_turned = q_all.astype(F32).T.astype(BF16)
        g_turned = g_all.astype(F32).T.astype(BF16)
        for side in range(2):
            mine = (lane < HD) if side == 0 else (lane >= HD)
            own = slice(side * HD, (side + 1) * HD)
            delta = jnp.sum(jnp.where(mine, product, 0.0), -1, keepdims=True)
            d_tail = pick_lanes(
                jnp.zeros((LONG, PAIR), F32), lane, 0, [part.astype(F32) for part in split_three(-delta)]
            )
            ones = jnp.where((lane >= 3 * side) & (lane < 3 * side + 3), 1.0, early).astype(BF16)
            heads.append(
                (
                    jnp.where(mine, k_all, zero),
                    q_turned[own],
                    g_turned[own],
                    jnp.concatenate([jnp.where(mine, q_all, zero), x_all], 1),
                    jnp.concatenate([jnp.where(mine, g_all, zero), d_tail.astype(BF16)], 1),
                    jnp.concatenate([k_all, ones], 1),
                    v_wide,
                )
            )

    def products(unit):
        strip, head = unit
        lo, hi = strip * STRIP, (strip + 1) * STRIP
        unused, unused, unused, q_wide, g_wide, k_wide, v_wide = heads[head]
        return dot_nt(q_wide[lo:hi], k_wide[:hi]), dot_nt(g_wide[lo:hi], v_wide[:hi])

    def soften(unit, scores, slope):
        lo = unit[0] * STRIP
        soft = jnp.exp(scores)
        last = jnp.where(causal, soft[:, lo:], 0.0)
        soft = jnp.concatenate([soft[:, :lo], last], 1) if lo else last
        return soft.astype(BF16), (soft * slope).astype(BF16)

    key_sum, value_sum = {}, {}

    def gradients(unit, soft, scores):
        strip, head = unit
        lo, hi = strip * STRIP, (strip + 1) * STRIP
        k_head, q_turned, g_turned, *unused = heads[head]
        value_part = dot_nn(g_turned[:, lo:hi], soft)
        key_part = dot_nn(q_turned[:, lo:hi], scores)
        for block in range(strip + 1):
            cols, at = slice(block * STRIP, (block + 1) * STRIP), (block, head)
            for total, part in ((value_sum, value_part), (key_sum, key_part)):
                total[at] = total[at] + part[:, cols] if at in total else part[:, cols]
        return dot_nn(scores, k_head[:hi])

    units = [(strip, head) for strip in range(strips) for head in range(len(heads))]
    results = pipeline(units, 1, products, soften, gradients)
    for block in range(strips):
        rows = slice(block * STRIP, (block + 1) * STRIP)
        for pair in range(pairs):
            cols = slice(pair * PAIR, (pair + 1) * PAIR)
            ends = [(block, 2 * pair), (block, 2 * pair + 1)]
            two = results[ends[0]] + results[ends[1]]
            grad_query[rows, cols] = (two * (1.0 / math.sqrt(HD))).astype(BF16)
            grad_key[rows, cols] = jnp.concatenate([key_sum[at] for at in ends], 0).T.astype(BF16)
            grad_value[rows, cols] = jnp.concatenate([value_sum[at] for at in ends], 0).T.astype(BF16)


def backward_body(steps, where, query, key, value, extra, attended, grad, hidden, late, *refs):
    (grad_query, grad_key, grad_value), keep = refs[:3], refs[3 : 3 + HALF]
    send, total, rows, sems = refs[3 + HALF :]
    step = pl.program_id(0)
    attend_back_rows(query, key, value, extra, attended, grad, grad_query, grad_key, grad_value)
    three = jnp.concatenate([grad_query[...], grad_key[...], grad_value[...]], 1)
    now = dot_tn(hidden[...], three)

    @pl.when(step == 0)
    def _():
        total[...] = now

    @pl.when(step > 0)
    def _():
        total[...] = total[...] + now

    @pl.when(step == steps - 1)
    def _():
        for part, at in enumerate((ROW_QUERY, ROW_KEY, ROW_VALUE)):
            rows[at : at + D, :] = total[:, part * GROUP : (part + 1) * GROUP].astype(BF16)
        rows[ROW_OUT:, :] = late[...]
        copies = emit_copies(rows, 0, 0, where, keep, send, sems)
        start_all(copies)
        wait_all(copies)


def backward_group(group, where, query, key, value, extra, attended, grad, hidden, late, through):
    total = query.shape[0]
    steps = total // LONG
    part = pl.BlockSpec((LONG, GROUP), lambda s, *refs: (s, 0))
    return call_kernel(
        functools.partial(backward_body, steps),
        [where, query, key, value, extra, attended, grad, hidden, late],
        through,
        [part] * 5
        + [
            pl.BlockSpec((LONG, GROUP), lambda s, *refs: (s, group)),
            pl.BlockSpec((LONG, D), lambda s, *refs: (s, 0)),
            pl.BlockSpec((late.shape[0], GROUP), lambda s, *refs: (0, group), pipeline_mode=pl.Buffered(1)),
        ],
        [part] * 3 + PLANE_SPEC,
        [jax.ShapeDtypeStruct((total, GROUP), BF16)] * 3 + plane_out(GROUP),
        (steps,),
        "backward_group",
        (14e9, 16e6, 4e6),
        scratch=[
            pltpu.VMEM((D, 3 * GROUP), F32),
            pltpu.VMEM((ROW_OUT + late.shape[0], GROUP), BF16),
            COPY_SEMS,
        ],
    )


MID_ROWS = 512
HALF_ROWS = 256
STAGE_ROWS = 256
STAGE = 8
CHUNKS = FF // D
TANH_SCALE = math.sqrt(2.0 / math.pi)


def spread_matrix(size):
    quarter = size // CHUNKS
    to = lax.broadcasted_iota(jnp.int32, (size, size), 0)
    source = lax.broadcasted_iota(jnp.int32, (size, size), 1)
    return (source == CHUNKS * (to % quarter) + to // quarter).astype(BF16)


def interleave(parts):
    started, live = 0, []
    while started < len(parts) or live:
        if started < len(parts):
            live.append(parts[started])
            started += 1
        live = [part for part in live if next(part, True) is None]


def middle_body(steps, pieces, where, tok, grad_out, hidden_a, *refs):
    att_refs, wo_refs, refs = refs[:GROUPS], refs[GROUPS : 2 * GROUPS], refs[2 * GROUPS :]
    sources, refs = refs[: len(pieces)], refs[len(pieces) :]
    (outputs, grad_middle_ref, grad_za_ref, grad_attended, grad_a_ref, gate_copy) = refs[:6]
    keep, send = refs[6 : 6 + HALF], refs[6 + HALF]
    carry, weights, wide, slope, s_vec, kept, s_hid_f, s_grad_f, s_grad_zf = refs[7 + HALF : -3]
    load_sems, sems_three, sems_two = refs[-3:]
    step = pl.program_id(0)
    base = ROW_OUT

    @pl.when(step == 0)
    def _():
        staged = []
        for piece, source in zip(pieces, sources):
            for index in range(len(piece.blocks)):
                slot = len(staged)
                to = kept.at[slot // STAGE, pl.ds(slot % STAGE * STAGE_ROWS, BLOCK), :]
                staged.append((to, pltpu.make_async_copy(source.at[index, pl.ds(0, BLOCK), :], to, load_sems.at[slot])))
                staged[-1][1].start()
        weights[...] = jnp.zeros_like(weights)
        for group in range(GROUPS):
            weights[: PLANE_END[0] - ROW_OUT, group * GROUP : (group + 1) * GROUP] = wo_refs[group][...]
        at_slot = 0
        for piece in pieces:
            count = len(piece.blocks)
            here = staged[at_slot : at_slot + count]
            wait_all([copy for unused, copy in here])
            place_piece(weights, base, where, piece, lambda index, here=here: here[index][0][...], False)
            at_slot += count
        shuffle = spread_matrix(256)
        for block in range(FF // 256):
            at = ROW_IN - base + block * 256
            part = dot_nn(shuffle, weights[at : at + 256, :]).astype(BF16)
            for chunk in range(CHUNKS):
                wide[chunk, block * 64 : (block + 1) * 64, :] = part[chunk * 64 : (chunk + 1) * 64]
        gate_copy[...] = weights[ROW_GATE_A - base : ROW_GATE_A - base + D, :]
        s_vec[...] = jnp.zeros_like(s_vec)

    w_out = weights.at[ROW_OUT - base : ROW_OUT - base + D]
    gate_attn = weights.at[ROW_GATE_A - base : ROW_GATE_A - base + D]
    gate_ffn = weights.at[ROW_GATE_F - base : ROW_GATE_F - base + D]
    w_down = weights.at[ROW_DOWN - base : ROW_DOWN - base + FF]
    vecs = weights[ROW_VEC - base : ROW_VEC - base + VEC_ROWS, :].astype(F32)
    chunks = [slice(chunk * D, (chunk + 1) * D) for chunk in range(CHUNKS)]

    first_row = pl.multiple_of(step * MID_ROWS, MID_ROWS)

    def part(at):
        here = slice(at, at + HALF_ROWS)
        there = pl.ds(first_row + at, HALF_ROWS)
        hid_a = hidden_a[here, :]
        att = jnp.concatenate([ref[here, :] for ref in att_refs], 1)
        grad = grad_out[here, :].astype(F32)
        branch_a = dot_nn(att, w_out[...])
        gate_a = dot_nn(hid_a, gate_attn[...])
        yield
        branch_a = branch_a + vecs[2:3]
        gate_a = sigmoid(gate_a + vecs[3:4])
        middle = tok[here, :].astype(F32) + gate_a * branch_a
        normed, inv_std = layer_stats(middle)
        hid_f = (normed * vecs[4:5] + vecs[5:6]).astype(BF16)
        s_hid_f[there, :] = hid_f
        yield
        gate_f = dot_nn(hid_f, gate_ffn[...])
        pre = dot_nn(hid_f, wide[0])
        yield
        branch_f = vecs[6:7]
        for chunk, cols in enumerate(chunks):
            pre = pre + vecs[8 + chunk : 9 + chunk]
            square = pre * pre
            bend = jnp.tanh(pre * (TANH_SCALE + (TANH_SCALE * 0.044715) * square))
            half = 0.5 * (1.0 + bend)
            active = (pre * half).astype(BF16)
            slope[here, cols] = half + (0.5 * pre) * (1.0 - bend * bend) * (
                TANH_SCALE + (3.0 * 0.044715 * TANH_SCALE) * square
            )
            kept[chunk, there, :] = active
            yield
            if chunk + 1 < CHUNKS:
                pre = dot_nn(hid_f, wide[chunk + 1])
            branch_f = branch_f + dot_nn(active, w_down[cols, :])
            yield
        gate_f = sigmoid(gate_f + vecs[7:8])
        outputs[here, :] = (middle + gate_f * branch_f).astype(BF16)
        grad_branch_f = (grad * gate_f).astype(BF16)
        grad_zf = (grad * branch_f * gate_f * (1.0 - gate_f)).astype(BF16)
        s_grad_f[there, :] = grad_branch_f
        s_grad_zf[there, :] = grad_zf
        s_vec[6] += fold_rows(grad_branch_f.astype(F32))
        s_vec[7] += fold_rows(grad_zf.astype(F32))
        yield
        grad_hidden = dot_nt(grad_zf, gate_ffn[...])
        grad_active = dot_nt(grad_branch_f, w_down[chunks[0], :])
        yield
        for chunk, cols in enumerate(chunks):
            grad_pre = (grad_active * slope[here, cols]).astype(BF16)
            kept[CHUNKS + chunk, there, :] = grad_pre
            s_vec[8 + chunk] += fold_rows(grad_pre.astype(F32))
            yield
            if chunk + 1 < CHUNKS:
                grad_active = dot_nt(grad_branch_f, w_down[chunks[chunk + 1], :])
            grad_hidden = grad_hidden + dot_nt(grad_pre, wide[chunk])
            yield
        s_vec[4] += fold_rows(grad_hidden * normed)
        s_vec[5] += fold_rows(grad_hidden)
        grad_middle = grad + norm_back(grad_hidden * vecs[4:5], normed, inv_std)
        grad_middle_ref[here, :] = grad_middle
        grad_branch_a = (grad_middle * gate_a).astype(BF16)
        grad_za = (grad_middle * branch_a * gate_a * (1.0 - gate_a)).astype(BF16)
        grad_za_ref[here, :] = grad_za
        grad_a_ref[here, :] = grad_branch_a
        s_vec[2] += fold_rows(grad_branch_a.astype(F32))
        s_vec[3] += fold_rows(grad_za.astype(F32))
        yield
        grad_attended[here, :] = dot_nt(grad_branch_a, w_out[...]).astype(BF16)
        yield

    interleave([part(at) for at in range(0, MID_ROWS, HALF_ROWS)])

    @pl.when(step == steps - 1)
    def _():
        for chunk in range(CHUNKS):
            at = ROW_DOWN - base + chunk * D
            weights[at : at + D, :] = dot_tn(kept[chunk], s_grad_f[...]).astype(BF16)
        weights[ROW_VEC - base :, :] = jnp.sum(s_vec[...], 1).astype(BF16)
        copies = emit_copies(weights, base, 3, where, keep, send, sems_three, D)
        start_all(copies)
        for chunk in range(CHUNKS):
            wide[chunk] = dot_tn(s_hid_f[...], kept[CHUNKS + chunk]).astype(BF16)
        shuffle = spread_matrix(256)
        for block in range(FF // 256):
            parts = [wide[chunk, block * 64 : (block + 1) * 64, :] for chunk in range(CHUNKS)]
            at = ROW_IN - base + block * 256
            weights[at : at + 256, :] = dot_tn(shuffle, jnp.concatenate(parts, 0)).astype(BF16)
        last = emit_copies(weights, base, 2, where, keep, send, sems_two)
        start_all(last)
        at = ROW_GATE_F - base
        weights[at : at + D, :] = dot_tn(s_hid_f[...], s_grad_zf[...]).astype(BF16)
        carry[...] = weights[ROW_GATE_F - base : PLANE_END[1] - base, :]
        wait_all(copies)
        wait_all(last)


def middle_part(where, tokens, grad_out, hidden_a, attended, w_outs, pieces):
    total = tokens.shape[0]
    steps = total // MID_ROWS
    carry = PLANE_END[1] - ROW_GATE_F
    rows_at = lambda width: pl.BlockSpec((MID_ROWS, width), lambda i, *refs: (i, 0))
    shape = lambda kind=BF16: jax.ShapeDtypeStruct((total, D), kind)
    results, unused = call_kernel(
        functools.partial(middle_body, steps, pieces),
        [where, tokens, grad_out, hidden_a, *attended, *w_outs, *[piece.array for piece in pieces]],
        [],
        [rows_at(D)] * 3
        + [rows_at(GROUP)] * GROUPS
        + [whole(w_outs[0].shape)] * GROUPS
        + [UNREAD] * len(pieces),
        [rows_at(D)] * 5 + [whole((D, D))] + PLANE_SPEC + [whole((carry, D))],
        [shape(), shape(F32)]
        + [shape()] * 3
        + [jax.ShapeDtypeStruct((D, D), BF16)]
        + plane_out(2 * D)
        + [jax.ShapeDtypeStruct((carry, D), BF16)],
        (steps,),
        "middle_part",
        (33e9, 50e6, 4e6),
        scratch=[
            pltpu.VMEM((ALL_ROWS - ROW_OUT, D), BF16),
            pltpu.VMEM((CHUNKS, D, D), BF16),
            pltpu.VMEM((MID_ROWS, FF), F32),
            pltpu.VMEM((VEC_ROWS, 8, D), F32),
            pltpu.VMEM((2 * CHUNKS, total, D), BF16),
            pltpu.VMEM((total, D), BF16),
            pltpu.VMEM((total, D), BF16),
            pltpu.VMEM((total, D), BF16),
            pltpu.SemaphoreType.DMA((SHARES,)),
            COPY_SEMS,
            COPY_SEMS,
        ],
    )
    return results


def gates_body(where, *refs):
    att_refs, refs = refs[:GROUPS], refs[GROUPS:]
    hidden_a, grad_a, grad_za, late, *refs = refs
    keep, send, carry, sides, rows, load_sems, sems = refs[:HALF], *refs[HALF:]
    loads = []

    def load(source, to):
        loads.append(pltpu.make_async_copy(source, to, load_sems.at[len(loads)]))
        loads[-1].start()

    for group, ref in enumerate(att_refs):
        load(ref, sides.at[0, :, pl.ds(group * GROUP, GROUP)])
    for slot, ref in enumerate((grad_a, hidden_a, grad_za)):
        load(ref, sides.at[1 + slot])
    rows[2 * D :, :] = late[...]
    for at in range(2):
        wait_all(loads[: GROUPS + 1] if at == 0 else loads[GROUPS + 2 * at - 1 : GROUPS + 2 * at + 1])
        rows[at * D : (at + 1) * D, :] = dot_tn(sides[2 * at], sides[2 * at + 1]).astype(BF16)
    copies = emit_copies(rows, ROW_OUT, 1, where, keep, send, sems)
    start_all(copies)
    carry[...] = rows[: PLANE_END[0] - ROW_OUT, :]
    wait_all(copies)


def gates_gradient(where, attended, hidden_a, grad_a, grad_za, late, through):
    total = hidden_a.shape[0]
    carry = PLANE_END[0] - ROW_OUT
    return call_kernel(
        gates_body,
        [where, *attended, hidden_a, grad_a, grad_za, late],
        through,
        [UNREAD] * (GROUPS + 3) + [whole(late.shape)],
        PLANE_SPEC + [whole((carry, D))],
        plane_out(D) + [jax.ShapeDtypeStruct((carry, D), BF16)],
        (1,),
        "gates_gradient",
        (2.1e9, 10e6, 0),
        scratch=[
            pltpu.VMEM((4, total, D), BF16),
            pltpu.VMEM((2 * D + late.shape[0], D), BF16),
            pltpu.SemaphoreType.DMA((GROUPS + 3,)),
            COPY_SEMS,
        ],
    )


LAST_ROWS = 512


def last_body(steps, tok, grad_middle, grad_za, *refs):
    grads, refs = refs[: 3 * GROUPS], refs[3 * GROUPS :]
    w_three, refs = refs[:GROUPS], refs[GROUPS:]
    gate_attn, vec, input_grad, d_vec, factors, s_vec = refs
    step = pl.program_id(0)

    @pl.when(step == 0)
    def _():
        s_vec[...] = jnp.zeros_like(s_vec)
        for group in range(GROUPS):
            factors[:, group * GROUP : (group + 1) * GROUP] = w_three[group][...]

    vecs = vec[...].astype(F32)

    def part(at):
        here = slice(at, at + HALF_ROWS)
        grad_hidden = dot_nt(grad_za[here, :], gate_attn[...])
        for side, row in enumerate((ROW_QUERY, ROW_KEY, ROW_VALUE)):
            grad = jnp.concatenate([grads[3 * group + side][here, :] for group in range(GROUPS)], 1)
            grad_hidden += dot_nt(grad, factors[row : row + D, :])
        yield
        normed, inv_std = layer_stats(tok[here, :].astype(F32))
        s_vec[0] += fold_rows(grad_hidden * normed)
        s_vec[1] += fold_rows(grad_hidden)
        back = norm_back(grad_hidden * vecs[0:1], normed, inv_std)
        input_grad[here, :] = (grad_middle[here, :] + back).astype(BF16)
        yield

    interleave([part(at) for at in range(0, LAST_ROWS, HALF_ROWS)])

    @pl.when(step == steps - 1)
    def _():
        d_vec[...] = jnp.sum(s_vec[...], 1)


def last_part(tokens, grad_middle, grad_za, grads, w_three, gate_attn, vec, through):
    total = tokens.shape[0]
    steps = total // LAST_ROWS
    rows_at = lambda width: pl.BlockSpec((LAST_ROWS, width), lambda i, *refs: (i, 0))
    return call_kernel(
        functools.partial(last_body, steps),
        [tokens, grad_middle, grad_za, *grads, *w_three, gate_attn, vec],
        through,
        [rows_at(D)] * 3
        + [rows_at(GROUP)] * (3 * GROUPS)
        + [whole((ROW_OUT, GROUP))] * GROUPS
        + [whole((D, D)), whole((VEC_ROWS, D))],
        [rows_at(D), whole((VEC_ROWS, D))],
        [jax.ShapeDtypeStruct((total, D), BF16), jax.ShapeDtypeStruct((VEC_ROWS, D), F32)],
        (steps,),
        "last_part",
        (4.3e9, 20e6, 0),
        scalars=0,
        scratch=[pltpu.VMEM((ROW_OUT, D), BF16), pltpu.VMEM((VEC_ROWS, 8, D), F32)],
    )


def local_part(where, longs, tokens, out_grad, first_pieces, middle_pieces, before, later, collect):
    subs, length, unused = tokens.shape
    rows = tokens.reshape(subs * length, D)
    grads_in = out_grad.reshape(subs * length, D)
    (*kept, hidden_a, vec), passed = forward_group(0, longs, where, rows, first_pieces, before("forward0"))
    later("forward0", passed)
    second, passed = forward_group(1, longs, where, hidden_a, first_pieces, before("forward1"))
    later("forward1", passed)
    groups = [kept, second]
    attended = [group[3] for group in groups]
    (outputs, grad_middle, grad_za, grad_attended, grad_a, gate_attn, *plane, carry) = (
        middle_part(where, rows, grads_in, hidden_a, attended, [group[6] for group in groups], middle_pieces())
    )
    collect("upper", plane)
    (*plane, carry), passed = gates_gradient(
        where, attended, hidden_a, grad_a, grad_za, carry, before("gates")
    )
    later("gates", passed)
    collect(1, plane)
    grads = []
    for group, (query, key, value, att, extra, *unused_two) in enumerate(groups):
        results, passed = backward_group(
            group, where, query, key, value, extra, att, grad_attended, hidden_a, carry, before(f"back{group}")
        )
        later(f"back{group}", passed)
        grads += results[:3]
        collect(("first", group), results[3:])
    w_three = [group[5] for group in groups]
    (input_grad, d_vec), passed = last_part(
        rows, grad_middle, grad_za, grads, w_three, gate_attn, vec, before("last")
    )
    later("last", passed)
    return outputs.reshape(tokens.shape), input_grad.reshape(tokens.shape), d_vec


def own_block(params, start, rows):
    share = params.shape[0]
    room = jnp.pad(params, (TILE, rows * D - share))
    return lax.dynamic_slice(room, (TILE - start % TILE,), (rows * D,)).reshape(rows, D).astype(BF16)


def move(axis, count, step):
    perm = [(i, step(i)) for i in range(count) if step(i) is not None]
    return lambda value: lax.ppermute(value, axis, perm)


def on_slice(tokens, out_grad, long_count, params):
    z, x, y, c = (lax.axis_index(axis) for axis in ("z", "x", "y", "c"))
    me = ((z * 2 + x) * 2 + y) * 2 + c
    share = params.shape[0]
    block = own_block(params, me * share, BLOCK)
    odd = z % 2 == 1
    ends = (z == 0) | (z == 3)
    swap_c = move("c", 2, lambda i: 1 - i)
    swap_x = move("x", 2, lambda i: 1 - i)
    swap_y = move("y", 2, lambda i: 1 - i)
    swap_xy = move(("x", "y"), 4, lambda i: 3 - i)
    z_one = move("z", 4, lambda i: i ^ 1)
    z_two = move("z", 4, lambda i: i ^ 2)
    inside = z < 4
    vec = block[VEC_AT : VEC_AT + VEC_ROWS]
    mine = jnp.concatenate([block, jnp.where(me == SHARES - 1, vec, jnp.zeros_like(vec))], 0)
    step_one = move("z", 4, {0: 2, 1: 0, 2: 3, 3: 1}.get)(mine)
    held = jnp.where(ends, mine, step_one)
    step_two = z_one(held)
    step_three = z_two(jnp.where(ends, step_one[:BLOCK], block))
    vec = jnp.where(odd, held, step_two)[BLOCK:]
    first = jnp.where(inside, jnp.where(z == 2, step_one, step_two)[:BLOCK], step_three)
    first = jnp.concatenate([first, vec], 0)[None]
    both = jnp.stack([jnp.where(z == 2, step_two, step_one)[:BLOCK], step_three])

    def in_plane(parts, planes):
        near = jnp.concatenate(parts, 0)
        blocks = [(plane, spot) for spot in range(HALF) for plane in planes]
        return [Piece(near, blocks, False), Piece(swap_c(near), blocks, True)]

    own = block[None]
    pieces = in_plane([own, swap_y(own), swap_x(own), swap_xy(own)], ((0,),))
    pieces += in_plane([first, swap_y(first), swap_x(first), swap_xy(first)], ((4,),))
    around = {"both": [swap_y(both), swap_x(both), swap_xy(both)]}
    top = {"both": both[:, :TILE_ROWS]}
    pair = ((5,), (6,))
    blocks = [(plane, 0) for plane in pair]
    both_pieces = [Piece(both, blocks, False), Piece(swap_c(both), blocks, True)]

    def middle_pieces():
        late = jnp.pad(top["both"], ((0, 0), (0, BLOCK - TILE_ROWS), (0, 0)))
        parts = around["both"]
        near = jnp.concatenate([jnp.where(inside, parts[0], late), *parts[1:]], 0)
        blocks = [(plane, spot) for spot in range(1, HALF) for plane in pair]
        return pieces + both_pieces + [Piece(near, blocks, False), Piece(swap_c(near), blocks, True)]

    early, late = ("first", 0), ("first", 1)
    arrived, at_chip, held = {}, {}, {}
    z_up = move("z", 4, lambda i: {0: 2, 1: 3}.get(i))
    z_down = move("z", 4, lambda i: {2: 0, 3: 1}.get(i))

    def collect(plane, blocks):
        arrived[plane] = [list(blocks[:HALF]), swap_c(blocks[HALF])]

    def send_around(name, planes, first=None):
        part = []
        for spot in range(HALF):
            sums = [arrived[plane][0][spot].astype(F32) + arrived[plane][1][spot].astype(F32) for plane in planes]
            sums = jnp.concatenate(sums, 1)
            if first is not None:
                sums = jnp.where(inside, sums, first[:, : sums.shape[1]])
            part.append(sums.astype(BF16))
        at_chip[name] = part[0]
        around[name] = (swap_y(part[1]), swap_x(part[2]), swap_xy(part[3]))

    def plane_sum(name):
        total = at_chip[name].astype(F32)
        for got in around[name]:
            total = total + got.astype(F32)
        return total

    def before(name):
        if name == "forward0":
            return []
        if name == "forward1":
            return [top["both"]]
        if name == "gates":
            return arrived["upper"][0]
        if name == "back0":
            send_around("upper", ("upper",))
            return [at_chip["upper"]]
        if name == "back1":
            held["upper"] = plane_sum("upper")
            held["up"] = z_up(held["upper"].astype(BF16))
            send_around("lower", (1, early), held["upper"])
            return [held["upper"], at_chip["lower"]]
        if name == "last":
            held["lower"] = plane_sum("lower")
            held["down"] = z_down(held["lower"].astype(BF16))
            send_around("late", (late,), held["lower"])
            upper = held["upper"] + held["up"].astype(F32)
            two, three, last = upper[:, :D], upper[:, D:], held["lower"][:, :D]
            held["give"] = jnp.where(inside, jnp.where(z == 2, three, two), last).astype(BF16)
            held["mine"] = jnp.where(inside, jnp.where(z == 2, two, three), last)
            return [held["give"], held["mine"], held["lower"], at_chip["late"]]
        return []

    def later(name, passed):
        if name == "forward1":
            top["both"] = passed[0]
        if name == "gates":
            arrived["upper"][0] = passed
        if name == "back0":
            at_chip["upper"] = passed[0]
        if name == "back1":
            held["upper"], at_chip["lower"] = passed
        if name == "last":
            held["give"], held["mine"], held["lower"], at_chip["late"] = passed

    planes = [jnp.where(z == 0, 3, 0), jnp.where(z == 0, 1, jnp.where(z == 3, 2, 3)), jnp.where(z < 2, 2, 1)]
    where = jnp.stack([z, x, y, c, *planes]).astype(jnp.int32)
    outputs, input_grad, d_vec = local_part(
        where,
        long_count.reshape(-1),
        tokens,
        out_grad,
        pieces,
        middle_pieces,
        before,
        later,
        collect,
    )
    low = plane_sum("late")
    lower = jnp.where(inside, held["lower"], jnp.concatenate([low] * 3, 1)) + held["down"].astype(F32)
    one, zero = lower[:, :D], jnp.concatenate([lower[:, D:]] * 2, 1)
    give = jnp.where(z == 0, one.astype(BF16), jnp.where(z == 1, zero.astype(BF16), held["give"]))
    given = z_one(give).astype(F32)
    total = jnp.where(z == 0, zero, jnp.where(z == 1, one, held["mine"])) + given
    gains = jnp.where(inside, d_vec[:2], jnp.concatenate([low[:2]] * 2, 1))
    gains = gains + swap_c(gains)
    gains = (gains + swap_x(gains) + swap_y(gains) + swap_xy(gains)).reshape(2 * GROUPS, GROUP)
    lines = jnp.pad(gains.astype(BF16), ((0, TILE_ROWS - 2 * GROUPS), (0, 0)))
    message = jnp.concatenate([jnp.where(inside, low, given[:, :GROUP]).astype(BF16), lines], 0)
    for step in ({3: 0, 0: 3}, {2: 0, 1: 3}, {1: 0, 2: 3}):
        got = move("z", 4, step.get)(message).astype(F32)
        low = low + got[:BLOCK]
        gains = gains + got[BLOCK : BLOCK + 2 * GROUPS]
    total = jnp.where(z == 0, jnp.concatenate([total[:, :GROUP], low], 1), total)
    gains = jnp.where(me == SHARES - 1, gains.reshape(2, D), jnp.zeros((2, D), F32))
    total = total + jnp.pad(gains, ((VEC_AT, BLOCK - VEC_AT - 2), (0, 0)))
    param_grad = lax.dynamic_slice(total.reshape(-1), ((me * share) % TILE,), (share,))
    return (outputs, input_grad, param_grad)


def on_any(axes, count, tokens, out_grad, long_count, params):
    share = params.shape[0]
    me = lax.axis_index(axes)
    starts = [index * share // TILE * TILE_ROWS for index in range(count)]
    rows = max(-(-((index + 1) * share) // TILE) * TILE_ROWS - starts[index] for index in range(count))
    gathered = lax.all_gather(own_block(params, me * share, rows), axes, axis=0)
    merged = jnp.zeros((starts[-1] + rows, D), BF16)
    for index in range(count):
        merged = merged.at[starts[index] : starts[index] + rows].add(gathered[index])
    merged = merged[:ALL_ROWS]
    near, far = [], []
    for plane in range(PLANES):
        blocks = []
        for index in range(plane * IN_PLANE, (plane + 1) * IN_PLANE):
            end = STARTS[index + 1] if index + 1 < SHARES else ALL_ROWS
            piece = merged[STARTS[index] : end]
            blocks.append(jnp.pad(piece, ((0, BLOCK - piece.shape[0]), (0, 0))))
        spots = [(plane, spot) for spot in range(HALF)]
        near.append(Piece(jnp.stack(blocks[0::2]), spots, False))
        far.append(Piece(jnp.stack(blocks[1::2]), spots, True))
    vec = merged[ROW_VEC : ROW_VEC + VEC_ROWS]
    first_pieces = []
    for piece in (near[0], far[0]):
        lines = jnp.zeros((HALF, VEC_ROWS, D), BF16)
        if piece is near[0]:
            lines = lines.at[0].set(vec)
        first_pieces.append(Piece(jnp.concatenate([piece.array, lines], 1), piece.blocks, piece.other))
    by_share = [None] * SHARES

    halves = []

    def collect(plane, blocks):
        if isinstance(plane, tuple):
            halves.append(blocks)
            if len(halves) < GROUPS:
                return
            blocks = [jnp.concatenate(parts, parts[0].ndim - 1) for parts in zip(*halves)]
            plane = 0
        places = (2, 3) if plane == "upper" else (plane,)
        for at, plane in enumerate(places):
            cols = slice(at * D, (at + 1) * D)
            for spot in range(HALF):
                by_share[plane * IN_PLANE + 2 * spot] = blocks[spot][:, cols]
                by_share[plane * IN_PLANE + 2 * spot + 1] = blocks[HALF][spot][:, cols]

    outputs, input_grad, d_vec = local_part(
        jnp.zeros((7,), jnp.int32),
        long_count.reshape(-1),
        tokens,
        out_grad,
        first_pieces,
        lambda: near[1:] + far[1:],
        lambda name: [],
        lambda name, passed: None,
        collect,
    )
    ends = STARTS[1:] + [ALL_ROWS]
    gradient = jnp.concatenate([part[: ends[i] - STARTS[i]] for i, part in enumerate(by_share)], 0)
    gradient = gradient.at[ROW_VEC : ROW_VEC + VEC_ROWS].add(d_vec.astype(BF16))
    gradient = jnp.pad(gradient, ((0, max(0, starts[-1] + rows - ALL_ROWS)), (0, 0)))
    spread = jnp.stack([gradient[start : start + rows] for start in starts])
    summed = lax.psum_scatter(spread, axes, scatter_dimension=0)
    param_grad = lax.dynamic_slice(summed.astype(F32).reshape(-1), ((me * share) % TILE,), (share,))
    return (outputs, input_grad, param_grad)


def solution(mesh):
    axes = ("wide", "narrow")
    count = math.prod(mesh.shape[axis] for axis in axes)
    step = functools.partial(on_any, axes, count)
    if mesh.shape["wide"] == 8 and mesh.shape["narrow"] == 4:
        axes = ("z", "x", "y", "c")
        mesh = Mesh(mesh.devices.reshape(4, 2, 2, 2), axes)
        step = on_slice
    return jax.shard_map(
        step,
        mesh=mesh,
        in_specs=(P(None, axes, None), P(None, axes, None), P(None, axes), P(axes)),
        out_specs=(P(None, axes, None), P(None, axes, None), P(axes)),
        check_vma=False,
    )
```
